32 devices in a mesh: dp: 8 (over z, core), fsdp: 4 (over y, x).
Axes of the slice: x: 2, y: 2, z: 4, core: 2. Of those that a mesh axis runs over, the one named last changes fastest.
Arguments:
- hidden: bfloat16 [65536, 768], P(('dp', 'fsdp')), may hold values from -6 to 6
- time_embed: bfloat16 [65536, 768], P(('dp', 'fsdp')), may hold values from -6 to 6
- segment_ids: int32 [65536], P(('dp', 'fsdp')), may hold values from -1 to 15, as said below
- ln1_gain: bfloat16 [768], P(('dp', 'fsdp')), may hold values from 0.5 to 1.5
- ln1_bias: bfloat16 [768], P(('dp', 'fsdp')), may hold values from -3 to 3
- w_qkv: bfloat16 [768, 2304], P(None, ('dp', 'fsdp')), may hold values from -0.21875 to 0.21875
- b_query: bfloat16 [768], P(('dp', 'fsdp')), may hold values from -3 to 3
- b_value: bfloat16 [768], P(('dp', 'fsdp')), may hold values from -3 to 3
- w_out: bfloat16 [768, 768], P(None, ('dp', 'fsdp')), may hold values from -0.875 to 0.875
- b_out: bfloat16 [768], P(('dp', 'fsdp')), may hold values from -3 to 3
- ln2_gain: bfloat16 [768], P(('dp', 'fsdp')), may hold values from 0.5 to 1.5
- ln2_bias: bfloat16 [768], P(('dp', 'fsdp')), may hold values from -3 to 3
- w_up: bfloat16 [768, 3072], P(None, ('dp', 'fsdp')), may hold values from -0.21875 to 0.21875
- b_up: bfloat16 [3072], P(('dp', 'fsdp')), may hold values from -3 to 3
- w_down: bfloat16 [3072, 768], P(None, ('dp', 'fsdp')), may hold values from -0.109375 to 0.109375
- b_down: bfloat16 [768], P(('dp', 'fsdp')), may hold values from -3 to 3
- cotangent: bfloat16 [65536, 768], P(('dp', 'fsdp')), may hold values from -6 to 6
Outputs:
- output: bfloat16 [65536, 768], P(('dp', 'fsdp'))
- grad_hidden: bfloat16 [65536, 768], P(('dp', 'fsdp'))
- grad_ln1_gain: float32 [768], P(('dp', 'fsdp'))
- grad_ln1_bias: float32 [768], P(('dp', 'fsdp'))
- grad_w_qkv: float32 [768, 2304], P(None, ('dp', 'fsdp'))
- grad_b_query: float32 [768], P(('dp', 'fsdp'))
- grad_b_value: float32 [768], P(('dp', 'fsdp'))
- grad_w_out: float32 [768, 768], P(None, ('dp', 'fsdp'))
- grad_b_out: float32 [768], P(('dp', 'fsdp'))
- grad_ln2_gain: float32 [768], P(('dp', 'fsdp'))
- grad_ln2_bias: float32 [768], P(('dp', 'fsdp'))
- grad_w_up: float32 [768, 3072], P(None, ('dp', 'fsdp'))
- grad_b_up: float32 [3072], P(('dp', 'fsdp'))
- grad_w_down: float32 [3072, 768], P(None, ('dp', 'fsdp'))
- grad_b_down: float32 [768], P(('dp', 'fsdp'))
The draws below stay inside these ranges and needn't reach their ends.
Inputs may be any that keep to these rules, and one draw needn't show every extreme that they name: `segment_ids`: each aligned row of 1024 tokens holds either one item of 1024 tokens (all 0) or k items of 64 tokens numbered 0 to k - 1 in order, followed by padding marked -1; k is at least 8.
All inputs are finite; a program needn't handle non-finite values.
Results may differ from the reference program's by a relative error of at most 0.012.
Values may be sent and summed in bfloat16 or wider, within the bound.
A program may use at most 448 MiB of HBM per device.

```python
import math
import jax
import jax.numpy as jnp
from jax import lax

D = 768
HEADS = 12
HEAD = 64
FF = 3072
ROW = 1024
SHORT = 64
TOKENS = 65536


def draw_segment_ids(key, part):
    key = jax.random.fold_in(key, 7)
    whole_rows = TOKENS // ROW
    long_key, count_key = jax.random.split(key)
    long_rows = jax.random.randint(long_key, (whole_rows,), 0, 4) == 0
    counts = jax.random.randint(count_key, (whole_rows,), ROW // (2 * SHORT), ROW // SHORT + 1)
    row_index = jnp.arange(whole_rows)
    counts = jnp.where(row_index == 0, ROW // SHORT, jnp.where(row_index == 1, ROW // (2 * SHORT), counts))
    long_rows = jnp.where(row_index < 2, False, long_rows)
    item_index = (jnp.arange(ROW) // SHORT)[None, :]
    numbers = jnp.where(item_index < counts[:, None], item_index, -1)
    numbers = jnp.where(long_rows[:, None], 0, numbers)
    return numbers.reshape(TOKENS).astype(jnp.int32)


def spiked(values, own_key, source, target, parts, factor):
    def block_of(dim):
        return (jnp.arange(values.shape[dim]) // (values.shape[dim] // parts)).reshape((-1,) + (1,) * (values.ndim - 1 - dim))

    near = jax.random.permutation(own_key, parts)[block_of(target)]
    second = (block_of(target) + parts // 2) % parts
    return jnp.where((block_of(source) == near) | (block_of(source) == second), factor * values, values)


def block_levels(rng, extent, cuts, least, largest):
    def one(axis_at, shards_of):
        steps = jax.random.uniform(jax.random.fold_in(jax.random.fold_in(rng, 6), axis_at), (shards_of,), jnp.float32, least / len(cuts), largest / len(cuts))
        return jnp.repeat(jnp.exp(steps), extent[axis_at] // shards_of).reshape((-1,) + (1,) * (len(extent) - axis_at - 1))

    factor_of = one(*cuts[0])
    for cut in cuts[1:]:
        factor_of = factor_of * one(*cut)
    return factor_of


def normal_values(rng, dims, width, limit, cuts=(), held_as=jnp.bfloat16):
    values = width * jax.random.normal(rng, dims, jnp.float32)
    if cuts:
        values = values * block_levels(rng, dims, cuts, -0.22, 0.18)
    return jnp.clip(values, -limit, limit).astype(held_as)


def noise_with(key, dims, width, most, pieces, heavy, kind=jnp.bfloat16):
    array = width * jax.random.normal(key, dims, jnp.float32)
    if pieces:
        array = array * block_levels(key, dims, pieces, -0.22, 0.18)
    return jnp.clip(spiked(array, jax.random.fold_in(key, 3), *heavy), -most, most).astype(kind)


def setup_inputs(seed: int = 0) -> dict:
    key_list = jax.random.split(jax.random.key(seed), 18)
    return {
        "hidden": normal_values(key_list[0], (TOKENS, D), 1.0, 6.0, ((0, 32),)),
        "time_embed": normal_values(key_list[1], (TOKENS, D), 1.0, 6.0, ((0, 32),)),
        "segment_ids": draw_segment_ids(jax.random.fold_in(key_list[17], 71), 0),
        "ln1_gain": jnp.clip(1.0 + 0.1 * jax.random.normal(key_list[3], (D,), jnp.float32), 0.5, 1.5).astype(jnp.bfloat16),
        "ln1_bias": normal_values(key_list[4], (D,), 0.5, 3.0, ((0, 32),)),
        "w_qkv": normal_values(key_list[5], (D, 3 * D), D ** -0.5, 0.21875, ((1, 32),)),
        "b_query": normal_values(key_list[6], (D,), 0.5, 3.0, ((0, 32),)),
        "b_value": normal_values(key_list[7], (D,), 0.5, 3.0, ((0, 32),)),
        "w_out": normal_values(key_list[8], (D, D), (D // 16) ** -0.5, 0.875, ((1, 32),)),
        "b_out": normal_values(key_list[9], (D,), 0.5, 3.0, ((0, 32),)),
        "ln2_gain": jnp.clip(1.0 + 0.1 * jax.random.normal(key_list[10], (D,), jnp.float32), 0.5, 1.5).astype(jnp.bfloat16),
        "ln2_bias": normal_values(key_list[11], (D,), 0.5, 3.0, ((0, 32),)),
        "w_up": normal_values(key_list[12], (D, FF), D ** -0.5, 0.21875, ((1, 32),)),
        "b_up": normal_values(key_list[13], (FF,), 0.5, 3.0, ((0, 32),)),
        "w_down": normal_values(key_list[14], (FF, D), FF ** -0.5, 0.109375, ((1, 32),)),
        "b_down": normal_values(key_list[15], (D,), 0.5, 3.0, ((0, 32),)),
        "cotangent": noise_with(key_list[16], (TOKENS, D), 1.0, 6.0, ((0, 32),), (0, 1, 32, 2.75)),
    }


epsilon = 1e-05

@jax.custom_vjp
def low(v):
    return lax.optimization_barrier(v.astype(jnp.bfloat16)).astype(jnp.float32)

@jax.custom_vjp
def low_back(v):
    return v

def low_keep(v):
    return (low(v), None)

def low_pass(kept, grad):
    return (grad,)

def back_keep(v):
    return (v, None)

def back_low(kept, grad):
    return (low(grad),)
low.defvjp(low_keep, low_pass)
low_back.defvjp(back_keep, back_low)

def highest(left_side, right_side):
    return jnp.dot(left_side, right_side, precision=lax.Precision.HIGHEST)

def layer_norm(values, gain_vec, shift_vec):
    centred = values - lax.optimization_barrier(jnp.mean(values, axis=-1, keepdims=True))
    variance = lax.optimization_barrier(jnp.mean(centred * centred, axis=-1, keepdims=True))
    return centred * lax.rsqrt(variance + epsilon) * gain_vec + shift_vec

def attend_row(block):
    queries, key_rows, value_rows, segment = block
    score_scale = 1.0 / math.sqrt(HEAD)
    query_heads = queries.reshape(ROW, HEADS, HEAD)
    key_heads = key_rows.reshape(ROW, HEADS, HEAD)
    value_heads = value_rows.reshape(ROW, HEADS, HEAD)
    scores = jnp.einsum('qhd,khd->hqk', query_heads, key_heads, precision=lax.Precision.HIGHEST) * score_scale
    allowed = segment[:, None] == segment[None, :]
    scores = low_back(jnp.where(allowed[None, :, :], scores, -1e+30))
    row_top = lax.optimization_barrier(jnp.max(scores, axis=-1, keepdims=True))
    weights = jnp.exp(scores - row_top)
    probs_full = weights / lax.optimization_barrier(jnp.sum(weights, axis=-1, keepdims=True))
    mixed = jnp.einsum('hqk,khd->qhd', low(probs_full), value_heads, precision=lax.Precision.HIGHEST)
    return mixed.reshape(ROW, HEADS * HEAD)

def reference(hidden, time_embed, segment_ids, ln1_gain, ln1_bias, w_qkv, b_query, b_value, w_out, b_out, ln2_gain, ln2_bias, w_up, b_up, w_down, b_down, cotangent):
    whole_rows = TOKENS // ROW
    row_segments = segment_ids.reshape(whole_rows, ROW)

    def forward(start_rows, embed_rows, gain_first, shift_first, pack_weight, bias_q, bias_v, out_weight, bias_out, gain_second, shift_second, up_weight, bias_up, down_weight, bias_down):
        entered = start_rows + embed_rows
        normed = low(layer_norm(entered, gain_first, shift_first))
        bias_all = jnp.concatenate([bias_q, jnp.zeros_like(bias_q), bias_v])
        packed = low_back(low(highest(normed, pack_weight) + bias_all))
        queries = packed[:, :D].reshape(whole_rows, ROW, D)
        key_rows = packed[:, D:2 * D].reshape(whole_rows, ROW, D)
        value_rows = packed[:, 2 * D:].reshape(whole_rows, ROW, D)
        mixed = lax.map(jax.checkpoint(attend_row), (queries, key_rows, value_rows, row_segments))
        attended = low_back(low(mixed.reshape(TOKENS, D)))
        branch = low_back(highest(attended, out_weight) + bias_out)
        middle = entered + branch
        normed_second = low(layer_norm(middle, gain_second, shift_second))
        pre_act = low_back(highest(normed_second, up_weight) + bias_up)
        activated = low(jax.nn.gelu(pre_act, approximate=True))
        result = low_back(highest(activated, down_weight) + bias_down)
        return middle + result
    floats = tuple((argument.astype(jnp.float32) for argument in (hidden, time_embed, ln1_gain, ln1_bias, w_qkv, b_query, b_value, w_out, b_out, ln2_gain, ln2_bias, w_up, b_up, w_down, b_down)))
    output, pullback = jax.vjp(forward, *floats)
    live_rows = (segment_ids >= 0).astype(jnp.float32)[:, None]
    gradients = pullback(cotangent.astype(jnp.float32) * live_rows)
    return (output.astype(jnp.bfloat16), gradients[0].astype(jnp.bfloat16), gradients[2], gradients[3], gradients[4], gradients[5], gradients[6], gradients[7], gradients[8], gradients[9], gradients[10], gradients[11], gradients[12], gradients[13], gradients[14])
```

```python
from functools import partial
import math

import jax
import jax.numpy as jnp
from jax import lax
from jax.experimental import pallas as pl
from jax.experimental.pallas import tpu as pltpu
from jax.sharding import PartitionSpec as P

D = 768
HEADS = 12
HEAD = 64
FF = 3072
ROW = 1024
BLOCKS = 32
QROWS = 3 * D // BLOCKS
OROWS = D // BLOCKS
UROWS = FF // BLOCKS
CHUNKS = FF // D
FIRST = QROWS + 8
SECOND = 2 * UROWS + OROWS + 8
SHARE = 2 * UROWS + OROWS + QROWS + 16
TOKB = 512
MIB = 2**20
MESH = pl.DeviceIdType.MESH
F32 = jnp.float32
BF16 = jnp.bfloat16
LOG2E = math.log2(math.e)
EPS = 1e-05


def mm(a, b, ca, cb):
    return lax.dot_general(a, b, (((ca,), (cb,)), ((), ())), preferred_element_type=F32)


def normalise(values):
    centred = values - jnp.mean(values, axis=-1, keepdims=True)
    inverse = lax.rsqrt(jnp.mean(centred * centred, axis=-1, keepdims=True) + EPS)
    return centred * inverse, inverse


def norm_back(grad, scaled, inverse, gain):
    u = grad * gain
    return inverse * (
        u
        - jnp.mean(u, axis=-1, keepdims=True)
        - scaled * jnp.mean(u * scaled, axis=-1, keepdims=True)
    )


def column(row):
    return jnp.broadcast_to(row, (128, row.shape[1])).T[:, :1]


def join_rows(source, start, rows, target, pairs):
    low = start // 16 * 16
    high = -(-(start + rows) // 16) * 16

    def step(p, _):
        parts = [
            source[2 * p + i, low:high, :].astype(F32)[start - low : start - low + rows]
            for i in range(2)
        ]
        at = pl.multiple_of(2 * rows * p, 2 * rows)
        target[pl.ds(at, 2 * rows), :] = jnp.concatenate(parts, axis=0).astype(BF16)
        return 0

    lax.fori_loop(0, pairs, step, 0)


def sum_rows(source, start):
    low = start // 16 * 16

    def step(d, total):
        return total + source[d, low : low + 16, :].astype(F32)[start - low : start - low + 8]

    return lax.fori_loop(0, BLOCKS, step, jnp.zeros((8, D), F32))


def mask_rows(segment):
    r = lax.broadcasted_iota(jnp.int32, (32, ROW), 0)
    hit = r == segment + 1
    query_side = jnp.where(hit, 1.0, 0.0).astype(BF16)
    key_side = jnp.where(hit | (r >= 17), 0.0, -1e30).astype(BF16)
    return query_side, key_side


def scaled_query(queries):
    wide = queries.astype(F32) * (LOG2E / 8)
    high = wide.astype(BF16)
    low = (wide - high.astype(F32)).astype(BF16)
    return high, low


def forward_kernel(
    first_ref, second_ref, hid_ref, emb_ref, seg_ref,
    packed_ref, mixed_ref, mid_ref, norm_ref, total_ref, vec_ref,
    w_qkv, w_out, bias_cols, mask_q, mask_k,
):
    row, step = pl.program_id(0), pl.program_id(1)

    @pl.when((row == 0) & (step == 0))
    def _():
        join_rows(first_ref, 0, QROWS, w_qkv, BLOCKS // 2)
        join_rows(second_ref, 0, OROWS, w_out, BLOCKS // 2)
        vec_ref[0] = sum_rows(first_ref, QROWS)
        vec_ref[1] = sum_rows(second_ref, OROWS)
        bias_cols[0] = column(vec_ref[0, 2:3, :])
        bias_cols[1] = jnp.zeros((D, 1), F32)
        bias_cols[2] = column(vec_ref[0, 3:4, :])

    @pl.when(step == 0)
    def _():
        for half in range(ROW // TOKB):
            at = slice(half * TOKB, (half + 1) * TOKB)
            entered = hid_ref[at, :].astype(F32) + emb_ref[at, :].astype(F32)
            scaled, _ = normalise(entered)
            normed = (scaled * vec_ref[0, 0:1, :] + vec_ref[0, 1:2, :]).astype(BF16)
            for part in range(3):
                rows = slice(part * D, (part + 1) * D)
                packed_ref[rows, at] = (mm(w_qkv[rows, :], normed, 1, 1) + bias_cols[part]).astype(BF16)
        query_side, key_side = mask_rows(seg_ref[0])
        mask_q[...] = query_side
        mask_k[...] = key_side

    @pl.when((step >= 1) & (step <= 6))
    def _():
        pair = step - 1
        ones_rows = jnp.where(lax.broadcasted_iota(jnp.int32, (HEAD, ROW), 0) == 0, 1.0, 0.0).astype(BF16)
        sides = []
        for h in range(2):
            at = pl.multiple_of(pair * 128, 128) + HEAD * h
            high, low = scaled_query(packed_ref[pl.ds(at, HEAD), :])
            keys = packed_ref[pl.ds(D + at, HEAD), :]
            sides.append((
                jnp.concatenate([high, low, mask_q[...]], axis=0),
                jnp.concatenate([keys, keys, mask_k[...]], axis=0),
                jnp.concatenate([packed_ref[pl.ds(2 * D + at, HEAD), :], ones_rows], axis=0),
            ))
        all_scores = [mm(sides[h][1], sides[h][0], 0, 0) for h in range(2)]
        mixed = []
        for h in range(2):
            scores = all_scores[h]
            top = jnp.max(scores, axis=0, keepdims=True)
            weights = jnp.exp2(scores - top).astype(BF16)
            summed = mm(sides[h][2], weights, 1, 0)
            total = summed[HEAD : HEAD + 1, :]
            mixed.append(summed[:HEAD, :] / total)
            total_ref[0, h : h + 1, :] = top + jnp.log2(total)
        mixed_ref[:, pl.ds(pl.multiple_of(pair * 128, 128), 128)] = jnp.concatenate(mixed, axis=0).T

    @pl.when(step == 7)
    def _():
        for half in range(ROW // TOKB):
            at = slice(half * TOKB, (half + 1) * TOKB)
            entered = hid_ref[at, :].astype(F32) + emb_ref[at, :].astype(F32)
            middle = entered + mm(mixed_ref[at, :].astype(BF16), w_out[...], 1, 1) + vec_ref[0, 4:5, :]
            scaled, _ = normalise(middle)
            mid_ref[at, :] = middle
            norm_ref[at, :] = (scaled * vec_ref[0, 5:6, :] + vec_ref[0, 6:7, :]).astype(BF16)


def forward(first, second, hidden, embed, segment):
    n = hidden.shape[0]
    rows = n // ROW
    one = pl.Buffered(1)
    tokens = pl.BlockSpec((ROW, D), lambda r, s: (r, 0))
    return pl.pallas_call(
        forward_kernel,
        grid=(rows, 8),
        in_specs=[
            pl.BlockSpec((BLOCKS, FIRST, D), lambda r, s: (0, 0, 0), pipeline_mode=one),
            pl.BlockSpec((BLOCKS, 32, D), lambda r, s: (0, 6, 0), pipeline_mode=one),
            tokens,
            tokens,
            pl.BlockSpec((1, 1, ROW), lambda r, s: (r, 0, 0)),
        ],
        out_specs=[
            pl.BlockSpec((3 * D, ROW), lambda r, s: (0, r)),
            tokens,
            tokens,
            tokens,
            pl.BlockSpec((1, 8, ROW), lambda r, s: (jnp.clip(s - 1, 0, 5), 0, r)),
            pl.BlockSpec((2, 8, D), lambda r, s: (0, 0, 0)),
        ],
        out_shape=[
            jax.ShapeDtypeStruct((3 * D, n), BF16),
            jax.ShapeDtypeStruct((n, D), F32),
            jax.ShapeDtypeStruct((n, D), F32),
            jax.ShapeDtypeStruct((n, D), BF16),
            jax.ShapeDtypeStruct((HEADS // 2, 8, n), F32),
            jax.ShapeDtypeStruct((2, 8, D), F32),
        ],
        scratch_shapes=[
            pltpu.VMEM((3 * D, D), BF16),
            pltpu.VMEM((D, D), BF16),
            pltpu.VMEM((3, D, 1), F32),
            pltpu.VMEM((32, ROW), BF16),
            pltpu.VMEM((32, ROW), BF16),
        ],
        compiler_params=pltpu.CompilerParams(vmem_limit_bytes=60 * MIB),
        name="attention_forward",
    )(first, second, hidden, embed, segment.reshape(rows, 1, ROW))


def feed_kernel(
    up_ref, down_ref, vec_ref, norm_ref, mid_ref, cot_ref, seg_ref,
    out_ref, gmid_ref, gup_ref, gdown_ref, gvec_ref,
    w_down, result, back, live,
):
    j, i = pl.program_id(0), pl.program_id(1)
    at = pl.ds(pl.multiple_of(i * TOKB, TOKB), TOKB)

    @pl.when(i == 0)
    def _():
        for chunk in range(CHUNKS):
            @pl.when(j == chunk)
            def _():
                join_rows(down_ref, chunk * OROWS, OROWS, w_down, BLOCKS // 2)

    @pl.when((j == 0) & (i == 0))
    def _():
        gvec_ref[...] = jnp.zeros_like(gvec_ref)

    @pl.when(j == 0)
    def _():
        keep = column(jnp.where(seg_ref[0] >= 0, 1.0, 0.0))
        grad_result = cot_ref[...].astype(F32) * keep
        live[at, :] = grad_result.astype(BF16)
        gvec_ref[4:5, :] += jnp.sum(grad_result, axis=0, keepdims=True)

    normed = norm_ref[...]
    grad_result = live[at, :]
    up = up_ref[...].reshape(D, D)
    down = w_down[...]
    x = mm(normed, up, 1, 1) + vec_ref[1, pl.ds(j, 1), :]
    grad_act = mm(grad_result, down, 1, 0)
    c0 = math.sqrt(2.0 / math.pi)
    c1 = 0.044715
    square = x * x
    th = jnp.tanh(x * (c0 + (c0 * c1) * square))
    half = 0.5 + 0.5 * th
    activated = (x * half).astype(BF16)
    slope = half + (0.5 * x) * ((1.0 - th * th) * (c0 + (3 * c0 * c1) * square))
    grad_pre32 = grad_act * slope
    grad_pre = grad_pre32.astype(BF16)
    gvec_ref[pl.ds(j, 1), :] += jnp.sum(grad_pre.astype(F32), axis=0, keepdims=True)
    part = mm(activated, down, 1, 1)
    part_back = mm(grad_pre, up, 1, 0)
    part_down = mm(grad_result, activated, 0, 0)
    part_up = mm(grad_pre, normed, 0, 0)

    @pl.when(i == 0)
    def _():
        gdown_ref[0] = part_down
        gup_ref[...] = part_up

    @pl.when(i > 0)
    def _():
        gdown_ref[0] += part_down
        gup_ref[...] += part_up

    @pl.when(j == 0)
    def _():
        result[at, :] = part
        back[at, :] = part_back

    @pl.when((j > 0) & (j < CHUNKS - 1))
    def _():
        result[at, :] += part
        back[at, :] += part_back

    @pl.when(j == CHUNKS - 1)
    def _():
        middle = mid_ref[...]
        out_ref[...] = (middle + (result[at, :] + part + vec_ref[0, 7:8, :])).astype(BF16)
        grad = back[at, :] + part_back
        scaled, inverse = normalise(middle)
        gvec_ref[5:6, :] += jnp.sum(grad * scaled, axis=0, keepdims=True)
        gvec_ref[6:7, :] += jnp.sum(grad, axis=0, keepdims=True)
        gmid_ref[...] = grad_result.astype(F32) + norm_back(grad, scaled, inverse, vec_ref[0, 5:6, :])


def feed(second, vec, normed, middle, cotangent, segment):
    n = normed.shape[0]
    blocks = n // TOKB
    one = pl.Buffered(1)
    last = CHUNKS - 1
    tokens = pl.BlockSpec((TOKB, D), lambda j, i: (i, 0))
    at_first = pl.BlockSpec((TOKB, D), lambda j, i: (jnp.where(j == 0, i, blocks - 1), 0))
    at_last = pl.BlockSpec((TOKB, D), lambda j, i: (jnp.where(j == last, i, 0), 0))
    return pl.pallas_call(
        feed_kernel,
        grid=(CHUNKS, blocks),
        in_specs=[
            pl.BlockSpec((BLOCKS // CHUNKS, UROWS, D), lambda j, i: (j, 0, 0)),
            pl.BlockSpec((BLOCKS, UROWS, D), lambda j, i: (0, 1, 0), pipeline_mode=one),
            pl.BlockSpec((2, 8, D), lambda j, i: (0, 0, 0)),
            tokens,
            at_last,
            at_first,
            pl.BlockSpec((1, 1, TOKB), lambda j, i: (i, 0, 0)),
        ],
        out_specs=[
            at_last,
            at_last,
            pl.BlockSpec((D, D), lambda j, i: (j, 0)),
            pl.BlockSpec((1, D, D), lambda j, i: (j, 0, 0)),
            pl.BlockSpec((8, D), lambda j, i: (0, 0)),
        ],
        out_shape=[
            jax.ShapeDtypeStruct((n, D), BF16),
            jax.ShapeDtypeStruct((n, D), F32),
            jax.ShapeDtypeStruct((FF, D), F32),
            jax.ShapeDtypeStruct((CHUNKS, D, D), F32),
            jax.ShapeDtypeStruct((8, D), F32),
        ],
        scratch_shapes=[
            pltpu.VMEM((D, D), BF16),
            pltpu.VMEM((n, D), F32),
            pltpu.VMEM((n, D), F32),
            pltpu.VMEM((n, D), BF16),
        ],
        compiler_params=pltpu.CompilerParams(vmem_limit_bytes=60 * MIB),
        name="feed_forward",
    )(second, second, vec, normed, middle, cotangent, segment.reshape(blocks, 1, TOKB))


def three_parts(row):
    r = lax.broadcasted_iota(jnp.int32, (16, row.shape[1]), 0)
    a = row.astype(BF16).astype(F32)
    b = (row - a).astype(BF16).astype(F32)
    c = row - a - b
    return jnp.where(r == 0, -a, jnp.where(r == 1, -b, jnp.where(r == 2, -c, 0.0))).astype(BF16)


def backward_kernel(
    first_ref, second_ref, vec_ref, hid_ref, emb_ref, seg_ref, packed_q, packed_k, packed_v,
    mixed_ref, total_ref, gmid_ref,
    ghid_ref, gout_ref, gqkv_ref, gvec_ref,
    w_qkv, w_out, mask_q, mask_k, grad_mixed, delta, grad_packed,
):
    row, step = pl.program_id(0), pl.program_id(1)

    @pl.when((row == 0) & (step == 0))
    def _():
        join_rows(first_ref, 0, QROWS, w_qkv, BLOCKS // 2)
        join_rows(second_ref, 0, OROWS, w_out, BLOCKS // 2)
        gvec_ref[...] = jnp.zeros_like(gvec_ref)
        gout_ref[...] = jnp.zeros_like(gout_ref)
        gqkv_ref[...] = jnp.zeros_like(gqkv_ref)

    @pl.when(step == 0)
    def _():
        query_side, key_side = mask_rows(seg_ref[0])
        mask_q[...] = query_side
        mask_k[...] = key_side

    @pl.when(step < 2)
    def _():
        at = pl.ds(pl.multiple_of(step * TOKB, TOKB), TOKB)
        mixed = mixed_ref[...]
        branch = gmid_ref[...].astype(BF16)
        gvec_ref[4:5, :] += jnp.sum(branch.astype(F32), axis=0, keepdims=True)
        gout_ref[...] += mm(branch, mixed.astype(BF16), 0, 0)
        grad = mm(branch, w_out[...], 1, 0).astype(BF16).astype(F32)
        grad_mixed[:, at] = grad.T.astype(BF16)
        inner = (grad * mixed).T
        delta[:, at] = jnp.concatenate(
            [jnp.sum(inner[HEAD * h : HEAD * (h + 1)], axis=0, keepdims=True) for h in range(HEADS)]
            + [jnp.zeros((16 - HEADS, TOKB), F32)],
            axis=0,
        )

    @pl.when((step >= 2) & (step < 8))
    def _():
        pair = step - 2
        r = lax.broadcasted_iota(jnp.int32, (16, ROW), 0)
        ones_rows = jnp.where(r < 3, 1.0, 0.0).astype(BF16)
        base = pl.multiple_of(pair * 128, 128)
        for h in range(2):
            rows = slice(HEAD * h, HEAD * (h + 1))
            queries, keys, values = packed_q[rows, :], packed_k[rows, :], packed_v[rows, :]
            grad = grad_mixed[pl.ds(base + HEAD * h, HEAD), :]
            high, low = scaled_query(queries)
            wide_q = jnp.concatenate([high, low, mask_q[...], three_parts(total_ref[0, h : h + 1, :])], axis=0)
            wide_k = jnp.concatenate([keys, keys, mask_k[...], ones_rows], axis=0)
            wide_g = jnp.concatenate([grad, three_parts(delta[pl.ds(2 * pair + h, 1), :])], axis=0)
            wide_v = jnp.concatenate([values, ones_rows], axis=0)
            grad_v = jnp.zeros((HEAD, ROW), F32)
            grad_k = jnp.zeros((HEAD, ROW), F32)
            grad_q = []
            for half in range(2):
                at = slice(half * (ROW // 2), (half + 1) * (ROW // 2))
                probs = jnp.exp2(mm(wide_q[:, at], wide_k, 0, 0))
                grad_probs = mm(wide_g[:, at], wide_v, 0, 0)
                grad_scores = (probs * grad_probs).astype(BF16)
                grad_v = grad_v + mm(grad[:, at], probs.astype(BF16), 1, 0)
                grad_k = grad_k + mm(queries[:, at], grad_scores, 1, 0)
                grad_q.append(mm(keys, grad_scores, 1, 1))
            grad_packed[pl.ds(base + HEAD * h, HEAD), :] = (jnp.concatenate(grad_q, axis=1) * 0.125).astype(BF16)
            grad_packed[pl.ds(D + base + HEAD * h, HEAD), :] = (grad_k * 0.125).astype(BF16)
            grad_packed[pl.ds(2 * D + base + HEAD * h, HEAD), :] = grad_v.astype(BF16)

    @pl.when(step >= 8)
    def _():
        at = pl.ds(pl.multiple_of((step - 8) * TOKB, TOKB), TOKB)
        entered = hid_ref[...].astype(F32) + emb_ref[...].astype(F32)
        scaled, inverse = normalise(entered)
        normed = (scaled * vec_ref[0, 0:1, :] + vec_ref[0, 1:2, :]).astype(BF16)
        for part in range(3):
            rows = slice(part * D, (part + 1) * D)
            gqkv_ref[rows, :] += mm(grad_packed[rows, at], normed, 1, 0)
        grad = mm(grad_packed[:, at], w_qkv[...], 0, 0)
        ones = jnp.ones((16, TOKB), BF16)
        gvec_ref[0:1, :] += jnp.sum(grad * scaled, axis=0, keepdims=True)
        gvec_ref[1:2, :] += jnp.sum(grad, axis=0, keepdims=True)
        gvec_ref[2:3, :] += mm(ones, grad_packed[0:D, at], 1, 1)[0:1, :]
        gvec_ref[3:4, :] += mm(ones, grad_packed[2 * D : 3 * D, at], 1, 1)[0:1, :]
        ghid_ref[...] = (gmid_ref[...] + norm_back(grad, scaled, inverse, vec_ref[0, 0:1, :])).astype(BF16)


def backward(first, second, vec, hidden, embed, segment, packed, mixed, totals, gmid):
    n = hidden.shape[0]
    rows = n // ROW
    one = pl.Buffered(1)

    def early(r, s):
        return (2 * r + jnp.clip(s, 0, 1), 0)

    def late(r, s):
        return (2 * r + jnp.clip(s - 8, 0, 1), 0)

    def both(r, s):
        return (2 * r + jnp.where(s < 8, jnp.clip(s, 0, 1), s - 8), 0)

    def pair(s):
        return jnp.clip(s - 2, 0, 5)

    return pl.pallas_call(
        backward_kernel,
        grid=(rows, 10),
        in_specs=[
            pl.BlockSpec((BLOCKS, FIRST, D), lambda r, s: (0, 0, 0), pipeline_mode=one),
            pl.BlockSpec((BLOCKS, 32, D), lambda r, s: (0, 6, 0), pipeline_mode=one),
            pl.BlockSpec((2, 8, D), lambda r, s: (0, 0, 0)),
            pl.BlockSpec((TOKB, D), late),
            pl.BlockSpec((TOKB, D), late),
            pl.BlockSpec((1, 1, ROW), lambda r, s: (r, 0, 0)),
            pl.BlockSpec((128, ROW), lambda r, s: (pair(s), r)),
            pl.BlockSpec((128, ROW), lambda r, s: (6 + pair(s), r)),
            pl.BlockSpec((128, ROW), lambda r, s: (12 + pair(s), r)),
            pl.BlockSpec((TOKB, D), early),
            pl.BlockSpec((1, 8, ROW), lambda r, s: (pair(s), 0, r)),
            pl.BlockSpec((TOKB, D), both),
        ],
        out_specs=[
            pl.BlockSpec((TOKB, D), late),
            pl.BlockSpec((D, D), lambda r, s: (0, 0)),
            pl.BlockSpec((3 * D, D), lambda r, s: (0, 0), pipeline_mode=one),
            pl.BlockSpec((8, D), lambda r, s: (0, 0)),
        ],
        out_shape=[
            jax.ShapeDtypeStruct((n, D), BF16),
            jax.ShapeDtypeStruct((D, D), F32),
            jax.ShapeDtypeStruct((3 * D, D), F32),
            jax.ShapeDtypeStruct((8, D), F32),
        ],
        scratch_shapes=[
            pltpu.VMEM((3 * D, D), BF16),
            pltpu.VMEM((D, D), BF16),
            pltpu.VMEM((32, ROW), BF16),
            pltpu.VMEM((32, ROW), BF16),
            pltpu.VMEM((D, ROW), BF16),
            pltpu.VMEM((16, ROW), F32),
            pltpu.VMEM((3 * D, ROW), BF16),
        ],
        compiler_params=pltpu.CompilerParams(vmem_limit_bytes=62 * MIB),
        name="attention_backward",
    )(first, second, vec, hidden, embed, segment.reshape(rows, 1, ROW), packed, packed, packed, mixed, totals, gmid)


class Place:
    def __init__(self, planes, side):
        self.planes, self.side = planes, side
        group, cell = lax.axis_index("dp"), lax.axis_index("fsdp")
        self.z, self.core = group // 2, group % 2
        y, x = cell // side, cell % side
        self.step_a = 1 + self.core * (side - 1)
        self.step_b = side - self.core * (side - 1)
        self.a = x + self.core * (y - x)
        self.b = y + self.core * (x - y)

    def plane(self, k):
        return lax.rem(self.z + k + self.planes, self.planes)

    def at(self, z, core, a, b):
        return (z * 2 + core, a * self.step_a + b * self.step_b)

    def block(self, z, a, b):
        return (z * 2 + self.core) * (self.side * self.side) + a * self.step_a + b * self.step_b

    def run(self, z, core):
        return (z * 2 + core) * (self.side * self.side)

    def across_a(self):
        return self.at(self.z, self.core, 1 - self.a, self.b)

    def across_b(self):
        return self.at(self.z, self.core, self.a, 1 - self.b)

    def other_core(self):
        return (self.z * 2 + 1 - self.core, self.a * self.step_a + self.b * self.step_b)

    def along_z(self, k):
        return self.at(self.plane(k), self.core, self.a, self.b)

    def greet(self):
        barrier = pltpu.get_barrier_semaphore()
        peers = [self.along_z(k) for k in range(1, self.planes)]
        peers += [self.across_a(), self.across_b(), self.other_core()]
        for peer in peers:
            pl.semaphore_signal(barrier, inc=1, device_id=peer, device_id_type=MESH)
        pl.semaphore_wait(barrier, len(peers))


def gather_steps(place, own, full, send, recv):
    planes = place.planes
    cells = place.side * place.side
    started = []

    def copy(slot, source, target, to):
        c = pltpu.make_async_remote_copy(
            src_ref=source, dst_ref=target, send_sem=send.at[slot], recv_sem=recv.at[slot],
            device_id=to, device_id_type=MESH,
        )
        c.start()
        started.append(c)
        return c

    me = place.block(place.z, place.a, place.b)
    state = {}
    local = pltpu.make_async_copy(own, full.at[me], send.at[5 * planes])

    def start():
        local.start()
        for k in range(1, planes):
            state["z", k] = copy(k, own, full.at[me], place.along_z(k))

    def column_block(k):
        if k == 0:
            return own, full.at[me]
        at = full.at[place.block(place.plane(-k), place.a, place.b)]
        return at, at

    def arrive_z(k):
        if k:
            state["z", k].wait_recv()
        source, target = column_block(k)
        state["a", k] = copy(planes + k, source, target, place.across_a())
        state["b", k] = copy(2 * planes + k, source, target, place.across_b())

    def arrive_a(k):
        state["a", k].wait_recv()
        at = full.at[place.block(place.plane(-k), 1 - place.a, place.b)]
        state["d", k] = copy(3 * planes + k, at, at, place.across_b())

    def arrive_b(k):
        state["b", k].wait_recv()
        state["d", k].wait_recv()
        if k == 0:
            local.wait()
        at = full.at[pl.ds(place.run(place.plane(-k), place.core), cells)]
        state["c", k] = copy(4 * planes + k, at, at, place.other_core())

    def finish():
        for k in range(planes):
            state["c", k].wait_recv()
        for c in started:
            c.wait_send()

    steps = [start]
    for t in range(planes + 2):
        if t < planes:
            steps.append(partial(arrive_z, t))
        if 0 <= t - 1 < planes:
            steps.append(partial(arrive_a, t - 1))
        if 0 <= t - 2 < planes:
            steps.append(partial(arrive_b, t - 2))
    steps.append(finish)
    return steps


def gather_kernel(planes, side, own1, own2, full1, full2, send1, recv1, send2, recv2):
    place = Place(planes, side)
    place.greet()
    for step in gather_steps(place, own1, full1, send1, recv1):
        step()
    for step in gather_steps(place, own2, full2, send2, recv2):
        step()


def gather(planes, side, own1, own2):
    sems = [pltpu.SemaphoreType.DMA((5 * planes + 1,))] * 4
    hbm = pl.BlockSpec(memory_space=pl.ANY)
    return pl.pallas_call(
        partial(gather_kernel, planes, side),
        in_specs=[hbm] * 2,
        out_specs=[hbm] * 2,
        out_shape=[
            jax.ShapeDtypeStruct((BLOCKS,) + own1.shape, BF16),
            jax.ShapeDtypeStruct((BLOCKS,) + own2.shape, BF16),
        ],
        scratch_shapes=sems,
        compiler_params=pltpu.CompilerParams(collective_id=1, has_side_effects=True),
        name="gather_weights",
    )(own1, own2)


def scatter_kernel(
    planes, side, up, down, out, qkv, vec,
    mine,
    theirs_up, theirs_down, theirs_out, theirs_qkv, theirs_vec,
    ours_up, ours_down, ours_out, ours_qkv, ours_vec,
    share, got_b, got_a, got_z,
    send1, recv1, load, send, recv, vec_sems,
):
    place = Place(planes, side)
    place.greet()
    cells = side * side

    def pieces(z, core):
        first = place.run(z, core)
        return (
            up.at[pl.ds(first * UROWS, cells * UROWS)],
            down.at[:, pl.ds(first * OROWS, cells * OROWS)],
            out.at[pl.ds(first * OROWS, cells * OROWS)],
            qkv.at[pl.ds(first * QROWS, cells * QROWS)],
        )

    theirs = (theirs_up, theirs_down, theirs_out, theirs_qkv)
    ours = (ours_up, ours_down, ours_out, ours_qkv)
    order = list(range(1, planes)) + [0]
    vec_copy = pltpu.make_async_remote_copy(
        src_ref=vec, dst_ref=theirs_vec, send_sem=vec_sems.at[0], recv_sem=vec_sems.at[1],
        device_id=place.other_core(), device_id_type=MESH,
    )
    vec_copy.start()
    vec_load = pltpu.make_async_copy(vec, ours_vec, vec_sems.at[2])
    vec_load.start()
    outgoing, started = {}, []
    for k in order:
        for i, piece in enumerate(pieces(place.plane(k), 1 - place.core)):
            c = pltpu.make_async_remote_copy(
                src_ref=piece, dst_ref=theirs[i].at[k], send_sem=send1.at[k, i], recv_sem=recv1.at[k, i],
                device_id=place.other_core(), device_id_type=MESH,
            )
            c.start()
            outgoing[k, i] = c
            started.append(c)

    def loads(t):
        k = order[t]
        return [
            pltpu.make_async_copy(piece, ours[i].at[t % 2], load.at[t % 2, i])
            for i, piece in enumerate(pieces(place.plane(k), place.core))
        ]

    def copy(slot, source, target, to):
        c = pltpu.make_async_remote_copy(
            src_ref=source, dst_ref=target, send_sem=send.at[slot], recv_sem=recv.at[slot],
            device_id=to, device_id_type=MESH,
        )
        c.start()
        started.append(c)
        return c

    state = {}
    for c in loads(0):
        c.start()
    vec_copy.wait()
    vec_load.wait()

    def arrive_core(t):
        k = order[t]
        if t + 1 < planes:
            for c in loads(t + 1):
                c.start()
        for i, c in enumerate(loads(t)):
            c.wait()
            outgoing[k, i].wait_recv()
        s = t % 2
        vec_sum = ours_vec[...] + theirs_vec[...]

        def one(cell, _):
            u = pl.ds(pl.multiple_of(cell * UROWS, UROWS), UROWS)
            o = pl.ds(pl.multiple_of(cell * OROWS, OROWS), OROWS)
            q = pl.ds(pl.multiple_of(cell * QROWS, QROWS), QROWS)
            rows = [ours_up[s, u] + theirs_up[k, u]]
            rows += [ours_down[s, c, o] + theirs_down[k, c, o] for c in range(CHUNKS)]
            rows += [ours_out[s, o] + theirs_out[k, o], ours_qkv[s, q] + theirs_qkv[k, q], vec_sum]
            y, x = cell // side, cell % side
            a = x + place.core * (y - x)
            b = y + place.core * (x - y)
            share[k, b, a] = jnp.concatenate(rows, axis=0).astype(BF16)
            return 0

        lax.fori_loop(0, cells, one, 0)
        state["b", k] = copy(k, share.at[k, 1 - place.b], got_b.at[k], place.across_b())

    def arrive_b(t):
        k = order[t]
        state["b", k].wait_recv()
        for a in range(side):
            share[k, place.b, a] = (share[k, place.b, a].astype(F32) + got_b[k, a].astype(F32)).astype(BF16)
        state["a", k] = copy(planes + k, share.at[k, place.b, 1 - place.a], got_a.at[k], place.across_a())

    def arrive_a(t):
        k = order[t]
        state["a", k].wait_recv()
        total = share[k, place.b, place.a].astype(F32) + got_a[k].astype(F32)
        if k == 0:
            mine[...] = total
        else:
            share[k, place.b, place.a] = total.astype(BF16)
            state["z", k] = copy(2 * planes + k, share.at[k, place.b, place.a], got_z.at[k], place.along_z(k))

    for t in range(planes + 2):
        if t < planes:
            arrive_core(t)
        if 0 <= t - 1 < planes:
            arrive_b(t - 1)
        if 0 <= t - 2 < planes:
            arrive_a(t - 2)
    for k in range(1, planes):
        state["z", k].wait_recv()
        mine[...] += got_z[k].astype(F32)
    for c in started:
        c.wait_send()


def scatter(planes, side, up, down, out, qkv, vec):
    cells = side * side
    hbm = pl.BlockSpec(memory_space=pl.ANY)
    wide = pltpu.VMEM

    def buffers(count):
        return [
            wide((count, cells * UROWS, D), F32),
            wide((count, CHUNKS, cells * OROWS, D), F32),
            wide((count, cells * OROWS, D), F32),
            wide((count, cells * QROWS, D), F32),
        ]

    return pl.pallas_call(
        partial(scatter_kernel, planes, side),
        in_specs=[hbm] * 5,
        out_specs=pl.BlockSpec(memory_space=pltpu.VMEM),
        out_shape=jax.ShapeDtypeStruct((SHARE, D), F32),
        scratch_shapes=buffers(planes)
        + [wide((16, D), F32)]
        + buffers(2)
        + [wide((16, D), F32)]
        + [
            wide((planes, side, side, SHARE, D), BF16),
            wide((planes, side, SHARE, D), BF16),
            wide((planes, SHARE, D), BF16),
            wide((planes, SHARE, D), BF16),
            pltpu.SemaphoreType.DMA((planes, 4)),
            pltpu.SemaphoreType.DMA((planes, 4)),
            pltpu.SemaphoreType.DMA((2, 4)),
            pltpu.SemaphoreType.DMA((3 * planes,)),
            pltpu.SemaphoreType.DMA((3 * planes,)),
            pltpu.SemaphoreType.DMA((3,)),
        ],
        compiler_params=pltpu.CompilerParams(
            collective_id=2, has_side_effects=True, vmem_limit_bytes=60 * MIB
        ),
        name="scatter_gradients",
    )(up, down, out, qkv, vec)


def placed(vector, index, devices):
    here = (jnp.arange(devices) == index)[:, None]
    return jnp.where(here, vector[None, :], jnp.zeros((), vector.dtype)).reshape(-1)


def body(
    planes, side, devices,
    hidden, time_embed, segment_ids,
    ln1_gain, ln1_bias, w_qkv, b_query, b_value, w_out, b_out, ln2_gain, ln2_bias, w_up, b_up, w_down, b_down,
    cotangent,
):
    index = lax.axis_index("dp") * lax.axis_size("fsdp") + lax.axis_index("fsdp")
    axes = ("dp", "fsdp")
    small = (ln1_gain, ln1_bias, b_query, b_value, b_out, ln2_gain, ln2_bias, b_down)
    if planes:
        vec1 = jnp.stack([placed(v, index, devices) for v in small])
        vec2 = placed(b_up, index, devices).reshape(CHUNKS, D)
        vec2 = jnp.concatenate([vec2, jnp.zeros((8 - CHUNKS, D), BF16)], axis=0)
        down_rows = w_down.T.reshape(OROWS, CHUNKS, D).transpose(1, 0, 2).reshape(UROWS, D)
        own1 = jnp.concatenate([w_qkv.T, vec1], axis=0)
        own2 = jnp.concatenate([w_up.T, down_rows, w_out.T, vec2], axis=0)
        first, second = gather(planes, side, own1, own2)
    else:
        def whole(a, dim):
            return lax.all_gather(a, axes, axis=dim, tiled=True)

        def only_first(rows):
            return jnp.concatenate([rows[None], jnp.zeros((BLOCKS - 1,) + rows.shape, BF16)], axis=0)

        vec1 = jnp.stack([whole(v, 0) for v in small])
        vec2 = jnp.concatenate([whole(b_up, 0).reshape(CHUNKS, D), jnp.zeros((8 - CHUNKS, D), BF16)], axis=0)
        down_rows = whole(w_down, 1).T.reshape(BLOCKS, OROWS, CHUNKS, D).transpose(0, 2, 1, 3)
        first = jnp.concatenate([whole(w_qkv, 1).T.reshape(BLOCKS, QROWS, D), only_first(vec1)], axis=1)
        second = jnp.concatenate(
            [
                whole(w_up, 1).T.reshape(BLOCKS, UROWS, D),
                down_rows.reshape(BLOCKS, UROWS, D),
                whole(w_out, 1).T.reshape(BLOCKS, OROWS, D),
                only_first(vec2),
            ],
            axis=1,
        )
    packed, mixed, middle, normed, totals, vec = forward(first, second, hidden, time_embed, segment_ids)
    output, gmid, gup, gdown, gvec_feed = feed(second, vec, normed, middle, cotangent, segment_ids)
    ghid, gout, gqkv, gvec = backward(
        first, second, vec, hidden, time_embed, segment_ids, packed, mixed, totals, gmid
    )
    if planes:
        mine = scatter(planes, side, gup, gdown, gout, gqkv, jnp.concatenate([gvec_feed, gvec], axis=0))
        cuts = (UROWS, 2 * UROWS, 2 * UROWS + OROWS, 2 * UROWS + OROWS + QROWS)
        part_up = mine[: cuts[0]]
        part_down = mine[cuts[0] : cuts[1]].reshape(CHUNKS, OROWS, D).transpose(1, 0, 2).reshape(OROWS, FF)
        part_out = mine[cuts[1] : cuts[2]]
        part_qkv = mine[cuts[2] : cuts[3]]
        vectors = mine[cuts[3] :]
        short = lax.dynamic_slice(vectors, (0, index * OROWS), (16, OROWS))
        part_bup = lax.dynamic_slice(vectors[:CHUNKS].reshape(-1), (index * UROWS,), (UROWS,))
    else:
        def shared(a, dim):
            return lax.psum_scatter(a, axes, scatter_dimension=dim, tiled=True)

        part_up = shared(gup, 0)
        part_down = shared(gdown.transpose(1, 0, 2).reshape(D, FF), 0)
        part_out = shared(gout, 0)
        part_qkv = shared(gqkv, 0)
        short = shared(jnp.concatenate([gvec_feed, gvec], axis=0), 1)
        part_bup = shared(gvec_feed[:CHUNKS].reshape(-1), 0)
    return (
        output, ghid,
        short[8], short[9], part_qkv.T, short[10], short[11], part_out.T, short[12],
        short[5], short[6], part_up.T, part_bup, part_down.T, short[4],
    )


def solution(mesh):
    groups, cells = mesh.shape["dp"], mesh.shape["fsdp"]
    side = math.isqrt(cells)
    own_transfers = groups * cells == BLOCKS and side == 2 and cells == 4 and groups % 2 == 0
    split = ("dp", "fsdp")
    rows, flat, cols = P(split, None), P(split), P(None, split)
    return jax.shard_map(
        partial(body, groups // 2 if own_transfers else 0, side, groups * cells),
        mesh=mesh,
        in_specs=(
            rows, rows, flat, flat, flat, cols, flat, flat, cols, flat, flat, flat, cols, flat, cols, flat, rows,
        ),
        out_specs=(
            rows, rows, flat, flat, cols, flat, flat, cols, flat, flat, flat, cols, flat, cols, flat,
        ),
        check_vma=False,
    )
```

```python
from functools import partial
import math

import jax
import jax.numpy as jnp
from jax import lax
from jax.experimental import pallas as pl
from jax.experimental.pallas import tpu as pltpu
from jax.sharding import PartitionSpec as P

D = 768
HEADS = 12
HEAD = 64
FF = 3072
ROW = 1024
BLOCKS = 32
QROWS = 3 * D // BLOCKS
OROWS = D // BLOCKS
UROWS = FF // BLOCKS
CHUNKS = FF // D
FIRST = QROWS + 8
SECOND = 2 * UROWS + OROWS + 8
SHARE = 2 * UROWS + OROWS + QROWS + 16
TOKB = 512
MIB = 2**20
MESH = pl.DeviceIdType.MESH
F32 = jnp.float32
BF16 = jnp.bfloat16
LOG2E = math.log2(math.e)
EPS = 1e-05


def mm(a, b, ca, cb):
    return lax.dot_general(a, b, (((ca,), (cb,)), ((), ())), preferred_element_type=F32)


def normalise(values):
    centred = values - jnp.mean(values, axis=-1, keepdims=True)
    inverse = lax.rsqrt(jnp.mean(centred * centred, axis=-1, keepdims=True) + EPS)
    return centred * inverse, inverse


def norm_back(grad, scaled, inverse, gain):
    u = grad * gain
    return inverse * (
        u
        - jnp.mean(u, axis=-1, keepdims=True)
        - scaled * jnp.mean(u * scaled, axis=-1, keepdims=True)
    )


def column(row):
    return jnp.broadcast_to(row, (128, row.shape[1])).T[:, :1]


def join_rows(source, start, rows, target, pairs):
    low = start // 16 * 16
    high = -(-(start + rows) // 16) * 16

    def step(p, _):
        parts = [
            source[2 * p + i, low:high, :].astype(F32)[start - low : start - low + rows]
            for i in range(2)
        ]
        at = pl.multiple_of(2 * rows * p, 2 * rows)
        target[pl.ds(at, 2 * rows), :] = jnp.concatenate(parts, axis=0).astype(BF16)
        return 0

    lax.fori_loop(0, pairs, step, 0)


def sum_rows(source, start):
    low = start // 16 * 16

    def step(d, total):
        return total + source[d, low : low + 16, :].astype(F32)[start - low : start - low + 8]

    return lax.fori_loop(0, BLOCKS, step, jnp.zeros((8, D), F32))


def mask_rows(segment):
    r = lax.broadcasted_iota(jnp.int32, (32, ROW), 0)
    hit = r == segment + 1
    query_side = jnp.where(hit, 1.0, 0.0).astype(BF16)
    key_side = jnp.where(hit | (r >= 17), 0.0, -1e30).astype(BF16)
    return query_side, key_side


def scaled_query(queries):
    wide = queries.astype(F32) * (LOG2E / 8)
    high = wide.astype(BF16)
    low = (wide - high.astype(F32)).astype(BF16)
    return high, low


class Place:
    def __init__(self, planes, side):
        self.planes, self.side = planes, side
        group, cell = lax.axis_index("dp"), lax.axis_index("fsdp")
        self.z, self.core = group // 2, group % 2
        y, x = cell // side, cell % side
        self.step_a = 1 + self.core * (side - 1)
        self.step_b = side - self.core * (side - 1)
        self.a = x + self.core * (y - x)
        self.b = y + self.core * (x - y)

    def plane(self, k):
        return lax.rem(self.z + k + self.planes, self.planes)

    def at(self, z, core, a, b):
        return (z * 2 + core, a * self.step_a + b * self.step_b)

    def block(self, z, a, b):
        return (z * 2 + self.core) * (self.side * self.side) + a * self.step_a + b * self.step_b

    def run(self, z, core):
        return (z * 2 + core) * (self.side * self.side)

    def across_a(self):
        return self.at(self.z, self.core, 1 - self.a, self.b)

    def across_b(self):
        return self.at(self.z, self.core, self.a, 1 - self.b)

    def other_core(self):
        return (self.z * 2 + 1 - self.core, self.a * self.step_a + self.b * self.step_b)

    def along_z(self, k):
        return self.at(self.plane(k), self.core, self.a, self.b)

    def greet(self):
        barrier = pltpu.get_barrier_semaphore()
        peers = [self.along_z(k) for k in range(1, self.planes)]
        peers += [self.across_a(), self.across_b(), self.other_core()]
        for peer in peers:
            pl.semaphore_signal(barrier, inc=1, device_id=peer, device_id_type=MESH)
        pl.semaphore_wait(barrier, len(peers))


class Gather:
    def __init__(self, place, own, full, send, recv):
        self.place, self.own, self.full, self.send, self.recv = place, own, full, send, recv
        self.planes = place.planes
        self.slots = Gather.all_slots(place.planes)

    @staticmethod
    def all_slots(planes):
        return [(0, 0)] + [(d, k) for k in range(1, planes) for d in (1, -1)]

    @staticmethod
    def semaphores(planes):
        return pltpu.SemaphoreType.DMA((5 * len(Gather.all_slots(planes)) + 1,))

    def plane(self, slot):
        return self.place.z - slot[0] * slot[1]

    def onward(self, d):
        return self.place.z + 1 < self.planes if d == 1 else self.place.z >= 1

    def here(self, slot):
        return self.place.z >= slot[1] if slot[0] == 1 else self.place.z + slot[1] < self.planes

    def when(self, slot, action):
        if slot[1]:
            pl.when(self.here(slot))(action)
        else:
            action()

    def copy(self, kind, slot):
        place, full, count = self.place, self.full, len(self.slots)
        d, k = slot
        column = full.at[place.block(self.plane(slot), place.a, place.b)]
        if kind == "z":
            at = full.at[place.block(place.z - d * (k - 1), place.a, place.b)]
            source, target = (self.own if k == 1 else at), at
            to, base = place.at(place.z + d, place.core, place.a, place.b), 0
        elif kind == "a" or kind == "b":
            source, target = (column if k else self.own), column
            to = place.across_a() if kind == "a" else place.across_b()
            base = count * (1 if kind == "a" else 2)
        elif kind == "d":
            source = target = full.at[place.block(self.plane(slot), 1 - place.a, place.b)]
            to, base = place.across_b(), 3 * count
        else:
            cells = place.side * place.side
            source = target = full.at[pl.ds(place.run(self.plane(slot), place.core), cells)]
            to, base = place.other_core(), 4 * count
        i = base + self.slots.index(slot)
        return pltpu.make_async_remote_copy(
            src_ref=source, dst_ref=target, send_sem=self.send.at[i], recv_sem=self.recv.at[i],
            device_id=to, device_id_type=MESH,
        )

    def keep(self):
        place = self.place
        return pltpu.make_async_copy(
            self.own, self.full.at[place.block(place.z, place.a, place.b)], self.send.at[5 * len(self.slots)]
        )

    def start(self):
        self.keep().start()
        for d in (1, -1):
            pl.when(self.onward(d))(lambda d=d: self.copy("z", (d, 1)).start())
        self.copy("a", (0, 0)).start()
        self.copy("b", (0, 0)).start()

    def arrive_z(self, slot):
        d, k = slot

        def action():
            self.copy("z", slot).wait_recv()
            if k + 1 < self.planes:
                pl.when(self.onward(d))(lambda: self.copy("z", (d, k + 1)).start())
            self.copy("a", slot).start()
            self.copy("b", slot).start()

        self.when(slot, action)

    def arrive_a(self, slot):
        def action():
            self.copy("a", slot).wait_recv()
            self.copy("d", slot).start()

        self.when(slot, action)

    def arrive_b(self, slot):
        def action():
            self.copy("b", slot).wait_recv()
            self.copy("d", slot).wait_recv()
            if slot[1] == 0:
                self.keep().wait()
            self.copy("c", slot).start()

        self.when(slot, action)

    def finish(self):
        for slot in self.slots:
            self.when(slot, lambda slot=slot: self.copy("c", slot).wait_recv())
        for slot in self.slots:
            d, k = slot
            if k:
                sent = self.onward(d) if k == 1 else self.onward(d) & self.here((d, k - 1))
                pl.when(sent)(lambda slot=slot: self.copy("z", slot).wait_send())

            def action(slot=slot):
                for kind in "abdc":
                    self.copy(kind, slot).wait_send()

            self.when(slot, action)

    def tick(self, t):
        if t == 0:
            self.start()
        elif t == self.planes + 3:
            self.finish()
        else:
            for ahead, act in ((0, self.arrive_z), (1, self.arrive_a), (2, self.arrive_b)):
                for slot in self.slots:
                    if slot[1] == t - ahead and (ahead or slot[1]):
                        act(slot)


def forward_kernel(
    planes, side, rows,
    first_ref, second_ref, hid_ref, emb_ref, seg_ref,
    packed_ref, mixed_ref, mid_ref, norm_ref, total_ref, vec_ref, w_qkv, w_out, *rest,
):
    if planes:
        full2, first, tail, bias_cols, mask_q, mask_k, load, send1, recv1, send2, recv2 = rest
    else:
        first, tail, bias_cols, mask_q, mask_k, load = rest
        full2 = second_ref
    step = pl.program_id(0)
    attending = step < 8 * rows
    row, phase = step // 8, step % 8

    if planes:
        place = Place(planes, side)
        gather2 = Gather(place, second_ref, full2, send2, recv2)

        @pl.when(step == 0)
        def _():
            place.greet()
            gather1 = Gather(place, first_ref, first, send1, recv1)
            for t in range(planes + 4):
                if t == planes + 2:
                    gather2.tick(0)
                gather1.tick(t)

        for at, t in zip((1, 3, 5, 8, 9, 11, 15), range(1, planes + 4)):
            @pl.when(step == at)
            def _(t=t):
                gather2.tick(t)
    else:
        @pl.when(step == 0)
        def _():
            c = pltpu.make_async_copy(first_ref, first, load.at[0])
            c.start()
            c.wait()

    @pl.when(step == 0)
    def _():
        join_rows(first, 0, QROWS, w_qkv, BLOCKS // 2)
        vec_ref[0] = sum_rows(first, QROWS)
        bias_cols[0] = column(vec_ref[0, 2:3, :])
        bias_cols[1] = jnp.zeros((D, 1), F32)
        bias_cols[2] = column(vec_ref[0, 3:4, :])

    @pl.when(attending & (phase < 2))
    def _():
        at = pl.ds(pl.multiple_of(phase * TOKB, TOKB), TOKB)
        entered = hid_ref[...].astype(F32) + emb_ref[...].astype(F32)
        scaled, _ = normalise(entered)
        normed = (scaled * vec_ref[0, 0:1, :] + vec_ref[0, 1:2, :]).astype(BF16)
        for part in range(3):
            rows_at = slice(part * D, (part + 1) * D)
            packed_ref[rows_at, at] = (mm(w_qkv[rows_at, :], normed, 1, 1) + bias_cols[part]).astype(BF16)

    @pl.when(attending & (phase == 0))
    def _():
        query_side, key_side = mask_rows(seg_ref[0])
        mask_q[...] = query_side
        mask_k[...] = key_side

    @pl.when(attending & (phase >= 2))
    def _():
        base = pl.multiple_of((phase - 2) * 128, 128)
        ones_rows = jnp.where(lax.broadcasted_iota(jnp.int32, (HEAD, ROW), 0) == 0, 1.0, 0.0).astype(BF16)
        sides = []
        for h in range(2):
            at = base + HEAD * h
            high, low = scaled_query(packed_ref[pl.ds(at, HEAD), :])
            keys = packed_ref[pl.ds(D + at, HEAD), :]
            sides.append((
                jnp.concatenate([high, low, mask_q[...]], axis=0),
                jnp.concatenate([keys, keys, mask_k[...]], axis=0),
                jnp.concatenate([packed_ref[pl.ds(2 * D + at, HEAD), :], ones_rows], axis=0),
            ))
        all_scores = [mm(sides[h][1], sides[h][0], 0, 0) for h in range(2)]
        mixed = []
        for h in range(2):
            scores = all_scores[h]
            top = jnp.max(scores, axis=0, keepdims=True)
            weights = jnp.exp2(scores - top).astype(BF16)
            summed = mm(sides[h][2], weights, 1, 0)
            total = summed[HEAD : HEAD + 1, :]
            mixed.append(summed[:HEAD, :] / total)
            total_ref[0, h : h + 1, :] = top + jnp.log2(total)
        tokens = pl.ds(pl.multiple_of(row * ROW, ROW), ROW)
        mixed_ref[tokens, pl.ds(base, 128)] = jnp.concatenate(mixed, axis=0).T

    @pl.when(step == 8 * rows)
    def _():
        c = pltpu.make_async_copy(full2.at[:, pl.ds(2 * UROWS, 32)], tail, load.at[0])
        c.start()
        c.wait()
        join_rows(tail, 0, OROWS, w_out, BLOCKS // 2)
        vec_ref[1] = sum_rows(tail, OROWS)

    @pl.when(step >= 8 * rows)
    def _():
        tokens = pl.ds(pl.multiple_of((step - 8 * rows) * TOKB, TOKB), TOKB)
        entered = hid_ref[...].astype(F32) + emb_ref[...].astype(F32)
        middle = entered + mm(mixed_ref[tokens, :].astype(BF16), w_out[...], 1, 1) + vec_ref[0, 4:5, :]
        scaled, _ = normalise(middle)
        mid_ref[...] = middle
        norm_ref[...] = (scaled * vec_ref[0, 5:6, :] + vec_ref[0, 6:7, :]).astype(BF16)


def forward(planes, side, first, second, hidden, embed, segment):
    n = hidden.shape[0]
    rows = n // ROW
    one = pl.Buffered(1)
    hbm = pl.BlockSpec(memory_space=pl.ANY)

    def row(s):
        return jnp.minimum(s // 8, rows - 1)

    def entry(s):
        return (jnp.where(s < 8 * rows, 2 * (s // 8) + jnp.minimum(s % 8, 1), s - 8 * rows), 0)

    def leave(s):
        return (jnp.maximum(s - 8 * rows, 0), 0)

    def pair(s):
        return jnp.where(s < 8 * rows, jnp.maximum(s % 8 - 2, 0), 5)

    entering = pl.BlockSpec((TOKB, D), entry)
    leaving = pl.BlockSpec((TOKB, D), leave)
    out_specs = [
        pl.BlockSpec((3 * D, ROW), lambda s: (0, row(s))),
        pl.BlockSpec((n, D), lambda s: (0, 0), pipeline_mode=one),
        leaving,
        leaving,
        pl.BlockSpec((1, 8, ROW), lambda s: (pair(s), 0, row(s))),
        pl.BlockSpec((2, 8, D), lambda s: (0, 0, 0)),
        pl.BlockSpec((3 * D, D), lambda s: (0, 0), pipeline_mode=one),
        pl.BlockSpec((D, D), lambda s: (0, 0), pipeline_mode=one),
    ]
    out_shape = [
        jax.ShapeDtypeStruct((3 * D, n), BF16),
        jax.ShapeDtypeStruct((n, D), F32),
        jax.ShapeDtypeStruct((n, D), F32),
        jax.ShapeDtypeStruct((n, D), BF16),
        jax.ShapeDtypeStruct((HEADS // 2, 8, n), F32),
        jax.ShapeDtypeStruct((2, 8, D), F32),
        jax.ShapeDtypeStruct((3 * D, D), BF16),
        jax.ShapeDtypeStruct((D, D), BF16),
    ]
    scratch = [
        pltpu.VMEM((BLOCKS, FIRST, D), BF16),
        pltpu.VMEM((BLOCKS, 32, D), BF16),
        pltpu.VMEM((3, D, 1), F32),
        pltpu.VMEM((32, ROW), BF16),
        pltpu.VMEM((32, ROW), BF16),
        pltpu.SemaphoreType.DMA((1,)),
    ]
    params = dict(vmem_limit_bytes=62 * MIB)
    if planes:
        out_specs.append(hbm)
        out_shape.append(jax.ShapeDtypeStruct((BLOCKS, SECOND, D), BF16))
        scratch += [Gather.semaphores(planes)] * 4
        params.update(collective_id=1, has_side_effects=True)
    outs = pl.pallas_call(
        partial(forward_kernel, planes, side, rows),
        grid=(10 * rows,),
        in_specs=[
            hbm,
            hbm,
            entering,
            entering,
            pl.BlockSpec((1, 1, ROW), lambda s: (row(s), 0, 0)),
        ],
        out_specs=out_specs,
        out_shape=out_shape,
        scratch_shapes=scratch,
        compiler_params=pltpu.CompilerParams(**params),
        name="attention_forward",
    )(first, second, hidden, embed, segment.reshape(rows, 1, ROW))
    return outs if planes else list(outs) + [second]


def feed_kernel(
    up_ref, down_ref, vec_ref, norm_ref, mid_ref, cot_ref, seg_ref,
    out_ref, gmid_ref, gup_ref, gdown_ref, gvec_ref,
    w_down, result, back, live,
):
    j, i = pl.program_id(0), pl.program_id(1)
    at = pl.ds(pl.multiple_of(i * TOKB, TOKB), TOKB)

    @pl.when(i == 0)
    def _():
        for chunk in range(CHUNKS):
            @pl.when(j == chunk)
            def _():
                join_rows(down_ref, chunk * OROWS, OROWS, w_down, BLOCKS // 2)

    @pl.when((j == 0) & (i == 0))
    def _():
        gvec_ref[...] = jnp.zeros_like(gvec_ref)

    @pl.when(j == 0)
    def _():
        keep = column(jnp.where(seg_ref[0] >= 0, 1.0, 0.0))
        grad_result = cot_ref[...].astype(F32) * keep
        live[at, :] = grad_result.astype(BF16)
        gvec_ref[4:5, :] += jnp.sum(grad_result, axis=0, keepdims=True)

    normed = norm_ref[...]
    grad_result = live[at, :]
    up = up_ref[...].reshape(D, D)
    down = w_down[...]
    x = mm(normed, up, 1, 1) + vec_ref[1, pl.ds(j, 1), :]
    grad_act = mm(grad_result, down, 1, 0)
    c0 = math.sqrt(2.0 / math.pi)
    c1 = 0.044715
    square = x * x
    th = jnp.tanh(x * (c0 + (c0 * c1) * square))
    half = 0.5 + 0.5 * th
    activated = (x * half).astype(BF16)
    slope = half + (0.5 * x) * ((1.0 - th * th) * (c0 + (3 * c0 * c1) * square))
    grad_pre32 = grad_act * slope
    grad_pre = grad_pre32.astype(BF16)
    gvec_ref[pl.ds(j, 1), :] += jnp.sum(grad_pre.astype(F32), axis=0, keepdims=True)
    part = mm(activated, down, 1, 1)
    part_back = mm(grad_pre, up, 1, 0)
    part_down = mm(grad_result, activated, 0, 0)
    part_up = mm(grad_pre, normed, 0, 0)

    @pl.when(i == 0)
    def _():
        gdown_ref[0] = part_down
        gup_ref[...] = part_up

    @pl.when(i > 0)
    def _():
        gdown_ref[0] += part_down
        gup_ref[...] += part_up

    @pl.when(j == 0)
    def _():
        result[at, :] = part
        back[at, :] = part_back

    @pl.when((j > 0) & (j < CHUNKS - 1))
    def _():
        result[at, :] += part
        back[at, :] += part_back

    @pl.when(j == CHUNKS - 1)
    def _():
        middle = mid_ref[...]
        out_ref[...] = (middle + (result[at, :] + part + vec_ref[0, 7:8, :])).astype(BF16)
        grad = back[at, :] + part_back
        scaled, inverse = normalise(middle)
        gvec_ref[5:6, :] += jnp.sum(grad * scaled, axis=0, keepdims=True)
        gvec_ref[6:7, :] += jnp.sum(grad, axis=0, keepdims=True)
        gmid_ref[...] = grad_result.astype(F32) + norm_back(grad, scaled, inverse, vec_ref[0, 5:6, :])


def feed(second, vec, normed, middle, cotangent, segment):
    n = normed.shape[0]
    blocks = n // TOKB
    one = pl.Buffered(1)
    last = CHUNKS - 1
    tokens = pl.BlockSpec((TOKB, D), lambda j, i: (i, 0))
    at_first = pl.BlockSpec((TOKB, D), lambda j, i: (jnp.where(j == 0, i, blocks - 1), 0))
    at_last = pl.BlockSpec((TOKB, D), lambda j, i: (jnp.where(j == last, i, 0), 0))
    return pl.pallas_call(
        feed_kernel,
        grid=(CHUNKS, blocks),
        in_specs=[
            pl.BlockSpec((BLOCKS // CHUNKS, UROWS, D), lambda j, i: (j, 0, 0)),
            pl.BlockSpec((BLOCKS, UROWS, D), lambda j, i: (0, 1, 0), pipeline_mode=one),
            pl.BlockSpec((2, 8, D), lambda j, i: (0, 0, 0)),
            tokens,
            at_last,
            at_first,
            pl.BlockSpec((1, 1, TOKB), lambda j, i: (i, 0, 0)),
        ],
        out_specs=[
            at_last,
            at_last,
            pl.BlockSpec((D, D), lambda j, i: (j, 0)),
            pl.BlockSpec((1, D, D), lambda j, i: (j, 0, 0)),
            pl.BlockSpec((8, D), lambda j, i: (0, 0)),
        ],
        out_shape=[
            jax.ShapeDtypeStruct((n, D), BF16),
            jax.ShapeDtypeStruct((n, D), F32),
            jax.ShapeDtypeStruct((FF, D), F32),
            jax.ShapeDtypeStruct((CHUNKS, D, D), F32),
            jax.ShapeDtypeStruct((8, D), F32),
        ],
        scratch_shapes=[
            pltpu.VMEM((D, D), BF16),
            pltpu.VMEM((n, D), F32),
            pltpu.VMEM((n, D), F32),
            pltpu.VMEM((n, D), BF16),
        ],
        compiler_params=pltpu.CompilerParams(vmem_limit_bytes=60 * MIB),
        name="feed_forward",
    )(second, second, vec, normed, middle, cotangent, segment.reshape(blocks, 1, TOKB))


def three_parts(row):
    r = lax.broadcasted_iota(jnp.int32, (16, row.shape[1]), 0)
    a = row.astype(BF16).astype(F32)
    b = (row - a).astype(BF16).astype(F32)
    c = row - a - b
    return jnp.where(r == 0, -a, jnp.where(r == 1, -b, jnp.where(r == 2, -c, 0.0))).astype(BF16)


def backward_kernel(
    w_qkv, w_out, vec_ref, hid_ref, emb_ref, seg_ref, packed_q, packed_k, packed_v,
    mixed_ref, total_ref, gmid_ref,
    ghid_ref, gout_ref, gqkv_ref, gvec_ref,
    mask_q, mask_k, grad_mixed, delta, grad_packed,
):
    row, step = pl.program_id(0), pl.program_id(1)

    @pl.when((row == 0) & (step == 0))
    def _():
        gvec_ref[...] = jnp.zeros_like(gvec_ref)
        gout_ref[...] = jnp.zeros_like(gout_ref)
        gqkv_ref[...] = jnp.zeros_like(gqkv_ref)

    @pl.when(step == 0)
    def _():
        query_side, key_side = mask_rows(seg_ref[0])
        mask_q[...] = query_side
        mask_k[...] = key_side

    @pl.when(step < 2)
    def _():
        at = pl.ds(pl.multiple_of(step * TOKB, TOKB), TOKB)
        mixed = mixed_ref[...]
        branch = gmid_ref[...].astype(BF16)
        gvec_ref[4:5, :] += jnp.sum(branch.astype(F32), axis=0, keepdims=True)
        gout_ref[...] += mm(branch, mixed.astype(BF16), 0, 0)
        grad = mm(branch, w_out[...], 1, 0).astype(BF16).astype(F32)
        grad_mixed[:, at] = grad.T.astype(BF16)
        inner = (grad * mixed).T
        delta[:, at] = jnp.concatenate(
            [jnp.sum(inner[HEAD * h : HEAD * (h + 1)], axis=0, keepdims=True) for h in range(HEADS)]
            + [jnp.zeros((16 - HEADS, TOKB), F32)],
            axis=0,
        )

    @pl.when((step >= 2) & (step < 8))
    def _():
        pair = step - 2
        r = lax.broadcasted_iota(jnp.int32, (16, ROW), 0)
        ones_rows = jnp.where(r < 3, 1.0, 0.0).astype(BF16)
        base = pl.multiple_of(pair * 128, 128)
        for h in range(2):
            rows = slice(HEAD * h, HEAD * (h + 1))
            queries, keys, values = packed_q[rows, :], packed_k[rows, :], packed_v[rows, :]
            grad = grad_mixed[pl.ds(base + HEAD * h, HEAD), :]
            high, low = scaled_query(queries)
            wide_q = jnp.concatenate([high, low, mask_q[...], three_parts(total_ref[0, h : h + 1, :])], axis=0)
            wide_k = jnp.concatenate([keys, keys, mask_k[...], ones_rows], axis=0)
            wide_g = jnp.concatenate([grad, three_parts(delta[pl.ds(2 * pair + h, 1), :])], axis=0)
            wide_v = jnp.concatenate([values, ones_rows], axis=0)
            grad_v = jnp.zeros((HEAD, ROW), F32)
            grad_k = jnp.zeros((HEAD, ROW), F32)
            grad_q = []
            for half in range(2):
                at = slice(half * (ROW // 2), (half + 1) * (ROW // 2))
                probs = jnp.exp2(mm(wide_q[:, at], wide_k, 0, 0))
                grad_probs = mm(wide_g[:, at], wide_v, 0, 0)
                grad_scores = (probs * grad_probs).astype(BF16)
                grad_v = grad_v + mm(grad[:, at], probs.astype(BF16), 1, 0)
                grad_k = grad_k + mm(queries[:, at], grad_scores, 1, 0)
                grad_q.append(mm(keys, grad_scores, 1, 1))
            grad_packed[pl.ds(base + HEAD * h, HEAD), :] = (jnp.concatenate(grad_q, axis=1) * 0.125).astype(BF16)
            grad_packed[pl.ds(D + base + HEAD * h, HEAD), :] = (grad_k * 0.125).astype(BF16)
            grad_packed[pl.ds(2 * D + base + HEAD * h, HEAD), :] = grad_v.astype(BF16)

    @pl.when(step >= 8)
    def _():
        at = pl.ds(pl.multiple_of((step - 8) * TOKB, TOKB), TOKB)
        entered = hid_ref[...].astype(F32) + emb_ref[...].astype(F32)
        scaled, inverse = normalise(entered)
        normed = (scaled * vec_ref[0, 0:1, :] + vec_ref[0, 1:2, :]).astype(BF16)
        for part in range(3):
            rows = slice(part * D, (part + 1) * D)
            gqkv_ref[rows, :] += mm(grad_packed[rows, at], normed, 1, 0)
        grad = mm(grad_packed[:, at], w_qkv[...], 0, 0)
        ones = jnp.ones((16, TOKB), BF16)
        gvec_ref[0:1, :] += jnp.sum(grad * scaled, axis=0, keepdims=True)
        gvec_ref[1:2, :] += jnp.sum(grad, axis=0, keepdims=True)
        gvec_ref[2:3, :] += mm(ones, grad_packed[0:D, at], 1, 1)[0:1, :]
        gvec_ref[3:4, :] += mm(ones, grad_packed[2 * D : 3 * D, at], 1, 1)[0:1, :]
        ghid_ref[...] = (gmid_ref[...] + norm_back(grad, scaled, inverse, vec_ref[0, 0:1, :])).astype(BF16)


def backward(w_qkv, w_out, vec, hidden, embed, segment, packed, mixed, totals, gmid):
    n = hidden.shape[0]
    rows = n // ROW
    one = pl.Buffered(1)

    def early(r, s):
        return (2 * r + jnp.clip(s, 0, 1), 0)

    def late(r, s):
        return (2 * r + jnp.clip(s - 8, 0, 1), 0)

    def both(r, s):
        return (2 * r + jnp.where(s < 8, jnp.clip(s, 0, 1), s - 8), 0)

    def pair(s):
        return jnp.clip(s - 2, 0, 5)

    return pl.pallas_call(
        backward_kernel,
        grid=(rows, 10),
        in_specs=[
            pl.BlockSpec((3 * D, D), lambda r, s: (0, 0), pipeline_mode=one),
            pl.BlockSpec((D, D), lambda r, s: (0, 0), pipeline_mode=one),
            pl.BlockSpec((2, 8, D), lambda r, s: (0, 0, 0)),
            pl.BlockSpec((TOKB, D), late),
            pl.BlockSpec((TOKB, D), late),
            pl.BlockSpec((1, 1, ROW), lambda r, s: (r, 0, 0)),
            pl.BlockSpec((128, ROW), lambda r, s: (pair(s), r)),
            pl.BlockSpec((128, ROW), lambda r, s: (6 + pair(s), r)),
            pl.BlockSpec((128, ROW), lambda r, s: (12 + pair(s), r)),
            pl.BlockSpec((TOKB, D), early),
            pl.BlockSpec((1, 8, ROW), lambda r, s: (pair(s), 0, r)),
            pl.BlockSpec((TOKB, D), both),
        ],
        out_specs=[
            pl.BlockSpec((TOKB, D), late),
            pl.BlockSpec((D, D), lambda r, s: (0, 0)),
            pl.BlockSpec((3 * D, D), lambda r, s: (0, 0), pipeline_mode=one),
            pl.BlockSpec((8, D), lambda r, s: (0, 0)),
        ],
        out_shape=[
            jax.ShapeDtypeStruct((n, D), BF16),
            jax.ShapeDtypeStruct((D, D), F32),
            jax.ShapeDtypeStruct((3 * D, D), F32),
            jax.ShapeDtypeStruct((8, D), F32),
        ],
        scratch_shapes=[
            pltpu.VMEM((32, ROW), BF16),
            pltpu.VMEM((32, ROW), BF16),
            pltpu.VMEM((D, ROW), BF16),
            pltpu.VMEM((16, ROW), F32),
            pltpu.VMEM((3 * D, ROW), BF16),
        ],
        compiler_params=pltpu.CompilerParams(vmem_limit_bytes=62 * MIB),
        name="attention_backward",
    )(w_qkv, w_out, vec, hidden, embed, segment.reshape(rows, 1, ROW), packed, packed, packed, mixed, totals, gmid)


def scatter_kernel(
    planes, side, up, down, out, qkv, vec,
    mine,
    theirs_up, theirs_down, theirs_out, theirs_qkv, theirs_vec,
    ours_up, ours_down, ours_out, ours_qkv, ours_vec,
    share, got_b, got_a, got_z,
    send1, recv1, load, send, recv, vec_sems,
):
    place = Place(planes, side)
    place.greet()
    cells = side * side

    def pieces(z, core):
        first = place.run(z, core)
        return (
            up.at[pl.ds(first * UROWS, cells * UROWS)],
            down.at[:, pl.ds(first * OROWS, cells * OROWS)],
            out.at[pl.ds(first * OROWS, cells * OROWS)],
            qkv.at[pl.ds(first * QROWS, cells * QROWS)],
        )

    theirs = (theirs_up, theirs_down, theirs_out, theirs_qkv)
    ours = (ours_up, ours_down, ours_out, ours_qkv)
    order = list(range(1, planes)) + [0]
    vec_copy = pltpu.make_async_remote_copy(
        src_ref=vec, dst_ref=theirs_vec, send_sem=vec_sems.at[0], recv_sem=vec_sems.at[1],
        device_id=place.other_core(), device_id_type=MESH,
    )
    vec_copy.start()
    vec_load = pltpu.make_async_copy(vec, ours_vec, vec_sems.at[2])
    vec_load.start()
    outgoing, started = {}, []
    for k in order:
        for i, piece in enumerate(pieces(place.plane(k), 1 - place.core)):
            c = pltpu.make_async_remote_copy(
                src_ref=piece, dst_ref=theirs[i].at[k], send_sem=send1.at[k, i], recv_sem=recv1.at[k, i],
                device_id=place.other_core(), device_id_type=MESH,
            )
            c.start()
            outgoing[k, i] = c
            started.append(c)

    def loads(t):
        k = order[t]
        return [
            pltpu.make_async_copy(piece, ours[i].at[t % 2], load.at[t % 2, i])
            for i, piece in enumerate(pieces(place.plane(k), place.core))
        ]

    def copy(slot, source, target, to):
        c = pltpu.make_async_remote_copy(
            src_ref=source, dst_ref=target, send_sem=send.at[slot], recv_sem=recv.at[slot],
            device_id=to, device_id_type=MESH,
        )
        c.start()
        started.append(c)
        return c

    state = {}
    for c in loads(0):
        c.start()
    vec_copy.wait()
    vec_load.wait()

    def arrive_core(t):
        k = order[t]
        if t + 1 < planes:
            for c in loads(t + 1):
                c.start()
        for i, c in enumerate(loads(t)):
            c.wait()
            outgoing[k, i].wait_recv()
        s = t % 2
        vec_sum = ours_vec[...] + theirs_vec[...]

        def one(cell, _):
            u = pl.ds(pl.multiple_of(cell * UROWS, UROWS), UROWS)
            o = pl.ds(pl.multiple_of(cell * OROWS, OROWS), OROWS)
            q = pl.ds(pl.multiple_of(cell * QROWS, QROWS), QROWS)
            rows = [ours_up[s, u] + theirs_up[k, u]]
            rows += [ours_down[s, c, o] + theirs_down[k, c, o] for c in range(CHUNKS)]
            rows += [ours_out[s, o] + theirs_out[k, o], ours_qkv[s, q] + theirs_qkv[k, q], vec_sum]
            y, x = cell // side, cell % side
            a = x + place.core * (y - x)
            b = y + place.core * (x - y)
            share[k, b, a] = jnp.concatenate(rows, axis=0).astype(BF16)
            return 0

        lax.fori_loop(0, cells, one, 0)
        state["b", k] = copy(k, share.at[k, 1 - place.b], got_b.at[k], place.across_b())

    def arrive_b(t):
        k = order[t]
        state["b", k].wait_recv()
        for a in range(side):
            share[k, place.b, a] = (share[k, place.b, a].astype(F32) + got_b[k, a].astype(F32)).astype(BF16)
        state["a", k] = copy(planes + k, share.at[k, place.b, 1 - place.a], got_a.at[k], place.across_a())

    def arrive_a(t):
        k = order[t]
        state["a", k].wait_recv()
        total = share[k, place.b, place.a].astype(F32) + got_a[k].astype(F32)
        if k == 0:
            mine[...] = total
        else:
            share[k, place.b, place.a] = total.astype(BF16)
            state["z", k] = copy(2 * planes + k, share.at[k, place.b, place.a], got_z.at[k], place.along_z(k))

    for t in range(planes + 2):
        if t < planes:
            arrive_core(t)
        if 0 <= t - 1 < planes:
            arrive_b(t - 1)
        if 0 <= t - 2 < planes:
            arrive_a(t - 2)
    for k in range(1, planes):
        state["z", k].wait_recv()
        mine[...] += got_z[k].astype(F32)
    for c in started:
        c.wait_send()


def scatter(planes, side, up, down, out, qkv, vec):
    cells = side * side
    hbm = pl.BlockSpec(memory_space=pl.ANY)
    wide = pltpu.VMEM

    def buffers(count):
        return [
            wide((count, cells * UROWS, D), F32),
            wide((count, CHUNKS, cells * OROWS, D), F32),
            wide((count, cells * OROWS, D), F32),
            wide((count, cells * QROWS, D), F32),
        ]

    return pl.pallas_call(
        partial(scatter_kernel, planes, side),
        in_specs=[hbm] * 5,
        out_specs=pl.BlockSpec(memory_space=pltpu.VMEM),
        out_shape=jax.ShapeDtypeStruct((SHARE, D), F32),
        scratch_shapes=buffers(planes)
        + [wide((16, D), F32)]
        + buffers(2)
        + [wide((16, D), F32)]
        + [
            wide((planes, side, side, SHARE, D), BF16),
            wide((planes, side, SHARE, D), BF16),
            wide((planes, SHARE, D), BF16),
            wide((planes, SHARE, D), BF16),
            pltpu.SemaphoreType.DMA((planes, 4)),
            pltpu.SemaphoreType.DMA((planes, 4)),
            pltpu.SemaphoreType.DMA((2, 4)),
            pltpu.SemaphoreType.DMA((3 * planes,)),
            pltpu.SemaphoreType.DMA((3 * planes,)),
            pltpu.SemaphoreType.DMA((3,)),
        ],
        compiler_params=pltpu.CompilerParams(
            collective_id=2, has_side_effects=True, vmem_limit_bytes=60 * MIB
        ),
        name="scatter_gradients",
    )(up, down, out, qkv, vec)


def placed(vector, index, devices):
    here = (jnp.arange(devices) == index)[:, None]
    return jnp.where(here, vector[None, :], jnp.zeros((), vector.dtype)).reshape(-1)


def body(
    planes, side, devices,
    hidden, time_embed, segment_ids,
    ln1_gain, ln1_bias, w_qkv, b_query, b_value, w_out, b_out, ln2_gain, ln2_bias, w_up, b_up, w_down, b_down,
    cotangent,
):
    index = lax.axis_index("dp") * lax.axis_size("fsdp") + lax.axis_index("fsdp")
    axes = ("dp", "fsdp")
    small = (ln1_gain, ln1_bias, b_query, b_value, b_out, ln2_gain, ln2_bias, b_down)
    if planes:
        vec1 = jnp.stack([placed(v, index, devices) for v in small])
        vec2 = placed(b_up, index, devices).reshape(CHUNKS, D)
        vec2 = jnp.concatenate([vec2, jnp.zeros((8 - CHUNKS, D), BF16)], axis=0)
        down_rows = w_down.T.reshape(OROWS, CHUNKS, D).transpose(1, 0, 2).reshape(UROWS, D)
        own1 = jnp.concatenate([w_qkv.T, vec1], axis=0)
        own2 = jnp.concatenate([w_up.T, down_rows, w_out.T, vec2], axis=0)
        first, second = own1, own2
    else:
        def whole(a, dim):
            return lax.all_gather(a, axes, axis=dim, tiled=True)

        def only_first(rows):
            return jnp.concatenate([rows[None], jnp.zeros((BLOCKS - 1,) + rows.shape, BF16)], axis=0)

        vec1 = jnp.stack([whole(v, 0) for v in small])
        vec2 = jnp.concatenate([whole(b_up, 0).reshape(CHUNKS, D), jnp.zeros((8 - CHUNKS, D), BF16)], axis=0)
        down_rows = whole(w_down, 1).T.reshape(BLOCKS, OROWS, CHUNKS, D).transpose(0, 2, 1, 3)
        first = jnp.concatenate([whole(w_qkv, 1).T.reshape(BLOCKS, QROWS, D), only_first(vec1)], axis=1)
        second = jnp.concatenate(
            [
                whole(w_up, 1).T.reshape(BLOCKS, UROWS, D),
                down_rows.reshape(BLOCKS, UROWS, D),
                whole(w_out, 1).T.reshape(BLOCKS, OROWS, D),
                only_first(vec2),
            ],
            axis=1,
        )
    packed, mixed, middle, normed, totals, vec, full_qkv, full_out, second = forward(
        planes, side, first, second, hidden, time_embed, segment_ids
    )
    output, gmid, gup, gdown, gvec_feed = feed(second, vec, normed, middle, cotangent, segment_ids)
    ghid, gout, gqkv, gvec = backward(
        full_qkv, full_out, vec, hidden, time_embed, segment_ids, packed, mixed, totals, gmid
    )
    if planes:
        mine = scatter(planes, side, gup, gdown, gout, gqkv, jnp.concatenate([gvec_feed, gvec], axis=0))
        cuts = (UROWS, 2 * UROWS, 2 * UROWS + OROWS, 2 * UROWS + OROWS + QROWS)
        part_up = mine[: cuts[0]]
        part_down = mine[cuts[0] : cuts[1]].reshape(CHUNKS, OROWS, D).transpose(1, 0, 2).reshape(OROWS, FF)
        part_out = mine[cuts[1] : cuts[2]]
        part_qkv = mine[cuts[2] : cuts[3]]
        vectors = mine[cuts[3] :]
        short = lax.dynamic_slice(vectors, (0, index * OROWS), (16, OROWS))
        part_bup = lax.dynamic_slice(vectors[:CHUNKS].reshape(-1), (index * UROWS,), (UROWS,))
    else:
        def shared(a, dim):
            return lax.psum_scatter(a, axes, scatter_dimension=dim, tiled=True)

        part_up = shared(gup, 0)
        part_down = shared(gdown.transpose(1, 0, 2).reshape(D, FF), 0)
        part_out = shared(gout, 0)
        part_qkv = shared(gqkv, 0)
        short = shared(jnp.concatenate([gvec_feed, gvec], axis=0), 1)
        part_bup = shared(gvec_feed[:CHUNKS].reshape(-1), 0)
    return (
        output, ghid,
        short[8], short[9], part_qkv.T, short[10], short[11], part_out.T, short[12],
        short[5], short[6], part_up.T, part_bup, part_down.T, short[4],
    )


def solution(mesh):
    groups, cells = mesh.shape["dp"], mesh.shape["fsdp"]
    side = math.isqrt(cells)
    own_transfers = groups * cells == BLOCKS and side == 2 and cells == 4 and groups % 2 == 0
    split = ("dp", "fsdp")
    rows, flat, cols = P(split, None), P(split), P(None, split)
    return jax.shard_map(
        partial(body, groups // 2 if own_transfers else 0, side, groups * cells),
        mesh=mesh,
        in_specs=(
            rows, rows, flat, flat, flat, cols, flat, flat, cols, flat, flat, flat, cols, flat, cols, flat, rows,
        ),
        out_specs=(
            rows, rows, flat, flat, cols, flat, flat, cols, flat, flat, flat, cols, flat, cols, flat,
        ),
        check_vma=False,
    )
```

```python
from functools import partial
import math

import jax
import jax.numpy as jnp
from jax import lax
from jax.experimental import pallas as pl
from jax.experimental.pallas import tpu as pltpu
from jax.sharding import PartitionSpec as P

D = 768
HEADS = 12
HEAD = 64
FF = 3072
ROW = 1024
BLOCKS = 32
QROWS = 3 * D // BLOCKS
OROWS = D // BLOCKS
UROWS = FF // BLOCKS
CHUNKS = FF // D
FIRST = QROWS + 8
SECOND = 2 * UROWS + OROWS + 8
TOKB = 512
MIB = 2**20
MESH = pl.DeviceIdType.MESH
F32 = jnp.float32
BF16 = jnp.bfloat16
LOG2E = math.log2(math.e)
EPS = 1e-05
SCHED = (2, 5, 8, 10, 13, 15, 16)
BACK = (
    (1, 0, "arrive_core"), (2, 1, "arrive_core"), (3, 0, "arrive_b"), (4, 2, "arrive_core"), (5, 1, "arrive_b"),
    (5, 0, "arrive_a"), (6, 3, "arrive_core"), (7, 2, "arrive_b"), (8, 1, "arrive_a"), (9, 3, "arrive_b"),
    (9, 2, "arrive_a"), (11, 3, "arrive_a"),
)
ENTER = (
    (0, 0, "arrive_core"), (1, 1, "arrive_core"), (2, 0, "arrive_b"), (2, 2, "arrive_core"), (3, 3, "arrive_core"),
    (3, 1, "arrive_b"),
)
ENTER_LAST = (
    (0, "arrive_a"), (2, "arrive_b"), (1, "arrive_a"), (3, "arrive_b"), (2, "arrive_a"), (3, "arrive_a"),
)


def mm(a, b, ca, cb):
    return lax.dot_general(a, b, (((ca,), (cb,)), ((), ())), preferred_element_type=F32)


def normalise(values):
    centred = values - jnp.mean(values, axis=-1, keepdims=True)
    inverse = lax.rsqrt(jnp.mean(centred * centred, axis=-1, keepdims=True) + EPS)
    return centred * inverse, inverse


def norm_back(grad, scaled, inverse, gain):
    u = grad * gain
    return inverse * (
        u
        - jnp.mean(u, axis=-1, keepdims=True)
        - scaled * jnp.mean(u * scaled, axis=-1, keepdims=True)
    )


def column(row):
    return jnp.broadcast_to(row, (128, row.shape[1])).T[:, :1]


def join_rows(source, start, rows, target, pairs):
    low = start // 16 * 16
    high = -(-(start + rows) // 16) * 16

    def step(p, _):
        parts = [
            source[2 * p + i, low:high, :].astype(F32)[start - low : start - low + rows]
            for i in range(2)
        ]
        at = pl.multiple_of(2 * rows * p, 2 * rows)
        target[pl.ds(at, 2 * rows), :] = jnp.concatenate(parts, axis=0).astype(BF16)
        return 0

    lax.fori_loop(0, pairs, step, 0)


def sum_rows(source, start):
    low = start // 16 * 16

    def step(d, total):
        return total + source[d, low : low + 16, :].astype(F32)[start - low : start - low + 8]

    return lax.fori_loop(0, BLOCKS, step, jnp.zeros((8, D), F32))


def mask_rows(segment):
    r = lax.broadcasted_iota(jnp.int32, (32, ROW), 0)
    hit = r == segment + 1
    query_side = jnp.where(hit, 1.0, 0.0).astype(BF16)
    key_side = jnp.where(hit | (r >= 17), 0.0, -1e30).astype(BF16)
    return query_side, key_side


def scaled_query(queries):
    wide = queries.astype(F32) * (LOG2E / 8)
    high = wide.astype(BF16)
    low = (wide - high.astype(F32)).astype(BF16)
    return high, low


class Place:
    def __init__(self, planes, side):
        self.planes, self.side = planes, side
        group, cell = lax.axis_index("dp"), lax.axis_index("fsdp")
        self.z, self.core = group // 2, group % 2
        y, x = cell // side, cell % side
        self.step_a = 1 + self.core * (side - 1)
        self.step_b = side - self.core * (side - 1)
        self.a = x + self.core * (y - x)
        self.b = y + self.core * (x - y)

    def plane(self, k):
        return lax.rem(self.z + k + self.planes, self.planes)

    def at(self, z, core, a, b):
        return (z * 2 + core, a * self.step_a + b * self.step_b)

    def block(self, z, a, b):
        return (z * 2 + self.core) * (self.side * self.side) + a * self.step_a + b * self.step_b

    def run(self, z, core):
        return (z * 2 + core) * (self.side * self.side)

    def across_a(self):
        return self.at(self.z, self.core, 1 - self.a, self.b)

    def across_b(self):
        return self.at(self.z, self.core, self.a, 1 - self.b)

    def other_core(self):
        return (self.z * 2 + 1 - self.core, self.a * self.step_a + self.b * self.step_b)

    def along_z(self, k):
        return self.at(self.plane(k), self.core, self.a, self.b)

    def greet(self):
        barrier = pltpu.get_barrier_semaphore()
        peers = [self.along_z(k) for k in range(1, self.planes)]
        peers += [self.across_a(), self.across_b(), self.other_core()]
        for peer in peers:
            pl.semaphore_signal(barrier, inc=1, device_id=peer, device_id_type=MESH)
        pl.semaphore_wait(barrier, len(peers))


class Gather:
    def __init__(self, place, own, full, send, recv):
        self.place, self.own, self.full, self.send, self.recv = place, own, full, send, recv
        self.planes = place.planes
        self.slots = Gather.all_slots(place.planes)

    @staticmethod
    def all_slots(planes):
        return [(0, 0)] + [(d, k) for k in range(1, planes) for d in (1, -1)]

    @staticmethod
    def semaphores(planes):
        return pltpu.SemaphoreType.DMA((5 * len(Gather.all_slots(planes)) + 1,))

    def plane(self, slot):
        return self.place.z - slot[0] * slot[1]

    def onward(self, d):
        return self.place.z + 1 < self.planes if d == 1 else self.place.z >= 1

    def here(self, slot):
        return self.place.z >= slot[1] if slot[0] == 1 else self.place.z + slot[1] < self.planes

    def when(self, slot, action):
        if slot[1]:
            pl.when(self.here(slot))(action)
        else:
            action()

    def copy(self, kind, slot):
        place, full, count = self.place, self.full, len(self.slots)
        d, k = slot
        column = full.at[place.block(self.plane(slot), place.a, place.b)]
        if kind == "z":
            at = full.at[place.block(place.z - d * (k - 1), place.a, place.b)]
            source, target = (self.own if k == 1 else at), at
            to, base = place.at(place.z + d, place.core, place.a, place.b), 0
        elif kind == "a" or kind == "b":
            source, target = (column if k else self.own), column
            to = place.across_a() if kind == "a" else place.across_b()
            base = count * (1 if kind == "a" else 2)
        elif kind == "d":
            source = target = full.at[place.block(self.plane(slot), 1 - place.a, place.b)]
            to, base = place.across_b(), 3 * count
        else:
            cells = place.side * place.side
            source = target = full.at[pl.ds(place.run(self.plane(slot), place.core), cells)]
            to, base = place.other_core(), 4 * count
        i = base + self.slots.index(slot)
        return pltpu.make_async_remote_copy(
            src_ref=source, dst_ref=target, send_sem=self.send.at[i], recv_sem=self.recv.at[i],
            device_id=to, device_id_type=MESH,
        )

    def keep(self):
        place = self.place
        return pltpu.make_async_copy(
            self.own, self.full.at[place.block(place.z, place.a, place.b)], self.send.at[5 * len(self.slots)]
        )

    def start(self):
        self.keep().start()
        for d in (1, -1):
            pl.when(self.onward(d))(lambda d=d: self.copy("z", (d, 1)).start())
        self.copy("a", (0, 0)).start()
        self.copy("b", (0, 0)).start()

    def arrive_z(self, slot):
        d, k = slot

        def action():
            self.copy("z", slot).wait_recv()
            if k + 1 < self.planes:
                pl.when(self.onward(d))(lambda: self.copy("z", (d, k + 1)).start())
            self.copy("a", slot).start()
            self.copy("b", slot).start()

        self.when(slot, action)

    def arrive_a(self, slot):
        def action():
            self.copy("a", slot).wait_recv()
            self.copy("d", slot).start()

        self.when(slot, action)

    def arrive_b(self, slot):
        def action():
            self.copy("b", slot).wait_recv()
            self.copy("d", slot).wait_recv()
            if slot[1] == 0:
                self.keep().wait()
            self.copy("c", slot).start()

        self.when(slot, action)

    def finish(self):
        for slot in self.slots:
            self.when(slot, lambda slot=slot: self.copy("c", slot).wait_recv())
        for slot in self.slots:
            d, k = slot
            if k:
                sent = self.onward(d) if k == 1 else self.onward(d) & self.here((d, k - 1))
                pl.when(sent)(lambda slot=slot: self.copy("z", slot).wait_send())

            def action(slot=slot):
                for kind in "abdc":
                    self.copy(kind, slot).wait_send()

            self.when(slot, action)

    def tick(self, t):
        if t == 0:
            self.start()
        elif t == self.planes + 3:
            self.finish()
        else:
            for ahead, act in ((0, self.arrive_z), (1, self.arrive_a), (2, self.arrive_b)):
                for slot in self.slots:
                    if slot[1] == t - ahead and (ahead or slot[1]):
                        act(slot)


class Scatter:
    def __init__(self, place, sources, land, ours, got_b, got_a, got_z, mine, load, send, recv):
        self.place, self.sources, self.land, self.ours = place, sources, land, ours
        self.got_b, self.got_a, self.got_z, self.mine = got_b, got_a, got_z, mine
        self.load, self.send, self.recv = load, send, recv
        self.planes, self.side = place.planes, place.side
        self.cells = place.side * place.side
        self.parts = len(sources)
        self.order = list(range(1, self.planes)) + [0]
        self.offsets = [sum(s.shape[1] for s in sources[:i]) for i in range(self.parts + 1)]

    @staticmethod
    def scratch(planes, side, parts, rows):
        cells = side * side
        count = planes * (parts + 4)
        return [
            pltpu.VMEM((planes, cells, rows, D), BF16),
            pltpu.VMEM((2, cells, rows, D), BF16),
            pltpu.VMEM((planes, side, rows, D), BF16),
            pltpu.VMEM((planes, rows, D), BF16),
            pltpu.VMEM((planes, rows, D), BF16),
            pltpu.SemaphoreType.DMA((2, parts)),
            pltpu.SemaphoreType.DMA((count,)),
            pltpu.SemaphoreType.DMA((count,)),
        ]

    def remote(self, slot, source, target, to):
        return pltpu.make_async_remote_copy(
            src_ref=source, dst_ref=target, send_sem=self.send.at[slot], recv_sem=self.recv.at[slot],
            device_id=to, device_id_type=MESH,
        )

    def rows(self, part):
        return pl.ds(self.offsets[part], self.offsets[part + 1] - self.offsets[part])

    def cell(self, a, b):
        return a * self.place.step_a + b * self.place.step_b

    def core_copy(self, k, part):
        place = self.place
        group = pl.ds(place.run(place.plane(k), 1 - place.core), self.cells)
        return self.remote(
            k * self.parts + part, self.sources[part].at[group], self.land.at[k, :, self.rows(part)],
            place.other_core(),
        )

    def load_copy(self, t, part):
        place = self.place
        group = pl.ds(place.run(place.plane(self.order[t]), place.core), self.cells)
        return pltpu.make_async_copy(
            self.sources[part].at[group], self.ours.at[t % 2, :, self.rows(part)], self.load.at[t % 2, part]
        )

    def b_copy(self, k, a):
        place = self.place
        base = self.planes * self.parts
        return self.remote(
            base + 2 * k + a, self.land.at[k, self.cell(a, 1 - place.b)], self.got_b.at[k, a], place.across_b()
        )

    def a_copy(self, k):
        place = self.place
        base = self.planes * (self.parts + 2)
        return self.remote(
            base + k, self.land.at[k, self.cell(1 - place.a, place.b)], self.got_a.at[k], place.across_a()
        )

    def z_copy(self, k):
        place = self.place
        base = self.planes * (self.parts + 3)
        return self.remote(
            base + k, self.land.at[k, self.cell(place.a, place.b)], self.got_z.at[k], place.along_z(k)
        )

    def start(self, part):
        for k in self.order:
            self.core_copy(k, part).start()

    def load_first(self):
        for part in range(self.parts):
            self.load_copy(0, part).start()

    def arrive_core(self, t):
        k = self.order[t]
        if t + 1 < self.planes:
            for part in range(self.parts):
                self.load_copy(t + 1, part).start()
        for part in range(self.parts):
            self.load_copy(t, part).wait()
            self.core_copy(k, part).wait_recv()

        def add(cell, _):
            self.land[k, cell] = self.land[k, cell] + self.ours[t % 2, cell]
            return 0

        lax.fori_loop(0, self.cells, add, 0)
        for a in range(self.side):
            self.b_copy(k, a).start()

    def arrive_b(self, t):
        k = self.order[t]
        for a in range(self.side):
            self.b_copy(k, a).wait_recv()
            at = self.cell(a, self.place.b)
            self.land[k, at] = self.land[k, at] + self.got_b[k, a]
        self.a_copy(k).start()

    def arrive_a(self, t):
        k = self.order[t]
        self.a_copy(k).wait_recv()
        at = self.cell(self.place.a, self.place.b)
        if k:
            self.land[k, at] = self.land[k, at] + self.got_a[k]
            self.z_copy(k).start()
        else:
            self.mine[...] = self.land[k, at].astype(F32) + self.got_a[k].astype(F32)

    def finish(self):
        for k in range(1, self.planes):
            self.z_copy(k).wait_recv()
            self.mine[...] += self.got_z[k].astype(F32)
        for k in range(self.planes):
            for part in range(self.parts):
                self.core_copy(k, part).wait_send()
            for a in range(self.side):
                self.b_copy(k, a).wait_send()
            self.a_copy(k).wait_send()
            if k:
                self.z_copy(k).wait_send()


def forward_kernel(
    planes, side, rows,
    first_ref, second_ref, hid_ref, emb_ref, seg_ref,
    packed_ref, mixed_ref, mid_ref, norm_ref, total_ref, vec_ref, w_qkv, w_out, *rest,
):
    if planes:
        full2, first, tail, bias_cols, mask_q, mask_k, load, send1, recv1, send2, recv2 = rest
    else:
        first, tail, bias_cols, mask_q, mask_k, load = rest
        full2 = second_ref
    step = pl.program_id(0)
    attending = step < 8 * rows
    row, phase = step // 8, step % 8

    if planes:
        place = Place(planes, side)
        gather2 = Gather(place, second_ref, full2, send2, recv2)

        @pl.when(step == 0)
        def _():
            place.greet()
            gather1 = Gather(place, first_ref, first, send1, recv1)
            for t in range(planes + 4):
                if t == planes + 2:
                    gather2.tick(0)
                gather1.tick(t)

        for at, t in zip(SCHED, range(1, planes + 4)):
            @pl.when(step == at)
            def _(t=t):
                gather2.tick(t)
    else:
        @pl.when(step == 0)
        def _():
            c = pltpu.make_async_copy(first_ref, first, load.at[0])
            c.start()
            c.wait()

    @pl.when(step == 0)
    def _():
        join_rows(first, 0, QROWS, w_qkv, BLOCKS // 2)
        vec_ref[0] = sum_rows(first, QROWS)
        bias_cols[0] = column(vec_ref[0, 2:3, :])
        bias_cols[1] = jnp.zeros((D, 1), F32)
        bias_cols[2] = column(vec_ref[0, 3:4, :])

    @pl.when(attending & (phase < 2))
    def _():
        at = pl.ds(pl.multiple_of(phase * TOKB, TOKB), TOKB)
        entered = hid_ref[...].astype(F32) + emb_ref[...].astype(F32)
        scaled, _ = normalise(entered)
        normed = (scaled * vec_ref[0, 0:1, :] + vec_ref[0, 1:2, :]).astype(BF16)
        for part in range(3):
            rows_at = slice(part * D, (part + 1) * D)
            packed_ref[rows_at, at] = (mm(w_qkv[rows_at, :], normed, 1, 1) + bias_cols[part]).astype(BF16)

    @pl.when(attending & (phase == 0))
    def _():
        query_side, key_side = mask_rows(seg_ref[0])
        mask_q[...] = query_side
        mask_k[...] = key_side

    @pl.when(attending & (phase >= 2))
    def _():
        base = pl.multiple_of((phase - 2) * 128, 128)
        ones_rows = jnp.where(lax.broadcasted_iota(jnp.int32, (HEAD, ROW), 0) == 0, 1.0, 0.0).astype(BF16)
        sides = []
        for h in range(2):
            at = base + HEAD * h
            high, low = scaled_query(packed_ref[pl.ds(at, HEAD), :])
            keys = packed_ref[pl.ds(D + at, HEAD), :]
            sides.append((
                jnp.concatenate([high, low, mask_q[...]], axis=0),
                jnp.concatenate([keys, keys, mask_k[...]], axis=0),
                jnp.concatenate([packed_ref[pl.ds(2 * D + at, HEAD), :], ones_rows], axis=0),
            ))
        all_scores = [mm(sides[h][1], sides[h][0], 0, 0) for h in range(2)]
        mixed = []
        for h in range(2):
            scores = all_scores[h]
            top = jnp.max(scores, axis=0, keepdims=True)
            weights = jnp.exp2(scores - top).astype(BF16)
            summed = mm(sides[h][2], weights, 1, 0)
            total = summed[HEAD : HEAD + 1, :]
            mixed.append(summed[:HEAD, :] / total)
            total_ref[0, h : h + 1, :] = top + jnp.log2(total)
        tokens = pl.ds(pl.multiple_of(row * ROW, ROW), ROW)
        mixed_ref[tokens, pl.ds(base, 128)] = jnp.concatenate(mixed, axis=0).T

    @pl.when(step == 8 * rows)
    def _():
        c = pltpu.make_async_copy(full2.at[:, pl.ds(2 * UROWS, 32)], tail, load.at[0])
        c.start()
        c.wait()
        join_rows(tail, 0, OROWS, w_out, BLOCKS // 2)
        vec_ref[1] = sum_rows(tail, OROWS)

    @pl.when(step >= 8 * rows)
    def _():
        tokens = pl.ds(pl.multiple_of((step - 8 * rows) * TOKB, TOKB), TOKB)
        entered = hid_ref[...].astype(F32) + emb_ref[...].astype(F32)
        middle = entered + mm(mixed_ref[tokens, :].astype(BF16), w_out[...], 1, 1) + vec_ref[0, 4:5, :]
        scaled, _ = normalise(middle)
        mid_ref[...] = middle
        norm_ref[...] = (scaled * vec_ref[0, 5:6, :] + vec_ref[0, 6:7, :]).astype(BF16)


def forward(planes, side, first, second, hidden, embed, segment):
    n = hidden.shape[0]
    rows = n // ROW
    one = pl.Buffered(1)
    hbm = pl.BlockSpec(memory_space=pl.ANY)

    def row(s):
        return jnp.minimum(s // 8, rows - 1)

    def entry(s):
        return (jnp.where(s < 8 * rows, 2 * (s // 8) + jnp.minimum(s % 8, 1), s - 8 * rows), 0)

    def leave(s):
        return (jnp.maximum(s - 8 * rows, 0), 0)

    def pair(s):
        return jnp.where(s < 8 * rows, jnp.maximum(s % 8 - 2, 0), 5)

    entering = pl.BlockSpec((TOKB, D), entry)
    leaving = pl.BlockSpec((TOKB, D), leave)
    out_specs = [
        pl.BlockSpec((3 * D, ROW), lambda s: (0, row(s))),
        pl.BlockSpec((n, D), lambda s: (0, 0), pipeline_mode=one),
        leaving,
        leaving,
        pl.BlockSpec((1, 8, ROW), lambda s: (pair(s), 0, row(s))),
        pl.BlockSpec((2, 8, D), lambda s: (0, 0, 0)),
        pl.BlockSpec((3 * D, D), lambda s: (0, 0), pipeline_mode=one),
        pl.BlockSpec((D, D), lambda s: (0, 0), pipeline_mode=one),
    ]
    out_shape = [
        jax.ShapeDtypeStruct((3 * D, n), BF16),
        jax.ShapeDtypeStruct((n, D), F32),
        jax.ShapeDtypeStruct((n, D), F32),
        jax.ShapeDtypeStruct((n, D), BF16),
        jax.ShapeDtypeStruct((HEADS // 2, 8, n), F32),
        jax.ShapeDtypeStruct((2, 8, D), F32),
        jax.ShapeDtypeStruct((3 * D, D), BF16),
        jax.ShapeDtypeStruct((D, D), BF16),
    ]
    scratch = [
        pltpu.VMEM((BLOCKS, FIRST, D), BF16),
        pltpu.VMEM((BLOCKS, 32, D), BF16),
        pltpu.VMEM((3, D, 1), F32),
        pltpu.VMEM((32, ROW), BF16),
        pltpu.VMEM((32, ROW), BF16),
        pltpu.SemaphoreType.DMA((1,)),
    ]
    params = dict(vmem_limit_bytes=62 * MIB)
    if planes:
        out_specs.append(hbm)
        out_shape.append(jax.ShapeDtypeStruct((BLOCKS, SECOND, D), BF16))
        scratch += [Gather.semaphores(planes)] * 4
        params.update(collective_id=1, has_side_effects=True)
    outs = pl.pallas_call(
        partial(forward_kernel, planes, side, rows),
        grid=(10 * rows,),
        in_specs=[
            hbm,
            hbm,
            entering,
            entering,
            pl.BlockSpec((1, 1, ROW), lambda s: (row(s), 0, 0)),
        ],
        out_specs=out_specs,
        out_shape=out_shape,
        scratch_shapes=scratch,
        compiler_params=pltpu.CompilerParams(**params),
        name="attention_forward",
    )(first, second, hidden, embed, segment.reshape(rows, 1, ROW))
    return outs if planes else list(outs) + [second]


def feed_kernel(
    blocks,
    up_ref, down_ref, vec_ref, norm_ref, mid_ref, cot_ref, seg_ref,
    out_ref, gmid_ref, gup_ref, gdown_ref, gvec_ref,
    w_down, result, back, live, sum_up, sum_down,
):
    j, i = pl.program_id(0), pl.program_id(1)
    at = pl.ds(pl.multiple_of(i * TOKB, TOKB), TOKB)

    @pl.when(i == 0)
    def _():
        for chunk in range(CHUNKS):
            @pl.when(j == chunk)
            def _():
                join_rows(down_ref, chunk * OROWS, OROWS, w_down, BLOCKS // 2)

    @pl.when((j == 0) & (i == 0))
    def _():
        gvec_ref[...] = jnp.zeros_like(gvec_ref)

    @pl.when(j == 0)
    def _():
        keep = column(jnp.where(seg_ref[0] >= 0, 1.0, 0.0))
        grad_result = cot_ref[...].astype(F32) * keep
        live[at, :] = grad_result.astype(BF16)
        gvec_ref[4:5, :] += jnp.sum(grad_result, axis=0, keepdims=True)

    normed = norm_ref[...]
    grad_result = live[at, :]
    up = up_ref[...].reshape(D, D)
    down = w_down[...]
    x = mm(normed, up, 1, 1) + vec_ref[1, pl.ds(j, 1), :]
    grad_act = mm(grad_result, down, 1, 0)
    c0 = math.sqrt(2.0 / math.pi)
    c1 = 0.044715
    square = x * x
    th = jnp.tanh(x * (c0 + (c0 * c1) * square))
    half = 0.5 + 0.5 * th
    activated = (x * half).astype(BF16)
    slope = half + (0.5 * x) * ((1.0 - th * th) * (c0 + (3 * c0 * c1) * square))
    grad_pre32 = grad_act * slope
    grad_pre = grad_pre32.astype(BF16)
    gvec_ref[pl.ds(j, 1), :] += jnp.sum(grad_pre.astype(F32), axis=0, keepdims=True)
    part = mm(activated, down, 1, 1)
    part_back = mm(grad_pre, up, 1, 0)
    part_down = mm(grad_result, activated, 0, 0)
    part_up = mm(grad_pre, normed, 0, 0)

    odd = j % 2

    @pl.when(i == 0)
    def _():
        sum_down[odd] = part_down
        sum_up[...] = part_up

    @pl.when(i > 0)
    def _():
        sum_down[odd] += part_down
        sum_up[...] += part_up

    @pl.when(i == blocks - 1)
    def _():
        gup_ref[...] = sum_up[...].astype(BF16)

    @pl.when((i == blocks - 1) & (odd == 1))
    def _():
        def pack(d, _):
            at = pl.ds(pl.multiple_of(d * OROWS, 8), OROWS)
            gdown_ref[d] = jnp.concatenate([sum_down[0, at], sum_down[1, at]], axis=0).astype(BF16)
            return 0

        lax.fori_loop(0, BLOCKS, pack, 0)

    @pl.when(j == 0)
    def _():
        result[at, :] = part
        back[at, :] = part_back

    @pl.when((j > 0) & (j < CHUNKS - 1))
    def _():
        result[at, :] += part
        back[at, :] += part_back

    @pl.when(j == CHUNKS - 1)
    def _():
        middle = mid_ref[...]
        out_ref[...] = (middle + (result[at, :] + part + vec_ref[0, 7:8, :])).astype(BF16)
        grad = back[at, :] + part_back
        scaled, inverse = normalise(middle)
        gvec_ref[5:6, :] += jnp.sum(grad * scaled, axis=0, keepdims=True)
        gvec_ref[6:7, :] += jnp.sum(grad, axis=0, keepdims=True)
        gmid_ref[...] = grad_result.astype(F32) + norm_back(grad, scaled, inverse, vec_ref[0, 5:6, :])


def feed(second, vec, normed, middle, cotangent, segment):
    n = normed.shape[0]
    blocks = n // TOKB
    one = pl.Buffered(1)
    last = CHUNKS - 1
    tokens = pl.BlockSpec((TOKB, D), lambda j, i: (i, 0))
    at_first = pl.BlockSpec((TOKB, D), lambda j, i: (jnp.where(j == 0, i, blocks - 1), 0))
    at_last = pl.BlockSpec((TOKB, D), lambda j, i: (jnp.where(j == last, i, 0), 0))
    return pl.pallas_call(
        partial(feed_kernel, blocks),
        grid=(CHUNKS, blocks),
        in_specs=[
            pl.BlockSpec((BLOCKS // CHUNKS, UROWS, D), lambda j, i: (j, 0, 0)),
            pl.BlockSpec((BLOCKS, UROWS, D), lambda j, i: (0, 1, 0), pipeline_mode=one),
            pl.BlockSpec((2, 8, D), lambda j, i: (0, 0, 0)),
            tokens,
            at_last,
            at_first,
            pl.BlockSpec((1, 1, TOKB), lambda j, i: (i, 0, 0)),
        ],
        out_specs=[
            at_last,
            at_last,
            pl.BlockSpec((D, D), lambda j, i: (j, 0)),
            pl.BlockSpec((BLOCKS, 2 * OROWS, D), lambda j, i: (0, j // 2, 0)),
            pl.BlockSpec((8, D), lambda j, i: (0, 0)),
        ],
        out_shape=[
            jax.ShapeDtypeStruct((n, D), BF16),
            jax.ShapeDtypeStruct((n, D), F32),
            jax.ShapeDtypeStruct((FF, D), BF16),
            jax.ShapeDtypeStruct((BLOCKS, UROWS, D), BF16),
            jax.ShapeDtypeStruct((8, D), F32),
        ],
        scratch_shapes=[
            pltpu.VMEM((D, D), BF16),
            pltpu.VMEM((n, D), F32),
            pltpu.VMEM((n, D), F32),
            pltpu.VMEM((n, D), BF16),
            pltpu.VMEM((D, D), F32),
            pltpu.VMEM((2, D, D), F32),
        ],
        compiler_params=pltpu.CompilerParams(vmem_limit_bytes=60 * MIB),
        name="feed_forward",
    )(second, second, vec, normed, middle, cotangent, segment.reshape(blocks, 1, TOKB))


def three_parts(row):
    r = lax.broadcasted_iota(jnp.int32, (16, row.shape[1]), 0)
    a = row.astype(BF16).astype(F32)
    b = (row - a).astype(BF16).astype(F32)
    c = row - a - b
    return jnp.where(r == 0, -a, jnp.where(r == 1, -b, jnp.where(r == 2, -c, 0.0))).astype(BF16)


def backward_kernel(
    planes, side, rows,
    w_out, seg_ref, packed_q, packed_k, packed_v, mixed_ref, total_ref, gmid_ref, gvec_ref, gup_ref, gdown_ref,
    grad_q_ref, grad_k_ref, grad_v_ref, sums_ref, *rest,
):
    if planes:
        mine, mask_q, mask_k, grad_mixed, delta, sum_out, sum_bias, tail, *transfer = rest
    else:
        tail, mask_q, mask_k, grad_mixed, delta, sum_out, sum_bias = rest
    step = pl.program_id(0)
    entry = 2 * rows
    heads = step >= entry

    if planes:
        place = Place(planes, side)
        scatter = Scatter(place, (gup_ref, gdown_ref, tail), *transfer[:5], mine, *transfer[5:])

        @pl.when(step == 0)
        def _():
            place.greet()
            scatter.start(0)
            scatter.start(1)

        @pl.when(step == entry)
        def _():
            scatter.start(2)
            scatter.load_first()

        for at, t, act in BACK:
            @pl.when(step == entry + at)
            def _(t=t, act=act):
                getattr(scatter, act)(t)

    @pl.when(step == 0)
    def _():
        sum_out[...] = jnp.zeros_like(sum_out)
        sum_bias[...] = jnp.zeros_like(sum_bias)

    @pl.when(step < entry)
    def _():
        at = pl.ds(pl.multiple_of(step * TOKB, TOKB), TOKB)
        mixed = mixed_ref[...]
        branch = gmid_ref[...].astype(BF16)
        sum_bias[0:1, :] += jnp.sum(branch.astype(F32), axis=0, keepdims=True)
        sum_out[...] += mm(branch, mixed.astype(BF16), 0, 0)
        grad = mm(branch, w_out[...], 1, 0).astype(BF16).astype(F32)
        grad_mixed[:, at] = grad.T.astype(BF16)
        inner = (grad * mixed).T
        delta[:, at] = jnp.concatenate(
            [jnp.sum(inner[HEAD * h : HEAD * (h + 1)], axis=0, keepdims=True) for h in range(HEADS)]
            + [jnp.zeros((16 - HEADS, TOKB), F32)],
            axis=0,
        )

    @pl.when(step == entry - 1)
    def _():
        r = lax.broadcasted_iota(jnp.int32, (8, D), 0)
        vectors = jnp.where(r == 7, sum_bias[0:1, :], gvec_ref[...])

        def pack(d, _):
            at = pl.ds(pl.multiple_of(d * OROWS, 8), OROWS)
            tail[d] = jnp.concatenate([sum_out[at, :], vectors], axis=0).astype(BF16)
            return 0

        lax.fori_loop(0, BLOCKS, pack, 0)

    row, pair = (step - entry) // 6, (step - entry) % 6

    @pl.when(heads & (pair == 0))
    def _():
        query_side, key_side = mask_rows(seg_ref[0])
        mask_q[...] = query_side
        mask_k[...] = key_side

    @pl.when(heads)
    def _():
        tokens = pl.ds(pl.multiple_of(row * ROW, ROW), ROW)
        r = lax.broadcasted_iota(jnp.int32, (16, ROW), 0)
        ones_rows = jnp.where(r < 3, 1.0, 0.0).astype(BF16)
        base = pl.multiple_of(pair * 128, 128)
        column_sums = []
        for h in range(2):
            at_rows = slice(HEAD * h, HEAD * (h + 1))
            queries, keys, values = packed_q[at_rows, :], packed_k[at_rows, :], packed_v[at_rows, :]
            grad = grad_mixed[pl.ds(base + HEAD * h, HEAD), tokens]
            high, low = scaled_query(queries)
            wide_q = jnp.concatenate([high, low, mask_q[...], three_parts(total_ref[0, h : h + 1, :])], axis=0)
            wide_k = jnp.concatenate([keys, keys, mask_k[...], ones_rows], axis=0)
            wide_g = jnp.concatenate([grad, three_parts(delta[pl.ds(2 * pair + h, 1), tokens])], axis=0)
            wide_v = jnp.concatenate([values, ones_rows], axis=0)
            grad_v = jnp.zeros((HEAD, ROW), F32)
            grad_k = jnp.zeros((HEAD, ROW), F32)
            grad_q = []
            for half in range(2):
                at = slice(half * (ROW // 2), (half + 1) * (ROW // 2))
                probs = jnp.exp2(mm(wide_q[:, at], wide_k, 0, 0))
                grad_probs = mm(wide_g[:, at], wide_v, 0, 0)
                grad_scores = (probs * grad_probs).astype(BF16)
                grad_v = grad_v + mm(grad[:, at], probs.astype(BF16), 1, 0)
                grad_k = grad_k + mm(queries[:, at], grad_scores, 1, 0)
                grad_q.append(mm(keys, grad_scores, 1, 1))
            grads = (
                (jnp.concatenate(grad_q, axis=1) * 0.125).astype(BF16),
                (grad_k * 0.125).astype(BF16),
                grad_v.astype(BF16),
            )
            for out, grad_rows in zip((grad_q_ref, grad_k_ref, grad_v_ref), grads):
                out[at_rows, :] = grad_rows
            column_sums.append([jnp.sum(g.astype(F32), axis=1, keepdims=True) for g in grads])
        for part in range(3):
            both = jnp.concatenate([column_sums[0][part], column_sums[1][part]], axis=0)
            at = pl.ds(part * D + base, 128)

            @pl.when(row == 0)
            def _():
                sums_ref[at, :] = both

            @pl.when(row > 0)
            def _():
                sums_ref[at, :] += both

    if planes:
        @pl.when(step == entry + 6 * rows - 1)
        def _():
            scatter.finish()


def backward(planes, side, w_out, segment, packed, mixed, totals, gmid, gvec, gup, gdown):
    n = mixed.shape[0]
    rows = n // ROW
    entry = 2 * rows
    one = pl.Buffered(1)
    hbm = pl.BlockSpec(memory_space=pl.ANY)

    def early(s):
        return (jnp.minimum(s, entry - 1), 0)

    def row(s):
        return jnp.maximum(s - entry, 0) // 6

    def pair(s):
        return jnp.maximum(s - entry, 0) % 6

    def heads(part):
        return pl.BlockSpec((128, ROW), lambda s: (6 * part + pair(s), row(s)))

    grads = [pl.BlockSpec((128, ROW), lambda s: (pair(s), row(s)))] * 3
    out_specs = grads + [pl.BlockSpec((3 * D, 1), lambda s: (0, 0), pipeline_mode=one)]
    out_shape = [jax.ShapeDtypeStruct((D, n), BF16)] * 3 + [jax.ShapeDtypeStruct((3 * D, 1), F32)]
    scratch = [
        pltpu.VMEM((32, ROW), BF16),
        pltpu.VMEM((32, ROW), BF16),
        pltpu.VMEM((D, n), BF16),
        pltpu.VMEM((16, n), F32),
        pltpu.VMEM((D, D), F32),
        pltpu.VMEM((8, D), F32),
    ]
    params = dict(vmem_limit_bytes=60 * MIB)
    if planes:
        rows1 = 2 * UROWS + 32
        out_specs.append(pl.BlockSpec((rows1, D), lambda s: (0, 0), pipeline_mode=one))
        out_shape.append(jax.ShapeDtypeStruct((rows1, D), F32))
        scratch.append(pltpu.VMEM((BLOCKS, 32, D), BF16))
        scratch += Scatter.scratch(planes, side, 3, rows1)
        params.update(collective_id=2, has_side_effects=True)
    else:
        out_specs.append(pl.BlockSpec((BLOCKS, 32, D), lambda s: (0, 0, 0), pipeline_mode=one))
        out_shape.append(jax.ShapeDtypeStruct((BLOCKS, 32, D), BF16))
    return pl.pallas_call(
        partial(backward_kernel, planes, side, rows),
        grid=(entry + 6 * rows,),
        in_specs=[
            pl.BlockSpec((D, D), lambda s: (0, 0), pipeline_mode=one),
            pl.BlockSpec((1, 1, ROW), lambda s: (row(s), 0, 0)),
            heads(0),
            heads(1),
            heads(2),
            pl.BlockSpec((TOKB, D), early),
            pl.BlockSpec((1, 8, ROW), lambda s: (pair(s), 0, row(s))),
            pl.BlockSpec((TOKB, D), early),
            pl.BlockSpec((8, D), lambda s: (0, 0)),
            hbm,
            hbm,
        ],
        out_specs=out_specs,
        out_shape=out_shape,
        scratch_shapes=scratch,
        compiler_params=pltpu.CompilerParams(**params),
        name="attention_backward",
    )(w_out, segment.reshape(rows, 1, ROW), packed, packed, packed, mixed, totals, gmid, gvec, gup, gdown)


def enter_kernel(
    planes, side, blocks,
    w_qkv, vec_ref, hid_ref, emb_ref, gmid_ref, grad_q, grad_k, grad_v, sums_ref,
    ghid_ref, out_ref, *rest,
):
    if planes:
        mine, (scaled_all, sum_w, packed, *transfer) = out_ref, rest
    else:
        packed, (scaled_all, sum_w) = out_ref, rest
    step = pl.program_id(0)
    grads = (grad_q, grad_k, grad_v)

    if planes:
        place = Place(planes, side)
        scatter = Scatter(place, (packed,), *transfer[:5], mine, *transfer[5:])

        @pl.when(step == 0)
        def _():
            place.greet()

    def entering():
        return normalise(hid_ref[...].astype(F32) + emb_ref[...].astype(F32))

    @pl.when(step < blocks)
    def _():
        scaled, _ = entering()
        scaled_all[pl.ds(pl.multiple_of(step * TOKB, TOKB), TOKB), :] = scaled.astype(BF16)

    @pl.when(step == blocks - 1)
    def _():
        gain, shift = vec_ref[0, 0:1, :], vec_ref[0, 1:2, :]
        grad_gain = jnp.zeros((1, D), F32)
        grad_shift = jnp.zeros((1, D), F32)
        for part in range(3):
            product = mm(grads[part][...], scaled_all[...], 1, 0)
            at = slice(part * D, (part + 1) * D)
            weight = w_qkv[at, :].astype(F32)
            sums = sums_ref[at, :]
            grad_gain += jnp.sum(weight * product, axis=0, keepdims=True)
            grad_shift += jnp.sum(weight * sums, axis=0, keepdims=True)
            sum_w[at, :] = product * gain + sums * shift
        ends = [jnp.broadcast_to(sums_ref[at : at + D, :], (D, 128)).T[0:1, :] for at in (0, 2 * D)]
        vectors = jnp.concatenate([grad_gain, grad_shift] + ends + [jnp.zeros((4, D), F32)], axis=0)

        def pack(d, _):
            at = pl.ds(pl.multiple_of(d * QROWS, 8), QROWS)
            packed[d] = jnp.concatenate([sum_w[at, :], vectors], axis=0).astype(BF16)
            return 0

        lax.fori_loop(0, BLOCKS, pack, 0)
        if planes:
            scatter.start(0)
            scatter.load_first()

    if planes:
        for at, t, act in ENTER:
            @pl.when(step == blocks + at)
            def _(t=t, act=act):
                getattr(scatter, act)(t)

    @pl.when(step >= blocks)
    def _():
        at = pl.ds(pl.multiple_of((step - blocks) * TOKB, TOKB), TOKB)
        scaled, inverse = entering()
        grad = mm(grad_q[:, at], w_qkv[0:D, :], 0, 0)
        grad += mm(grad_k[:, at], w_qkv[D : 2 * D, :], 0, 0)
        grad += mm(grad_v[:, at], w_qkv[2 * D : 3 * D, :], 0, 0)
        ghid_ref[...] = (gmid_ref[...] + norm_back(grad, scaled, inverse, vec_ref[0, 0:1, :])).astype(BF16)

    if planes:
        @pl.when(step == 2 * blocks - 1)
        def _():
            for t, act in ENTER_LAST:
                getattr(scatter, act)(t)
            scatter.finish()


def enter(planes, side, w_qkv, vec, hidden, embed, gmid, grads, sums):
    n = hidden.shape[0]
    blocks = n // TOKB
    one = pl.Buffered(1)

    def late(s):
        return (jnp.maximum(s - blocks, 0), 0)

    tokens = pl.BlockSpec((TOKB, D), lambda s: (s % blocks, 0))
    whole = pl.BlockSpec((D, n), lambda s: (0, 0), pipeline_mode=one)
    out_specs = [pl.BlockSpec((TOKB, D), late)]
    out_shape = [jax.ShapeDtypeStruct((n, D), BF16)]
    scratch = [pltpu.VMEM((n, D), BF16), pltpu.VMEM((3 * D, D), F32)]
    params = dict(vmem_limit_bytes=62 * MIB)
    if planes:
        out_specs.append(pl.BlockSpec((FIRST, D), lambda s: (0, 0), pipeline_mode=one))
        out_shape.append(jax.ShapeDtypeStruct((FIRST, D), F32))
        scratch.append(pltpu.VMEM((BLOCKS, FIRST, D), BF16))
        scratch += Scatter.scratch(planes, side, 1, FIRST)
        params.update(collective_id=3, has_side_effects=True)
    else:
        out_specs.append(pl.BlockSpec((BLOCKS, FIRST, D), lambda s: (0, 0, 0), pipeline_mode=one))
        out_shape.append(jax.ShapeDtypeStruct((BLOCKS, FIRST, D), BF16))
    return pl.pallas_call(
        partial(enter_kernel, planes, side, blocks),
        grid=(2 * blocks,),
        in_specs=[
            pl.BlockSpec((3 * D, D), lambda s: (0, 0), pipeline_mode=one),
            pl.BlockSpec((2, 8, D), lambda s: (0, 0, 0)),
            tokens,
            tokens,
            pl.BlockSpec((TOKB, D), late),
            whole,
            whole,
            whole,
            pl.BlockSpec((3 * D, 1), lambda s: (0, 0), pipeline_mode=one),
        ],
        out_specs=out_specs,
        out_shape=out_shape,
        scratch_shapes=scratch,
        compiler_params=pltpu.CompilerParams(**params),
        name="projection_backward",
    )(w_qkv, vec, hidden, embed, gmid, *grads, sums)


def placed(vector, index, devices):
    here = (jnp.arange(devices) == index)[:, None]
    return jnp.where(here, vector[None, :], jnp.zeros((), vector.dtype)).reshape(-1)


def body(
    planes, side, devices,
    hidden, time_embed, segment_ids,
    ln1_gain, ln1_bias, w_qkv, b_query, b_value, w_out, b_out, ln2_gain, ln2_bias, w_up, b_up, w_down, b_down,
    cotangent,
):
    index = lax.axis_index("dp") * lax.axis_size("fsdp") + lax.axis_index("fsdp")
    axes = ("dp", "fsdp")
    small = (ln1_gain, ln1_bias, b_query, b_value, b_out, ln2_gain, ln2_bias, b_down)
    if planes:
        vec1 = jnp.stack([placed(v, index, devices) for v in small])
        vec2 = placed(b_up, index, devices).reshape(CHUNKS, D)
        vec2 = jnp.concatenate([vec2, jnp.zeros((8 - CHUNKS, D), BF16)], axis=0)
        down_rows = w_down.T.reshape(OROWS, CHUNKS, D).transpose(1, 0, 2).reshape(UROWS, D)
        own1 = jnp.concatenate([w_qkv.T, vec1], axis=0)
        own2 = jnp.concatenate([w_up.T, down_rows, w_out.T, vec2], axis=0)
        first, second = own1, own2
    else:
        def whole(a, dim):
            return lax.all_gather(a, axes, axis=dim, tiled=True)

        def only_first(rows):
            return jnp.concatenate([rows[None], jnp.zeros((BLOCKS - 1,) + rows.shape, BF16)], axis=0)

        vec1 = jnp.stack([whole(v, 0) for v in small])
        vec2 = jnp.concatenate([whole(b_up, 0).reshape(CHUNKS, D), jnp.zeros((8 - CHUNKS, D), BF16)], axis=0)
        down_rows = whole(w_down, 1).T.reshape(BLOCKS, OROWS, CHUNKS, D).transpose(0, 2, 1, 3)
        first = jnp.concatenate([whole(w_qkv, 1).T.reshape(BLOCKS, QROWS, D), only_first(vec1)], axis=1)
        second = jnp.concatenate(
            [
                whole(w_up, 1).T.reshape(BLOCKS, UROWS, D),
                down_rows.reshape(BLOCKS, UROWS, D),
                whole(w_out, 1).T.reshape(BLOCKS, OROWS, D),
                only_first(vec2),
            ],
            axis=1,
        )
    packed, mixed, middle, normed, totals, vec, full_qkv, full_out, second = forward(
        planes, side, first, second, hidden, time_embed, segment_ids
    )
    output, gmid, gup, gdown, gvec = feed(second, vec, normed, middle, cotangent, segment_ids)
    gup = gup.reshape(BLOCKS, UROWS, D)
    *grads, sums, late = backward(
        planes, side, full_out, segment_ids, packed, mixed, totals, gmid, gvec, gup, gdown
    )
    ghid, last = enter(planes, side, full_qkv, vec, hidden, time_embed, gmid, grads, sums)
    if planes:
        part_up = late[:UROWS]
        part_down = late[UROWS : 2 * UROWS].reshape(CHUNKS, OROWS, D).transpose(1, 0, 2).reshape(OROWS, FF)
        part_out = late[2 * UROWS : 2 * UROWS + OROWS]
        part_qkv = last[:QROWS]
        vectors = jnp.concatenate([late[2 * UROWS + OROWS :], last[QROWS:]], axis=0)
        short = lax.dynamic_slice(vectors, (0, index * OROWS), (16, OROWS))
        part_bup = lax.dynamic_slice(vectors[:CHUNKS].reshape(-1), (index * UROWS,), (UROWS,))
    else:
        def shared(a, dim):
            return lax.psum_scatter(a.astype(F32), axes, scatter_dimension=dim, tiled=True)

        part_up = shared(gup.reshape(FF, D), 0)
        part_down = shared(gdown.reshape(BLOCKS, CHUNKS, OROWS, D).transpose(0, 2, 1, 3).reshape(D, FF), 0)
        part_out = shared(late[:, :OROWS].reshape(D, D), 0)
        part_qkv = shared(last[:, :QROWS].reshape(3 * D, D), 0)
        vectors = jnp.concatenate([late[0, OROWS:], last[0, QROWS:]], axis=0)
        short = shared(vectors, 1)
        part_bup = shared(vectors[:CHUNKS].reshape(-1), 0)
    return (
        output, ghid,
        short[8], short[9], part_qkv.T, short[10], short[11], part_out.T, short[7],
        short[5], short[6], part_up.T, part_bup, part_down.T, short[4],
    )


def solution(mesh):
    groups, cells = mesh.shape["dp"], mesh.shape["fsdp"]
    side = math.isqrt(cells)
    own_transfers = groups * cells == BLOCKS and side == 2 and cells == 4 and groups % 2 == 0
    split = ("dp", "fsdp")
    rows, flat, cols = P(split, None), P(split), P(None, split)
    return jax.shard_map(
        partial(body, groups // 2 if own_transfers else 0, side, groups * cells),
        mesh=mesh,
        in_specs=(
            rows, rows, flat, flat, flat, cols, flat, flat, cols, flat, flat, flat, cols, flat, cols, flat, rows,
        ),
        out_specs=(
            rows, rows, flat, flat, cols, flat, flat, cols, flat, flat, flat, cols, flat, cols, flat,
        ),
        check_vma=False,
    )
```

```python
from functools import partial
import math

import jax
import jax.numpy as jnp
from jax import lax
from jax.experimental import pallas as pl
from jax.experimental.pallas import tpu as pltpu
from jax.sharding import PartitionSpec as P

D = 768
HEADS = 12
HEAD = 64
FF = 3072
ROW = 1024
BLOCKS = 32
QROWS = 3 * D // BLOCKS
OROWS = D // BLOCKS
UROWS = FF // BLOCKS
CHUNKS = FF // D
FIRST = QROWS + 8
SECOND = 2 * UROWS + OROWS + 8
TOKB = 512
LAST = 256
MIB = 2**20
MESH = pl.DeviceIdType.MESH
F32 = jnp.float32
BF16 = jnp.bfloat16
LOG2E = math.log2(math.e)
EPS = 1e-05
FIRST_SCHED = (
    (0, "z", 1), (0, "a", 0), (0, "z", 2), (0, "a", 1), (0, "z", 3), (1, "s", 1), (1, "s", 2), (0, "b", 0), (0, "a", 2),
    (0, "b", 1), (0, "a", 3), (1, "o", 0), (0, "b", 2), (0, "b", 3), (0, "end", 0),
)
SCHED = (
    (0, "z", 1), (0, "s", 3), (1, "a", 0), (2, "a", 1), (2, "z", 2), (3, "b", 0), (5, "a", 2), (6, "z", 3), (6, "b", 1),
    (9, "a", 3), (9, "b", 2), (12, "b", 3), (13, "end", 0),
)
BACK = (
    (1, 0, "arrive_core"), (2, 1, "arrive_core"), (3, 0, "arrive_b"), (4, 2, "arrive_core"), (5, 1, "arrive_b"),
    (5, 0, "arrive_a"), (6, 3, "arrive_core"), (7, 2, "arrive_b"), (8, 1, "arrive_a"), (9, 3, "arrive_b"),
    (9, 2, "arrive_a"), (11, 3, "arrive_a"),
)
ENTER = (
    (2, 0, "arrive_core"), (3, 1, "arrive_core"), (4, 0, "arrive_b"), (4, 2, "arrive_core"), (5, 1, "arrive_b"),
    (5, 3, "arrive_core"), (6, 0, "arrive_a"), (6, 2, "arrive_b"), (7, 1, "arrive_a"), (7, 3, "arrive_b"),
)
ENTER_LAST = ((2, "arrive_a"), (3, "arrive_a"))


def mm(a, b, ca, cb):
    return lax.dot_general(a, b, (((ca,), (cb,)), ((), ())), preferred_element_type=F32)


def normalise(values):
    centred = values - jnp.mean(values, axis=-1, keepdims=True)
    inverse = lax.rsqrt(jnp.mean(centred * centred, axis=-1, keepdims=True) + EPS)
    return centred * inverse, inverse


def norm_back(grad, scaled, inverse, gain):
    u = grad * gain
    return inverse * (
        u
        - jnp.mean(u, axis=-1, keepdims=True)
        - scaled * jnp.mean(u * scaled, axis=-1, keepdims=True)
    )


def column(row):
    return jnp.broadcast_to(row, (128, row.shape[1])).T[:, :1]


def join_rows(source, start, rows, target, pairs):
    low = start // 16 * 16
    high = -(-(start + rows) // 16) * 16

    def step(p, _):
        parts = [
            source[2 * p + i, low:high, :].astype(F32)[start - low : start - low + rows]
            for i in range(2)
        ]
        at = pl.multiple_of(2 * rows * p, 2 * rows)
        target[pl.ds(at, 2 * rows), :] = jnp.concatenate(parts, axis=0).astype(BF16)
        return 0

    lax.fori_loop(0, pairs, step, 0)


def sum_rows(source, start):
    low = start // 16 * 16

    def step(d, total):
        return total + source[d, low : low + 16, :].astype(F32)[start - low : start - low + 8]

    return lax.fori_loop(0, BLOCKS, step, jnp.zeros((8, D), F32))


def mask_rows(segment):
    r = lax.broadcasted_iota(jnp.int32, (32, ROW), 0)
    hit = r == segment + 1
    query_side = jnp.where(hit, 1.0, 0.0).astype(BF16)
    key_side = jnp.where(hit | (r >= 17), 0.0, -1e30).astype(BF16)
    return query_side, key_side


def scaled_query(queries):
    wide = queries.astype(F32) * (LOG2E / 8)
    high = wide.astype(BF16)
    low = (wide - high.astype(F32)).astype(BF16)
    return high, low


class Place:
    def __init__(self, planes, side):
        self.planes, self.side = planes, side
        group, cell = lax.axis_index("dp"), lax.axis_index("fsdp")
        self.z, self.core = group // 2, group % 2
        y, x = cell // side, cell % side
        self.step_a = 1 + self.core * (side - 1)
        self.step_b = side - self.core * (side - 1)
        self.a = x + self.core * (y - x)
        self.b = y + self.core * (x - y)

    def plane(self, k):
        return lax.rem(self.z + k + self.planes, self.planes)

    def paired(self, k):
        plane, bit = self.z, 1
        while bit <= k:
            if k & bit:
                plane = plane + bit - 2 * bit * (self.z // bit % 2)
            bit *= 2
        return plane

    def at(self, z, core, a, b):
        return (z * 2 + core, a * self.step_a + b * self.step_b)

    def block(self, z, a, b):
        return (z * 2 + self.core) * (self.side * self.side) + a * self.step_a + b * self.step_b

    def run(self, z, core):
        return (z * 2 + core) * (self.side * self.side)

    def across_a(self):
        return self.at(self.z, self.core, 1 - self.a, self.b)

    def across_b(self):
        return self.at(self.z, self.core, self.a, 1 - self.b)

    def other_core(self):
        return (self.z * 2 + 1 - self.core, self.a * self.step_a + self.b * self.step_b)

    def along_z(self, k):
        return self.at(self.plane(k), self.core, self.a, self.b)

    def greet(self):
        barrier = pltpu.get_barrier_semaphore()
        peers = [self.along_z(k) for k in range(1, self.planes)]
        peers += [self.across_a(), self.across_b(), self.other_core()]
        for peer in peers:
            pl.semaphore_signal(barrier, inc=1, device_id=peer, device_id_type=MESH)
        pl.semaphore_wait(barrier, len(peers))


class Gather:
    def __init__(self, place, own, full, send, recv):
        self.place, self.own, self.full, self.send, self.recv = place, own, full, send, recv
        self.planes = place.planes

    @staticmethod
    def semaphores(planes):
        return pltpu.SemaphoreType.DMA((5 * planes + 1,))

    def copy(self, kind, k):
        place, full = self.place, self.full
        plane = place.paired(k)
        column = full.at[place.block(plane, place.a, place.b)]
        if kind == "z":
            source, target = self.own, full.at[place.block(place.z, place.a, place.b)]
            to = place.at(plane, place.core, place.a, place.b)
        elif kind == "a" or kind == "b":
            source, target = (column if k else self.own), column
            to = place.across_a() if kind == "a" else place.across_b()
        elif kind == "d":
            source = target = full.at[place.block(plane, 1 - place.a, place.b)]
            to = place.across_b()
        else:
            cells = place.side * place.side
            source = target = full.at[pl.ds(place.run(plane, place.core), cells)]
            to = place.other_core()
        i = "zabdc".index(kind) * self.planes + k
        return pltpu.make_async_remote_copy(
            src_ref=source, dst_ref=target, send_sem=self.send.at[i], recv_sem=self.recv.at[i],
            device_id=to, device_id_type=MESH,
        )

    def keep(self):
        place = self.place
        return pltpu.make_async_copy(
            self.own, self.full.at[place.block(place.z, place.a, place.b)], self.send.at[5 * self.planes]
        )

    def start_z(self, ways):
        for k in ways:
            self.copy("z", k).start()

    def start_ab(self):
        self.keep().start()
        self.copy("a", 0).start()
        self.copy("b", 0).start()

    def event(self, kind, k):
        if kind == "s":
            self.start_z((k,))
        elif kind == "o":
            self.start_ab()
        elif kind == "z":
            self.copy("z", k).wait_recv()
            self.copy("a", k).start()
            self.copy("b", k).start()
        elif kind == "a":
            self.copy("a", k).wait_recv()
            self.copy("d", k).start()
        elif kind == "b":
            self.copy("b", k).wait_recv()
            self.copy("d", k).wait_recv()
            if k == 0:
                self.keep().wait()
            self.copy("c", k).start()
        else:
            for k in range(self.planes):
                self.copy("c", k).wait_recv()
            for k in range(self.planes):
                for kind in "zabdc" if k else "abdc":
                    self.copy(kind, k).wait_send()


class Rider:
    def __init__(self, place, stages, got, send, recv):
        self.place, self.stages, self.got, self.send, self.recv = place, stages, got, send, recv

    @staticmethod
    def scratch(planes):
        count = 3 + planes
        return [
            pltpu.VMEM((4, 8, D), F32),
            pltpu.VMEM((count, 8, D), F32),
            pltpu.SemaphoreType.DMA((count,)),
            pltpu.SemaphoreType.DMA((count,)),
        ]

    def copy(self, i):
        place = self.place
        to = (place.other_core, place.across_b, place.across_a)[i]() if i < 3 else place.along_z(i - 3)
        return pltpu.make_async_remote_copy(
            src_ref=self.stages.at[min(i, 3)], dst_ref=self.got.at[i], send_sem=self.send.at[i], recv_sem=self.recv.at[i],
            device_id=to, device_id_type=MESH,
        )

    def start(self):
        self.copy(0).start()

    def arrive(self, i):
        self.copy(i).wait_recv()
        self.stages[i + 1] = self.stages[i] + self.got[i]
        if i < 2:
            self.copy(i + 1).start()
        else:
            for k in range(1, self.place.planes):
                self.copy(3 + k).start()

    def finish(self):
        total = self.stages[3]
        for k in range(1, self.place.planes):
            self.copy(3 + k).wait_recv()
            total = total + self.got[3 + k]
        for i in (0, 1, 2):
            self.copy(i).wait_send()
        for k in range(1, self.place.planes):
            self.copy(3 + k).wait_send()
        return total


class Scatter:
    def __init__(self, place, sources, land, ours, got_b, got_a, got_z, mine, load, send, recv):
        self.place, self.sources, self.land, self.ours = place, sources, land, ours
        self.got_b, self.got_a, self.got_z, self.mine = got_b, got_a, got_z, mine
        self.load, self.send, self.recv = load, send, recv
        self.planes, self.side = place.planes, place.side
        self.cells = place.side * place.side
        self.parts = len(sources)
        self.order = list(range(1, self.planes)) + [0]
        self.offsets = [sum(s.shape[1] for s in sources[:i]) for i in range(self.parts + 1)]

    @staticmethod
    def scratch(planes, side, parts, rows):
        cells = side * side
        count = planes * (parts + 4)
        return [
            pltpu.VMEM((planes, cells, rows, D), BF16),
            pltpu.VMEM((2, cells, rows, D), BF16),
            pltpu.VMEM((planes, side, rows, D), BF16),
            pltpu.VMEM((planes, rows, D), BF16),
            pltpu.VMEM((planes, rows, D), BF16),
            pltpu.SemaphoreType.DMA((2, parts)),
            pltpu.SemaphoreType.DMA((count,)),
            pltpu.SemaphoreType.DMA((count,)),
        ]

    def remote(self, slot, source, target, to):
        return pltpu.make_async_remote_copy(
            src_ref=source, dst_ref=target, send_sem=self.send.at[slot], recv_sem=self.recv.at[slot],
            device_id=to, device_id_type=MESH,
        )

    def rows(self, part):
        return pl.ds(self.offsets[part], self.offsets[part + 1] - self.offsets[part])

    def cell(self, a, b):
        return a * self.place.step_a + b * self.place.step_b

    def core_copy(self, k, part):
        place = self.place
        group = pl.ds(place.run(place.plane(k), 1 - place.core), self.cells)
        return self.remote(
            k * self.parts + part, self.sources[part].at[group], self.land.at[k, :, self.rows(part)],
            place.other_core(),
        )

    def load_copy(self, t, part):
        place = self.place
        group = pl.ds(place.run(place.plane(self.order[t]), place.core), self.cells)
        return pltpu.make_async_copy(
            self.sources[part].at[group], self.ours.at[t % 2, :, self.rows(part)], self.load.at[t % 2, part]
        )

    def b_copy(self, k, a):
        place = self.place
        base = self.planes * self.parts
        return self.remote(
            base + 2 * k + a, self.land.at[k, self.cell(a, 1 - place.b)], self.got_b.at[k, a], place.across_b()
        )

    def a_copy(self, k):
        place = self.place
        base = self.planes * (self.parts + 2)
        return self.remote(
            base + k, self.land.at[k, self.cell(1 - place.a, place.b)], self.got_a.at[k], place.across_a()
        )

    def z_copy(self, k):
        place = self.place
        base = self.planes * (self.parts + 3)
        return self.remote(
            base + k, self.land.at[k, self.cell(place.a, place.b)], self.got_z.at[k], place.along_z(k)
        )

    def start(self, part):
        for k in self.order:
            self.core_copy(k, part).start()

    def start_one(self, t):
        self.core_copy(self.order[t], 0).start()

    def load_first(self):
        for part in range(self.parts):
            self.load_copy(0, part).start()

    def arrive_core(self, t):
        k = self.order[t]
        if t + 1 < self.planes:
            for part in range(self.parts):
                self.load_copy(t + 1, part).start()
        for part in range(self.parts):
            self.load_copy(t, part).wait()
            self.core_copy(k, part).wait_recv()

        def add(cell, _):
            self.land[k, cell] = self.land[k, cell] + self.ours[t % 2, cell]
            return 0

        lax.fori_loop(0, self.cells, add, 0)
        for a in range(self.side):
            self.b_copy(k, a).start()

    def arrive_b(self, t):
        k = self.order[t]
        for a in range(self.side):
            self.b_copy(k, a).wait_recv()
            at = self.cell(a, self.place.b)
            self.land[k, at] = self.land[k, at] + self.got_b[k, a]
        self.a_copy(k).start()

    def arrive_a(self, t):
        k = self.order[t]
        self.a_copy(k).wait_recv()
        at = self.cell(self.place.a, self.place.b)
        if k:
            self.land[k, at] = self.land[k, at] + self.got_a[k]
            self.z_copy(k).start()
        else:
            self.mine[...] = self.land[k, at].astype(F32) + self.got_a[k].astype(F32)

    def finish(self):
        for k in range(1, self.planes):
            self.z_copy(k).wait_recv()
            self.mine[...] += self.got_z[k].astype(F32)
        for k in range(self.planes):
            for part in range(self.parts):
                self.core_copy(k, part).wait_send()
            for a in range(self.side):
                self.b_copy(k, a).wait_send()
            self.a_copy(k).wait_send()
            if k:
                self.z_copy(k).wait_send()


def own_blocks(place, wq, wo, wu, wd, small, b_up, own1, own2):
    index = place.run(place.z, place.core) + place.a * place.step_a + place.b * place.step_b

    def spread(size, first):
        lane = lax.broadcasted_iota(jnp.int32, (size, D), 1)
        return jnp.where(lane == first + lax.broadcasted_iota(jnp.int32, (size, D), 0), 1.0, 0.0).astype(BF16)

    per_row = D // UROWS
    vec1 = mm(small[...], spread(OROWS, index * OROWS), 1, 0)
    whole_row = jnp.broadcast_to(b_up[...].astype(F32), (8, UROWS))
    here = lax.broadcasted_iota(jnp.int32, (8, UROWS), 0) == index // per_row
    vec2 = mm(jnp.where(here, whole_row, 0.0).astype(BF16), spread(UROWS, index % per_row * UROWS), 1, 0)
    own1[...] = jnp.concatenate([wq[...].astype(F32), vec1], axis=0).astype(BF16)
    own2[0:UROWS, :] = wu[...]
    down = wd[...].astype(F32)
    rest = [down[:, c * D : (c + 1) * D] for c in range(CHUNKS)] + [wo[...].astype(F32), vec2]
    own2[UROWS:SECOND, :] = jnp.concatenate(rest, axis=0).astype(BF16)


def forward_kernel(planes, side, rows, *refs):
    if planes:
        wq, wo, wu, wd, small, b_up, *refs = refs
    else:
        first_ref, full2, *refs = refs
    hid_ref, emb_ref, seg_ref, packed_ref, mixed_ref, mid_ref, norm_ref, total_ref, vec_ref, w_qkv, w_out, *refs = refs
    if planes:
        full2, *refs = refs
    first, tail, bias_col, mask_q, mask_k, load, *refs = refs
    step = pl.program_id(0)
    begin = 2 * rows
    leave = begin + 7 * rows
    row, phase = (step - begin) // 7, (step - begin) % 7
    attending = (step >= begin) & (step < leave)
    tail_copy = pltpu.make_async_copy(full2.at[:, pl.ds(2 * UROWS, 32)], tail, load.at[0])

    if planes:
        own1, own2, send1, recv1, send2, recv2 = refs
        place = Place(planes, side)
        gather1 = Gather(place, own1, first, send1, recv1)
        gather2 = Gather(place, own2, full2, send2, recv2)

        @pl.when(step == 0)
        def _():
            own_blocks(place, wq, wo, wu, wd, small, b_up, own1, own2)
            place.greet()
            gather1.start_z(range(1, planes))
            gather1.start_ab()

        @pl.when(step == begin)
        def _():
            for which, kind, k in FIRST_SCHED:
                (gather1, gather2)[which].event(kind, k)

        for at, kind, k in SCHED:
            @pl.when(step == begin + at)
            def _(kind=kind, k=k):
                gather2.event(kind, k)

        @pl.when(step == begin + SCHED[-1][0])
        def _():
            tail_copy.start()
    else:
        @pl.when(step == 0)
        def _():
            tail_copy.start()
            c = pltpu.make_async_copy(first_ref, first, load.at[1])
            c.start()
            c.wait()

    @pl.when(step < begin)
    def _():
        scaled, _ = normalise(hid_ref[...].astype(F32) + emb_ref[...].astype(F32))
        mixed_ref[pl.ds(pl.multiple_of(step * TOKB, TOKB), TOKB), :] = scaled

    @pl.when(step == begin)
    def _():
        join_rows(first, 0, QROWS, w_qkv, BLOCKS // 2)
        vec_ref[0] = sum_rows(first, QROWS)
        bias_col[0:D] = column(vec_ref[0, 2:3, :])
        bias_col[D : 2 * D] = jnp.zeros((D, 1), F32)
        bias_col[2 * D : 3 * D] = column(vec_ref[0, 3:4, :])

    tokens = pl.ds(pl.multiple_of(row * ROW, ROW), ROW)

    @pl.when(attending & (phase == 0))
    def _():
        normed = (mixed_ref[tokens, :] * vec_ref[0, 0:1, :] + vec_ref[0, 1:2, :]).astype(BF16)
        packed_ref[...] = (mm(w_qkv[...], normed, 1, 1) + bias_col[...]).astype(BF16)
        query_side, key_side = mask_rows(seg_ref[0])
        mask_q[...] = query_side
        mask_k[...] = key_side

    @pl.when(attending & (phase >= 1))
    def _():
        base = pl.multiple_of((phase - 1) * 128, 128)
        ones_rows = jnp.where(lax.broadcasted_iota(jnp.int32, (HEAD, ROW), 0) == 0, 1.0, 0.0).astype(BF16)
        sides = []
        for h in range(2):
            at = base + HEAD * h
            high, low = scaled_query(packed_ref[pl.ds(at, HEAD), :])
            keys = packed_ref[pl.ds(D + at, HEAD), :]
            sides.append((
                jnp.concatenate([high, low, mask_q[...]], axis=0),
                jnp.concatenate([keys, keys, mask_k[...]], axis=0),
                jnp.concatenate([packed_ref[pl.ds(2 * D + at, HEAD), :], ones_rows], axis=0),
            ))
        all_scores = [mm(sides[h][1], sides[h][0], 0, 0) for h in range(2)]
        mixed = []
        for h in range(2):
            scores = all_scores[h]
            top = jnp.max(scores, axis=0, keepdims=True)
            weights = jnp.exp2(scores - top).astype(BF16)
            summed = mm(sides[h][2], weights, 1, 0)
            total = summed[HEAD : HEAD + 1, :]
            mixed.append(summed[:HEAD, :] / total)
            total_ref[0, h : h + 1, :] = top + jnp.log2(total)
        mixed_ref[tokens, pl.ds(base, 128)] = jnp.concatenate(mixed, axis=0).T

    @pl.when(step == leave)
    def _():
        tail_copy.wait()
        join_rows(tail, 0, OROWS, w_out, BLOCKS // 2)
        vec_ref[1] = sum_rows(tail, OROWS)

    @pl.when(step >= leave)
    def _():
        half = pl.ds(pl.multiple_of((step - leave) * TOKB, TOKB), TOKB)
        entered = hid_ref[...].astype(F32) + emb_ref[...].astype(F32)
        middle = entered + mm(mixed_ref[half, :].astype(BF16), w_out[...], 1, 1) + vec_ref[0, 4:5, :]
        scaled, _ = normalise(middle)
        mid_ref[...] = middle
        norm_ref[...] = (scaled * vec_ref[0, 5:6, :] + vec_ref[0, 6:7, :]).astype(BF16)


def forward(planes, side, weights, hidden, embed, segment):
    n = hidden.shape[0]
    rows = n // ROW
    begin = 2 * rows
    leave_at = begin + 7 * rows
    one = pl.Buffered(1)
    hbm = pl.BlockSpec(memory_space=pl.ANY)

    def row(s):
        return jnp.clip((s - begin) // 7, 0, rows - 1)

    def entry(s):
        return (jnp.where(s < leave_at, jnp.minimum(s, begin - 1), s - leave_at), 0)

    def leave(s):
        return (jnp.maximum(s - leave_at, 0), 0)

    def pair(s):
        return jnp.where(s < leave_at, jnp.maximum((s - begin) % 7 - 1, 0) * (s >= begin), 5)

    entering = pl.BlockSpec((TOKB, D), entry)
    leaving = pl.BlockSpec((TOKB, D), leave)
    out_specs = [
        pl.BlockSpec((3 * D, ROW), lambda s: (0, row(s))),
        pl.BlockSpec((n, D), lambda s: (0, 0), pipeline_mode=one),
        leaving,
        leaving,
        pl.BlockSpec((1, 8, ROW), lambda s: (pair(s), 0, row(s))),
        pl.BlockSpec((2, 8, D), lambda s: (0, 0, 0)),
        pl.BlockSpec((3 * D, D), lambda s: (0, 0), pipeline_mode=one),
        pl.BlockSpec((D, D), lambda s: (0, 0), pipeline_mode=one),
    ]
    out_shape = [
        jax.ShapeDtypeStruct((3 * D, n), BF16),
        jax.ShapeDtypeStruct((n, D), F32),
        jax.ShapeDtypeStruct((n, D), F32),
        jax.ShapeDtypeStruct((n, D), BF16),
        jax.ShapeDtypeStruct((HEADS // 2, 8, n), F32),
        jax.ShapeDtypeStruct((2, 8, D), F32),
        jax.ShapeDtypeStruct((3 * D, D), BF16),
        jax.ShapeDtypeStruct((D, D), BF16),
    ]
    scratch = [
        pltpu.VMEM((BLOCKS, FIRST, D), BF16),
        pltpu.VMEM((BLOCKS, 32, D), BF16),
        pltpu.VMEM((3 * D, 1), F32),
        pltpu.VMEM((32, ROW), BF16),
        pltpu.VMEM((32, ROW), BF16),
        pltpu.SemaphoreType.DMA((2,)),
    ]
    params = dict(vmem_limit_bytes=56 * MIB)
    if planes:
        in_specs = [pl.BlockSpec(w.shape, lambda s: (0, 0), pipeline_mode=one) for w in weights]
        out_specs.append(hbm)
        out_shape.append(jax.ShapeDtypeStruct((BLOCKS, SECOND, D), BF16))
        scratch += [pltpu.VMEM((FIRST, D), BF16), pltpu.VMEM((SECOND, D), BF16)]
        scratch += [Gather.semaphores(planes)] * 4
        params.update(collective_id=1, has_side_effects=True)
    else:
        in_specs = [hbm, hbm]
    outs = pl.pallas_call(
        partial(forward_kernel, planes, side, rows),
        grid=(leave_at + begin,),
        in_specs=in_specs + [entering, entering, pl.BlockSpec((1, 1, ROW), lambda s: (row(s), 0, 0))],
        out_specs=out_specs,
        out_shape=out_shape,
        scratch_shapes=scratch,
        compiler_params=pltpu.CompilerParams(**params),
        name="attention_forward",
    )(*weights, hidden, embed, segment.reshape(rows, 1, ROW))
    return outs if planes else list(outs) + [weights[1]]


def feed_kernel(
    rows,
    up_ref, down_ref, vec_ref, norm_ref, mid_ref, cot_ref, seg_ref,
    out_ref, gmid_ref, gup_ref, gdown_ref, gvec_ref,
    w_down, result, back, live, active, pre, hold,
):
    step = pl.program_id(0)
    working = step < CHUNKS * rows
    j, i = step // rows, step % rows
    at = pl.ds(pl.multiple_of(i * ROW, ROW), ROW)

    @pl.when(step == 0)
    def _():
        gvec_ref[...] = jnp.zeros_like(gvec_ref)

    for chunk in range(CHUNKS):
        @pl.when(step == chunk * rows)
        def _():
            join_rows(down_ref, chunk % 2 * OROWS, OROWS, w_down, BLOCKS // 2)

    @pl.when(step < rows)
    def _():
        keep = column(jnp.where(seg_ref[0] >= 0, 1.0, 0.0))
        grad_result = cot_ref[...].astype(F32) * keep
        live[at, :] = grad_result.astype(BF16)
        gvec_ref[4:5, :] += jnp.sum(grad_result, axis=0, keepdims=True)

    @pl.when(working)
    def _():
        up = up_ref[...].reshape(D, D)
        down = w_down[...]
        x = mm(norm_ref[at, :], up, 1, 1) + vec_ref[1, pl.ds(j, 1), :]
        grad_act = mm(live[at, :], down, 1, 0)
        c0 = math.sqrt(2.0 / math.pi)
        c1 = 0.044715
        square = x * x
        th = jnp.tanh(x * (c0 + (c0 * c1) * square))
        half = 0.5 + 0.5 * th
        slope = half + (0.5 * x) * ((1.0 - th * th) * (c0 + (3 * c0 * c1) * square))
        activated = (x * half).astype(BF16)
        grad_pre = (grad_act * slope).astype(BF16)
        active[at, :] = activated
        pre[at, :] = grad_pre
        gvec_ref[pl.ds(j, 1), :] += jnp.sum(grad_pre.astype(F32), axis=0, keepdims=True)

        @pl.when(j == 0)
        def _():
            result[at, :] = mm(activated, down, 1, 1)
            back[at, :] = mm(grad_pre, up, 1, 0)

        @pl.when(j > 0)
        def _():
            result[at, :] += mm(activated, down, 1, 1)
            back[at, :] += mm(grad_pre, up, 1, 0)

    @pl.when(working & (i == rows - 1))
    def _():
        gup_ref[...] = mm(pre[...], norm_ref[...], 0, 0).astype(BF16)
        part_down = mm(live[...], active[...], 0, 0)

        @pl.when(j % 2 == 0)
        def _():
            hold[0] = part_down

        @pl.when(j % 2 == 1)
        def _():
            hold[1] = part_down

            def pack(d, _):
                own = pl.ds(pl.multiple_of(d * OROWS, 8), OROWS)
                gdown_ref[d] = jnp.concatenate([hold[0, own], hold[1, own]], axis=0).astype(BF16)
                return 0

            lax.fori_loop(0, BLOCKS, pack, 0)

    @pl.when(step >= CHUNKS * rows)
    def _():
        tokens = pl.ds(pl.multiple_of((step - CHUNKS * rows) * LAST, LAST), LAST)
        middle = mid_ref[...]
        out_ref[...] = (middle + (result[tokens, :] + vec_ref[0, 7:8, :])).astype(BF16)
        grad = back[tokens, :]
        scaled, inverse = normalise(middle)
        gvec_ref[5:6, :] += jnp.sum(grad * scaled, axis=0, keepdims=True)
        gvec_ref[6:7, :] += jnp.sum(grad, axis=0, keepdims=True)
        gmid_ref[...] = live[tokens, :].astype(F32) + norm_back(grad, scaled, inverse, vec_ref[0, 5:6, :])


def feed(second, vec, normed, middle, cotangent, segment):
    n = normed.shape[0]
    rows = n // ROW
    one = pl.Buffered(1)

    def chunk(s):
        return jnp.minimum(s // rows, CHUNKS - 1)

    def late(s):
        return (jnp.maximum(s - CHUNKS * rows, 0), 0)

    leaving = pl.BlockSpec((LAST, D), late)
    return pl.pallas_call(
        partial(feed_kernel, rows),
        grid=(CHUNKS * rows + n // LAST,),
        in_specs=[
            pl.BlockSpec((BLOCKS // CHUNKS, UROWS, D), lambda s: (chunk(s), 0, 0)),
            pl.BlockSpec((BLOCKS, 2 * OROWS, D), lambda s: (0, 2 + chunk(s) // 2, 0), pipeline_mode=one),
            pl.BlockSpec((2, 8, D), lambda s: (0, 0, 0)),
            pl.BlockSpec((n, D), lambda s: (0, 0), pipeline_mode=one),
            leaving,
            pl.BlockSpec((ROW, D), lambda s: (jnp.minimum(s, rows - 1), 0), pipeline_mode=one),
            pl.BlockSpec((1, 1, ROW), lambda s: (jnp.minimum(s, rows - 1), 0, 0)),
        ],
        out_specs=[
            leaving,
            leaving,
            pl.BlockSpec((D, D), lambda s: (chunk(s), 0)),
            pl.BlockSpec((BLOCKS, 2 * OROWS, D), lambda s: (0, chunk(s) // 2, 0), pipeline_mode=one),
            pl.BlockSpec((8, D), lambda s: (0, 0)),
        ],
        out_shape=[
            jax.ShapeDtypeStruct((n, D), BF16),
            jax.ShapeDtypeStruct((n, D), F32),
            jax.ShapeDtypeStruct((FF, D), BF16),
            jax.ShapeDtypeStruct((BLOCKS, UROWS, D), BF16),
            jax.ShapeDtypeStruct((8, D), F32),
        ],
        scratch_shapes=[
            pltpu.VMEM((D, D), BF16),
            pltpu.VMEM((n, D), F32),
            pltpu.VMEM((n, D), F32),
            pltpu.VMEM((n, D), BF16),
            pltpu.VMEM((n, D), BF16),
            pltpu.VMEM((n, D), BF16),
            pltpu.VMEM((2, D, D), F32),
        ],
        compiler_params=pltpu.CompilerParams(vmem_limit_bytes=60 * MIB),
        name="feed_forward",
    )(second, second, vec, normed, middle, cotangent, segment.reshape(rows, 1, ROW))


def three_parts(row):
    r = lax.broadcasted_iota(jnp.int32, (16, row.shape[1]), 0)
    a = row.astype(BF16).astype(F32)
    b = (row - a).astype(BF16).astype(F32)
    c = row - a - b
    return jnp.where(r == 0, -a, jnp.where(r == 1, -b, jnp.where(r == 2, -c, 0.0))).astype(BF16)


def backward_kernel(
    planes, side, rows,
    w_out, seg_ref, packed_q, packed_k, packed_v, mixed_ref, total_ref, gmid_ref, gvec_ref, gup_ref, gdown_ref,
    gpacked_ref, sums_ref, *rest,
):
    if planes:
        mine, mask_q, mask_k, grad_mixed, delta, sum_out, sum_bias, tail, *transfer = rest
    else:
        tail, mask_q, mask_k, grad_mixed, delta, sum_out, sum_bias = rest
    step = pl.program_id(0)
    entry = 2 * rows
    heads = step >= entry

    if planes:
        place = Place(planes, side)
        scatter = Scatter(place, (gup_ref, gdown_ref, tail), *transfer[:5], mine, *transfer[5:])

        @pl.when(step == 0)
        def _():
            place.greet()
            scatter.start(0)
            scatter.start(1)

        @pl.when(step == entry)
        def _():
            scatter.start(2)
            scatter.load_first()

        for at, t, act in BACK:
            @pl.when(step == entry + at)
            def _(t=t, act=act):
                getattr(scatter, act)(t)

    @pl.when(step == 0)
    def _():
        sum_out[...] = jnp.zeros_like(sum_out)
        sum_bias[...] = jnp.zeros_like(sum_bias)

    @pl.when(step < entry)
    def _():
        at = pl.ds(pl.multiple_of(step * TOKB, TOKB), TOKB)
        mixed = mixed_ref[...]
        branch = gmid_ref[...].astype(BF16)
        sum_bias[0:1, :] += jnp.sum(branch.astype(F32), axis=0, keepdims=True)
        sum_out[...] += mm(branch, mixed.astype(BF16), 0, 0)
        grad = mm(branch, w_out[...], 1, 0).astype(BF16).astype(F32)
        grad_mixed[:, at] = grad.T.astype(BF16)
        inner = (grad * mixed).T
        delta[:, at] = jnp.concatenate(
            [jnp.sum(inner[HEAD * h : HEAD * (h + 1)], axis=0, keepdims=True) for h in range(HEADS)]
            + [jnp.zeros((16 - HEADS, TOKB), F32)],
            axis=0,
        )

    @pl.when(step == entry - 1)
    def _():
        r = lax.broadcasted_iota(jnp.int32, (8, D), 0)
        vectors = jnp.where(r == 7, sum_bias[0:1, :], gvec_ref[...])

        def pack(d, _):
            at = pl.ds(pl.multiple_of(d * OROWS, 8), OROWS)
            tail[d] = jnp.concatenate([sum_out[at, :], vectors], axis=0).astype(BF16)
            return 0

        lax.fori_loop(0, BLOCKS, pack, 0)

    row, pair = (step - entry) // 6, (step - entry) % 6

    @pl.when(heads & (pair == 0))
    def _():
        query_side, key_side = mask_rows(seg_ref[0])
        mask_q[...] = query_side
        mask_k[...] = key_side

    @pl.when(heads)
    def _():
        tokens = pl.ds(pl.multiple_of(row * ROW, ROW), ROW)
        r = lax.broadcasted_iota(jnp.int32, (16, ROW), 0)
        ones_rows = jnp.where(r < 3, 1.0, 0.0).astype(BF16)
        base = pl.multiple_of(pair * 128, 128)
        column_sums = []
        for h in range(2):
            at_rows = slice(HEAD * h, HEAD * (h + 1))
            queries, keys, values = packed_q[at_rows, :], packed_k[at_rows, :], packed_v[at_rows, :]
            grad = grad_mixed[pl.ds(base + HEAD * h, HEAD), tokens]
            high, low = scaled_query(queries)
            wide_q = jnp.concatenate([high, low, mask_q[...], three_parts(total_ref[0, h : h + 1, :])], axis=0)
            wide_k = jnp.concatenate([keys, keys, mask_k[...], ones_rows], axis=0)
            wide_g = jnp.concatenate([grad, three_parts(delta[pl.ds(2 * pair + h, 1), tokens])], axis=0)
            wide_v = jnp.concatenate([values, ones_rows], axis=0)
            grad_v = jnp.zeros((HEAD, ROW), F32)
            grad_k = jnp.zeros((HEAD, ROW), F32)
            grad_q = []
            for half in range(2):
                at = slice(half * (ROW // 2), (half + 1) * (ROW // 2))
                probs = jnp.exp2(mm(wide_q[:, at], wide_k, 0, 0))
                grad_probs = mm(wide_g[:, at], wide_v, 0, 0)
                grad_scores = (probs * grad_probs).astype(BF16)
                grad_v = grad_v + mm(grad[:, at], probs.astype(BF16), 1, 0)
                grad_k = grad_k + mm(queries[:, at], grad_scores, 1, 0)
                grad_q.append(mm(keys, grad_scores, 1, 1))
            grads = (
                (jnp.concatenate(grad_q, axis=1) * 0.125).astype(BF16),
                (grad_k * 0.125).astype(BF16),
                grad_v.astype(BF16),
            )
            for part in range(3):
                gpacked_ref[pl.ds(part * D + base + HEAD * h, HEAD), :] = grads[part]
            column_sums.append([jnp.sum(g.astype(F32), axis=1, keepdims=True) for g in grads])
        for part in range(3):
            both = jnp.concatenate([column_sums[0][part], column_sums[1][part]], axis=0)
            at = pl.ds(part * D + base, 128)

            @pl.when(row == 0)
            def _():
                sums_ref[at, :] = both

            @pl.when(row > 0)
            def _():
                sums_ref[at, :] += both

    if planes:
        @pl.when(step == entry + 6 * rows - 1)
        def _():
            scatter.finish()


def backward(planes, side, w_out, segment, packed, mixed, totals, gmid, gvec, gup, gdown):
    n = mixed.shape[0]
    rows = n // ROW
    entry = 2 * rows
    one = pl.Buffered(1)
    hbm = pl.BlockSpec(memory_space=pl.ANY)

    def early(s):
        return (jnp.minimum(s, entry - 1), 0)

    def row(s):
        return jnp.maximum(s - entry, 0) // 6

    def pair(s):
        return jnp.maximum(s - entry, 0) % 6

    def heads(part):
        return pl.BlockSpec((128, ROW), lambda s: (6 * part + pair(s), row(s)))

    out_specs = [
        pl.BlockSpec((3 * D, ROW), lambda s: (0, row(s))),
        pl.BlockSpec((3 * D, 1), lambda s: (0, 0), pipeline_mode=one),
    ]
    out_shape = [jax.ShapeDtypeStruct((3 * D, n), BF16), jax.ShapeDtypeStruct((3 * D, 1), F32)]
    scratch = [
        pltpu.VMEM((32, ROW), BF16),
        pltpu.VMEM((32, ROW), BF16),
        pltpu.VMEM((D, n), BF16),
        pltpu.VMEM((16, n), F32),
        pltpu.VMEM((D, D), F32),
        pltpu.VMEM((8, D), F32),
    ]
    params = dict(vmem_limit_bytes=56 * MIB)
    if planes:
        rows1 = 2 * UROWS + 32
        out_specs.append(pl.BlockSpec((rows1, D), lambda s: (0, 0), pipeline_mode=one))
        out_shape.append(jax.ShapeDtypeStruct((rows1, D), F32))
        scratch.append(pltpu.VMEM((BLOCKS, 32, D), BF16))
        scratch += Scatter.scratch(planes, side, 3, rows1)
        params.update(collective_id=2, has_side_effects=True)
    else:
        out_specs.append(pl.BlockSpec((BLOCKS, 32, D), lambda s: (0, 0, 0), pipeline_mode=one))
        out_shape.append(jax.ShapeDtypeStruct((BLOCKS, 32, D), BF16))
    return pl.pallas_call(
        partial(backward_kernel, planes, side, rows),
        grid=(entry + 6 * rows,),
        in_specs=[
            pl.BlockSpec((D, D), lambda s: (0, 0), pipeline_mode=one),
            pl.BlockSpec((1, 1, ROW), lambda s: (row(s), 0, 0)),
            heads(0),
            heads(1),
            heads(2),
            pl.BlockSpec((TOKB, D), early),
            pl.BlockSpec((1, 8, ROW), lambda s: (pair(s), 0, row(s))),
            pl.BlockSpec((TOKB, D), early),
            pl.BlockSpec((8, D), lambda s: (0, 0)),
            hbm,
            hbm,
        ],
        out_specs=out_specs,
        out_shape=out_shape,
        scratch_shapes=scratch,
        compiler_params=pltpu.CompilerParams(**params),
        name="attention_backward",
    )(w_out, segment.reshape(rows, 1, ROW), packed, packed, packed, mixed, totals, gmid, gvec, gup, gdown)


def enter_kernel(
    planes, side, blocks,
    w_hbm, vec_ref, hid_ref, emb_ref, gmid_ref, grad_hbm, sums_ref,
    ghid_ref, out_ref, *rest,
):
    if planes:
        mine, (scaled_all, w_qkv, grad_packed, totals, load, packed, *transfer) = out_ref, rest
    else:
        packed, (scaled_all, w_qkv, grad_packed, totals, load) = out_ref, rest
    step = pl.program_id(0)
    chunks = 4
    size = 3 * D // chunks
    begin, late = blocks, blocks + chunks
    loads = [
        pltpu.make_async_copy(grad_hbm, grad_packed, load.at[0]),
        pltpu.make_async_copy(w_hbm, w_qkv, load.at[1]),
    ]

    if planes:
        place = Place(planes, side)
        rider = Rider(place, *transfer[:4])
        scatter = Scatter(place, (packed,), *transfer[4:9], mine, *transfer[9:])

    @pl.when(step == 0)
    def _():
        for c in loads:
            c.start()
        totals[...] = jnp.zeros_like(totals)
        if planes:
            place.greet()

    def entering():
        return normalise(hid_ref[...].astype(F32) + emb_ref[...].astype(F32))

    @pl.when(step < begin)
    def _():
        scaled, _ = entering()
        scaled_all[pl.ds(pl.multiple_of(step * TOKB, TOKB), TOKB), :] = scaled.astype(BF16)

    @pl.when(step == begin)
    def _():
        for c in loads:
            c.wait()

    if planes:
        for at, t, act in ENTER:
            @pl.when(step == begin + at)
            def _(t=t, act=act):
                getattr(scatter, act)(t)
                if t == planes - 1:
                    rider.arrive(("arrive_core", "arrive_b", "arrive_a").index(act))

    @pl.when((step >= begin) & (step < late))
    def _():
        t = step - begin
        chunk = place.plane(t + 1) if planes else t
        at = pl.ds(pl.multiple_of(chunk * size, size), size)
        product = mm(grad_packed[at, :], scaled_all[...], 1, 0)
        weight = w_qkv[at, :].astype(F32)
        sums = sums_ref[at, :]
        totals[0:1, :] += jnp.sum(weight * product, axis=0, keepdims=True)
        totals[1:2, :] += jnp.sum(weight * sums, axis=0, keepdims=True)
        grad_w = product * vec_ref[0, 0:1, :] + sums * vec_ref[0, 1:2, :]
        count = BLOCKS // chunks
        for i in range(count):
            rows = [grad_w[i * QROWS : (i + 1) * QROWS], jnp.zeros((8, D), F32)]
            packed[chunk * count + i] = jnp.concatenate(rows, axis=0).astype(BF16)

    if planes:
        for t in range(planes):
            @pl.when(step == begin + t)
            def _(t=t):
                scatter.start_one(t)
                if t == 0:
                    scatter.load_first()

    @pl.when(step == late - 1)
    def _():
        ends = [jnp.broadcast_to(sums_ref[at : at + D, :], (D, 128)).T[0:1, :] for at in (0, 2 * D)]
        vectors = jnp.concatenate([totals[0:2, :]] + ends + [jnp.zeros((4, D), F32)], axis=0)
        if planes:
            rider.stages[0] = vectors
            rider.start()
        else:
            kept = packed[0, QROWS - 8 : QROWS + 8, :].astype(F32)[:8]
            packed[0, QROWS - 8 : QROWS + 8, :] = jnp.concatenate([kept, vectors], axis=0).astype(BF16)

    @pl.when(step >= late)
    def _():
        at = pl.ds(pl.multiple_of((step - late) * TOKB, TOKB), TOKB)
        scaled, inverse = entering()
        grad = mm(grad_packed[:, at], w_qkv[...], 0, 0)
        ghid_ref[...] = (gmid_ref[...] + norm_back(grad, scaled, inverse, vec_ref[0, 0:1, :])).astype(BF16)

    if planes:
        @pl.when(step == late + blocks - 1)
        def _():
            for t, act in ENTER_LAST:
                getattr(scatter, act)(t)
                if t == planes - 1:
                    rider.arrive(("arrive_core", "arrive_b", "arrive_a").index(act))
            scatter.finish()
            mine[QROWS : QROWS + 8, :] = rider.finish()


def enter(planes, side, w_qkv, vec, hidden, embed, gmid, gpacked, sums):
    n = hidden.shape[0]
    blocks = n // TOKB
    late_at = blocks + 4
    one = pl.Buffered(1)
    hbm = pl.BlockSpec(memory_space=pl.ANY)

    def late(s):
        return (jnp.maximum(s - late_at, 0), 0)

    tokens = pl.BlockSpec((TOKB, D), lambda s: (jnp.where(s < late_at, jnp.minimum(s, blocks - 1), s - late_at), 0))
    out_specs = [pl.BlockSpec((TOKB, D), late)]
    out_shape = [jax.ShapeDtypeStruct((n, D), BF16)]
    scratch = [
        pltpu.VMEM((n, D), BF16),
        pltpu.VMEM((3 * D, D), BF16),
        pltpu.VMEM((3 * D, n), BF16),
        pltpu.VMEM((8, D), F32),
        pltpu.SemaphoreType.DMA((2,)),
    ]
    params = dict(vmem_limit_bytes=56 * MIB)
    if planes:
        out_specs.append(pl.BlockSpec((FIRST, D), lambda s: (0, 0), pipeline_mode=one))
        out_shape.append(jax.ShapeDtypeStruct((FIRST, D), F32))
        scratch.append(pltpu.VMEM((BLOCKS, FIRST, D), BF16))
        scratch += Rider.scratch(planes) + Scatter.scratch(planes, side, 1, FIRST)
        params.update(collective_id=3, has_side_effects=True)
    else:
        out_specs.append(pl.BlockSpec((BLOCKS, FIRST, D), lambda s: (0, 0, 0), pipeline_mode=one))
        out_shape.append(jax.ShapeDtypeStruct((BLOCKS, FIRST, D), BF16))
    return pl.pallas_call(
        partial(enter_kernel, planes, side, blocks),
        grid=(late_at + blocks,),
        in_specs=[
            hbm,
            pl.BlockSpec((2, 8, D), lambda s: (0, 0, 0)),
            tokens,
            tokens,
            pl.BlockSpec((TOKB, D), late),
            hbm,
            pl.BlockSpec((3 * D, 1), lambda s: (0, 0), pipeline_mode=one),
        ],
        out_specs=out_specs,
        out_shape=out_shape,
        scratch_shapes=scratch,
        compiler_params=pltpu.CompilerParams(**params),
        name="projection_backward",
    )(w_qkv, vec, hidden, embed, gmid, gpacked, sums)


def body(
    planes, side, devices,
    hidden, time_embed, segment_ids,
    ln1_gain, ln1_bias, w_qkv, b_query, b_value, w_out, b_out, ln2_gain, ln2_bias, w_up, b_up, w_down, b_down,
    cotangent,
):
    index = lax.axis_index("dp") * lax.axis_size("fsdp") + lax.axis_index("fsdp")
    axes = ("dp", "fsdp")
    small = (ln1_gain, ln1_bias, b_query, b_value, b_out, ln2_gain, ln2_bias, b_down)
    if planes:
        weights = (w_qkv.T, w_out.T, w_up.T, w_down.T, jnp.stack(small), b_up[None, :])
    else:
        def whole(a, dim):
            return lax.all_gather(a, axes, axis=dim, tiled=True)

        def only_first(rows):
            return jnp.concatenate([rows[None], jnp.zeros((BLOCKS - 1,) + rows.shape, BF16)], axis=0)

        vec1 = jnp.stack([whole(v, 0) for v in small])
        vec2 = jnp.concatenate([whole(b_up, 0).reshape(CHUNKS, D), jnp.zeros((8 - CHUNKS, D), BF16)], axis=0)
        down_rows = whole(w_down, 1).T.reshape(BLOCKS, OROWS, CHUNKS, D).transpose(0, 2, 1, 3)
        first = jnp.concatenate([whole(w_qkv, 1).T.reshape(BLOCKS, QROWS, D), only_first(vec1)], axis=1)
        second = jnp.concatenate(
            [
                whole(w_up, 1).T.reshape(BLOCKS, UROWS, D),
                down_rows.reshape(BLOCKS, UROWS, D),
                whole(w_out, 1).T.reshape(BLOCKS, OROWS, D),
                only_first(vec2),
            ],
            axis=1,
        )
        weights = (first, second)
    packed, mixed, middle, normed, totals, vec, full_qkv, full_out, second = forward(
        planes, side, weights, hidden, time_embed, segment_ids
    )
    output, gmid, gup, gdown, gvec = feed(second, vec, normed, middle, cotangent, segment_ids)
    gup = gup.reshape(BLOCKS, UROWS, D)
    gpacked, sums, late = backward(
        planes, side, full_out, segment_ids, packed, mixed, totals, gmid, gvec, gup, gdown
    )
    ghid, last = enter(planes, side, full_qkv, vec, hidden, time_embed, gmid, gpacked, sums)
    if planes:
        part_up = late[:UROWS]
        part_down = late[UROWS : 2 * UROWS].reshape(CHUNKS, OROWS, D).transpose(1, 0, 2).reshape(OROWS, FF)
        part_out = late[2 * UROWS : 2 * UROWS + OROWS]
        part_qkv = last[:QROWS]
        vectors = jnp.concatenate([late[2 * UROWS + OROWS :], last[QROWS:]], axis=0)
        short = lax.dynamic_slice(vectors, (0, index * OROWS), (16, OROWS))
        part_bup = lax.dynamic_slice(vectors[:CHUNKS].reshape(-1), (index * UROWS,), (UROWS,))
    else:
        def shared(a, dim):
            return lax.psum_scatter(a.astype(F32), axes, scatter_dimension=dim, tiled=True)

        part_up = shared(gup.reshape(FF, D), 0)
        part_down = shared(gdown.reshape(BLOCKS, CHUNKS, OROWS, D).transpose(0, 2, 1, 3).reshape(D, FF), 0)
        part_out = shared(late[:, :OROWS].reshape(D, D), 0)
        part_qkv = shared(last[:, :QROWS].reshape(3 * D, D), 0)
        vectors = jnp.concatenate([late[0, OROWS:], last[0, QROWS:]], axis=0)
        short = shared(vectors, 1)
        part_bup = shared(vectors[:CHUNKS].reshape(-1), 0)
    return (
        output, ghid,
        short[8], short[9], part_qkv.T, short[10], short[11], part_out.T, short[7],
        short[5], short[6], part_up.T, part_bup, part_down.T, short[4],
    )


def solution(mesh):
    groups, cells = mesh.shape["dp"], mesh.shape["fsdp"]
    side = math.isqrt(cells)
    own_transfers = groups * cells == BLOCKS and side == 2 and cells == 4 and groups % 2 == 0
    split = ("dp", "fsdp")
    rows, flat, cols = P(split, None), P(split), P(None, split)
    return jax.shard_map(
        partial(body, groups // 2 if own_transfers else 0, side, groups * cells),
        mesh=mesh,
        in_specs=(
            rows, rows, flat, flat, flat, cols, flat, flat, cols, flat, flat, flat, cols, flat, cols, flat, rows,
        ),
        out_specs=(
            rows, rows, flat, flat, cols, flat, flat, cols, flat, flat, flat, cols, flat, cols, flat,
        ),
        check_vma=False,
    )
```

```python
from functools import partial
import math

import jax
import jax.numpy as jnp
from jax import lax
from jax.experimental import pallas as pl
from jax.experimental.pallas import tpu as pltpu
from jax.sharding import PartitionSpec as P

D = 768
HEADS = 12
HEAD = 64
FF = 3072
ROW = 1024
BLOCKS = 32
QROWS = 3 * D // BLOCKS
OROWS = D // BLOCKS
UROWS = FF // BLOCKS
CHUNKS = FF // D
FIRST = QROWS + 8
SECOND = 2 * UROWS + OROWS + 8
TOKB = 512
MIB = 2**20
MESH = pl.DeviceIdType.MESH
F32 = jnp.float32
BF16 = jnp.bfloat16
LOG2E = math.log2(math.e)
EPS = 1e-05
FIRST_SCHED = (
    (0, "z", 1), (0, "a", 0), (0, "z", 2), (0, "a", 1), (0, "z", 3), (1, "s", 1), (1, "s", 2), (0, "b", 0), (0, "a", 2),
    (0, "b", 1), (0, "a", 3), (1, "o", 0), (0, "b", 2), (0, "b", 3), (0, "end", 0),
)
SCHED = (
    (0, "z", 1), (0, "s", 3), (1, "a", 0), (2, "a", 1), (2, "z", 2), (3, "b", 0), (5, "a", 2), (6, "z", 3), (6, "b", 1),
    (9, "a", 3), (9, "b", 2), (12, "b", 3), (13, "end", 0),
)
BACK = (
    (1, 0, "arrive_core"), (2, 1, "arrive_core"), (3, 0, "arrive_b"), (4, 2, "arrive_core"), (5, 1, "arrive_b"),
    (5, 0, "arrive_a"), (6, 3, "arrive_core"), (7, 2, "arrive_b"), (8, 1, "arrive_a"), (9, 3, "arrive_b"),
    (9, 2, "arrive_a"), (11, 3, "arrive_a"),
)
ENTER = (
    (2, 0, "arrive_core"), (3, 1, "arrive_core"), (4, 0, "arrive_b"), (4, 2, "arrive_core"), (5, 1, "arrive_b"),
    (5, 3, "arrive_core"), (6, 0, "arrive_a"), (6, 2, "arrive_b"), (7, 1, "arrive_a"), (7, 3, "arrive_b"),
)
ENTER_LAST = ((2, "arrive_a"), (3, "arrive_a"))


def mm(a, b, ca, cb):
    return lax.dot_general(a, b, (((ca,), (cb,)), ((), ())), preferred_element_type=F32)


def normalise(values):
    centred = values - jnp.mean(values, axis=-1, keepdims=True)
    inverse = lax.rsqrt(jnp.mean(centred * centred, axis=-1, keepdims=True) + EPS)
    return centred * inverse, inverse


def norm_back(grad, scaled, inverse, gain):
    u = grad * gain
    return inverse * (
        u
        - jnp.mean(u, axis=-1, keepdims=True)
        - scaled * jnp.mean(u * scaled, axis=-1, keepdims=True)
    )


def column(row):
    return jnp.broadcast_to(row, (128, row.shape[1])).T[:, :1]


def join_rows(source, start, rows, target, pairs):
    low = start // 16 * 16
    high = -(-(start + rows) // 16) * 16

    def step(p, _):
        parts = [
            source[2 * p + i, low:high, :].astype(F32)[start - low : start - low + rows]
            for i in range(2)
        ]
        at = pl.multiple_of(2 * rows * p, 2 * rows)
        target[pl.ds(at, 2 * rows), :] = jnp.concatenate(parts, axis=0).astype(BF16)
        return 0

    lax.fori_loop(0, pairs, step, 0)


def sum_rows(source, start):
    low = start // 16 * 16

    def step(d, total):
        return total + source[d, low : low + 16, :].astype(F32)[start - low : start - low + 8]

    return lax.fori_loop(0, BLOCKS, step, jnp.zeros((8, D), F32))


def mask_rows(segment):
    r = lax.broadcasted_iota(jnp.int32, (32, ROW), 0)
    hit = r == segment + 1
    query_side = jnp.where(hit, 1.0, 0.0).astype(BF16)
    key_side = jnp.where(hit | (r >= 17), 0.0, -1e30).astype(BF16)
    return query_side, key_side


def scaled_query(queries):
    wide = queries.astype(F32) * (LOG2E / 8)
    high = wide.astype(BF16)
    low = (wide - high.astype(F32)).astype(BF16)
    return high, low


class Place:
    def __init__(self, planes, side):
        self.planes, self.side = planes, side
        group, cell = lax.axis_index("dp"), lax.axis_index("fsdp")
        self.z, self.core = group // 2, group % 2
        y, x = cell // side, cell % side
        self.step_a = 1 + self.core * (side - 1)
        self.step_b = side - self.core * (side - 1)
        self.a = x + self.core * (y - x)
        self.b = y + self.core * (x - y)

    def plane(self, k):
        return lax.rem(self.z + k + self.planes, self.planes)

    def paired(self, k):
        plane, bit = self.z, 1
        while bit <= k:
            if k & bit:
                plane = plane + bit - 2 * bit * (self.z // bit % 2)
            bit *= 2
        return plane

    def at(self, z, core, a, b):
        return (z * 2 + core, a * self.step_a + b * self.step_b)

    def block(self, z, a, b):
        return (z * 2 + self.core) * (self.side * self.side) + a * self.step_a + b * self.step_b

    def run(self, z, core):
        return (z * 2 + core) * (self.side * self.side)

    def across_a(self):
        return self.at(self.z, self.core, 1 - self.a, self.b)

    def across_b(self):
        return self.at(self.z, self.core, self.a, 1 - self.b)

    def other_core(self):
        return (self.z * 2 + 1 - self.core, self.a * self.step_a + self.b * self.step_b)

    def along_z(self, k):
        return self.at(self.plane(k), self.core, self.a, self.b)

    def greet(self):
        barrier = pltpu.get_barrier_semaphore()
        peers = [self.along_z(k) for k in range(1, self.planes)]
        peers += [self.across_a(), self.across_b(), self.other_core()]
        for peer in peers:
            pl.semaphore_signal(barrier, inc=1, device_id=peer, device_id_type=MESH)
        pl.semaphore_wait(barrier, len(peers))


class Gather:
    def __init__(self, place, own, full, send, recv):
        self.place, self.own, self.full, self.send, self.recv = place, own, full, send, recv
        self.planes = place.planes

    @staticmethod
    def semaphores(planes):
        return pltpu.SemaphoreType.DMA((5 * planes + 1,))

    def copy(self, kind, k):
        place, full = self.place, self.full
        plane = place.paired(k)
        column = full.at[place.block(plane, place.a, place.b)]
        if kind == "z":
            source, target = self.own, full.at[place.block(place.z, place.a, place.b)]
            to = place.at(plane, place.core, place.a, place.b)
        elif kind == "a" or kind == "b":
            source, target = (column if k else self.own), column
            to = place.across_a() if kind == "a" else place.across_b()
        elif kind == "d":
            source = target = full.at[place.block(plane, 1 - place.a, place.b)]
            to = place.across_b()
        else:
            cells = place.side * place.side
            source = target = full.at[pl.ds(place.run(plane, place.core), cells)]
            to = place.other_core()
        i = "zabdc".index(kind) * self.planes + k
        return pltpu.make_async_remote_copy(
            src_ref=source, dst_ref=target, send_sem=self.send.at[i], recv_sem=self.recv.at[i],
            device_id=to, device_id_type=MESH,
        )

    def keep(self):
        place = self.place
        return pltpu.make_async_copy(
            self.own, self.full.at[place.block(place.z, place.a, place.b)], self.send.at[5 * self.planes]
        )

    def start_z(self, ways):
        for k in ways:
            self.copy("z", k).start()

    def start_ab(self):
        self.keep().start()
        self.copy("a", 0).start()
        self.copy("b", 0).start()

    def event(self, kind, k):
        if kind == "s":
            self.start_z((k,))
        elif kind == "o":
            self.start_ab()
        elif kind == "z":
            self.copy("z", k).wait_recv()
            self.copy("a", k).start()
            self.copy("b", k).start()
        elif kind == "a":
            self.copy("a", k).wait_recv()
            self.copy("d", k).start()
        elif kind == "b":
            self.copy("b", k).wait_recv()
            self.copy("d", k).wait_recv()
            if k == 0:
                self.keep().wait()
            self.copy("c", k).start()
        else:
            for k in range(self.planes):
                self.copy("c", k).wait_recv()
            for k in range(self.planes):
                for kind in "zabdc" if k else "abdc":
                    self.copy(kind, k).wait_send()


class Rider:
    def __init__(self, place, stages, got, send, recv):
        self.place, self.stages, self.got, self.send, self.recv = place, stages, got, send, recv

    @staticmethod
    def scratch(planes):
        count = 3 + planes
        return [
            pltpu.VMEM((4, 8, D), F32),
            pltpu.VMEM((count, 8, D), F32),
            pltpu.SemaphoreType.DMA((count,)),
            pltpu.SemaphoreType.DMA((count,)),
        ]

    def copy(self, i):
        place = self.place
        to = (place.other_core, place.across_b, place.across_a)[i]() if i < 3 else place.along_z(i - 3)
        return pltpu.make_async_remote_copy(
            src_ref=self.stages.at[min(i, 3)], dst_ref=self.got.at[i], send_sem=self.send.at[i], recv_sem=self.recv.at[i],
            device_id=to, device_id_type=MESH,
        )

    def start(self):
        self.copy(0).start()

    def arrive(self, i):
        self.copy(i).wait_recv()
        self.stages[i + 1] = self.stages[i] + self.got[i]
        if i < 2:
            self.copy(i + 1).start()
        else:
            for k in range(1, self.place.planes):
                self.copy(3 + k).start()

    def finish(self):
        total = self.stages[3]
        for k in range(1, self.place.planes):
            self.copy(3 + k).wait_recv()
            total = total + self.got[3 + k]
        for i in (0, 1, 2):
            self.copy(i).wait_send()
        for k in range(1, self.place.planes):
            self.copy(3 + k).wait_send()
        return total


class Scatter:
    def __init__(self, place, sources, land, ours, got_b, got_a, got_z, mine, load, send, recv):
        self.place, self.sources, self.land, self.ours = place, sources, land, ours
        self.got_b, self.got_a, self.got_z, self.mine = got_b, got_a, got_z, mine
        self.load, self.send, self.recv = load, send, recv
        self.planes, self.side = place.planes, place.side
        self.cells = place.side * place.side
        self.parts = len(sources)
        self.order = list(range(1, self.planes)) + [0]
        self.offsets = [sum(s.shape[1] for s in sources[:i]) for i in range(self.parts + 1)]

    @staticmethod
    def scratch(planes, side, parts, rows):
        cells = side * side
        count = planes * (parts + 4)
        return [
            pltpu.VMEM((planes, cells, rows, D), BF16),
            pltpu.VMEM((2, cells, rows, D), BF16),
            pltpu.VMEM((planes, side, rows, D), BF16),
            pltpu.VMEM((planes, rows, D), BF16),
            pltpu.VMEM((planes, rows, D), BF16),
            pltpu.SemaphoreType.DMA((2, parts)),
            pltpu.SemaphoreType.DMA((count,)),
            pltpu.SemaphoreType.DMA((count,)),
        ]

    def remote(self, slot, source, target, to):
        return pltpu.make_async_remote_copy(
            src_ref=source, dst_ref=target, send_sem=self.send.at[slot], recv_sem=self.recv.at[slot],
            device_id=to, device_id_type=MESH,
        )

    def rows(self, part):
        return pl.ds(self.offsets[part], self.offsets[part + 1] - self.offsets[part])

    def cell(self, a, b):
        return a * self.place.step_a + b * self.place.step_b

    def core_copy(self, k, part):
        place = self.place
        group = pl.ds(place.run(place.plane(k), 1 - place.core), self.cells)
        return self.remote(
            k * self.parts + part, self.sources[part].at[group], self.land.at[k, :, self.rows(part)],
            place.other_core(),
        )

    def load_copy(self, t, part):
        place = self.place
        group = pl.ds(place.run(place.plane(self.order[t]), place.core), self.cells)
        return pltpu.make_async_copy(
            self.sources[part].at[group], self.ours.at[t % 2, :, self.rows(part)], self.load.at[t % 2, part]
        )

    def b_copy(self, k, a):
        place = self.place
        base = self.planes * self.parts
        return self.remote(
            base + 2 * k + a, self.land.at[k, self.cell(a, 1 - place.b)], self.got_b.at[k, a], place.across_b()
        )

    def a_copy(self, k):
        place = self.place
        base = self.planes * (self.parts + 2)
        return self.remote(
            base + k, self.land.at[k, self.cell(1 - place.a, place.b)], self.got_a.at[k], place.across_a()
        )

    def z_copy(self, k):
        place = self.place
        base = self.planes * (self.parts + 3)
        return self.remote(
            base + k, self.land.at[k, self.cell(place.a, place.b)], self.got_z.at[k], place.along_z(k)
        )

    def start(self, part):
        for k in self.order:
            self.core_copy(k, part).start()

    def start_one(self, t):
        self.core_copy(self.order[t], 0).start()

    def load_first(self):
        for part in range(self.parts):
            self.load_copy(0, part).start()

    def arrive_core(self, t):
        k = self.order[t]
        if t + 1 < self.planes:
            for part in range(self.parts):
                self.load_copy(t + 1, part).start()
        for part in range(self.parts):
            self.load_copy(t, part).wait()
            self.core_copy(k, part).wait_recv()

        def add(cell, _):
            self.land[k, cell] = self.land[k, cell] + self.ours[t % 2, cell]
            return 0

        lax.fori_loop(0, self.cells, add, 0)
        for a in range(self.side):
            self.b_copy(k, a).start()

    def arrive_b(self, t):
        k = self.order[t]
        for a in range(self.side):
            self.b_copy(k, a).wait_recv()
            at = self.cell(a, self.place.b)
            self.land[k, at] = self.land[k, at] + self.got_b[k, a]
        self.a_copy(k).start()

    def arrive_a(self, t):
        k = self.order[t]
        self.a_copy(k).wait_recv()
        at = self.cell(self.place.a, self.place.b)
        if k:
            self.land[k, at] = self.land[k, at] + self.got_a[k]
            self.z_copy(k).start()
        else:
            self.mine[...] = self.land[k, at].astype(F32) + self.got_a[k].astype(F32)

    def finish(self):
        for k in range(1, self.planes):
            self.z_copy(k).wait_recv()
            self.mine[...] += self.got_z[k].astype(F32)
        for k in range(self.planes):
            for part in range(self.parts):
                self.core_copy(k, part).wait_send()
            for a in range(self.side):
                self.b_copy(k, a).wait_send()
            self.a_copy(k).wait_send()
            if k:
                self.z_copy(k).wait_send()


def own_blocks(place, wq, wo, wu, wd, small, b_up, own1, own2):
    index = place.run(place.z, place.core) + place.a * place.step_a + place.b * place.step_b

    def spread(size, first):
        lane = lax.broadcasted_iota(jnp.int32, (size, D), 1)
        return jnp.where(lane == first + lax.broadcasted_iota(jnp.int32, (size, D), 0), 1.0, 0.0).astype(BF16)

    per_row = D // UROWS
    vec1 = mm(small[...], spread(OROWS, index * OROWS), 1, 0)
    whole_row = jnp.broadcast_to(b_up[...].astype(F32), (8, UROWS))
    here = lax.broadcasted_iota(jnp.int32, (8, UROWS), 0) == index // per_row
    vec2 = mm(jnp.where(here, whole_row, 0.0).astype(BF16), spread(UROWS, index % per_row * UROWS), 1, 0)
    own1[...] = jnp.concatenate([wq[...].astype(F32), vec1], axis=0).astype(BF16)
    own2[0:UROWS, :] = wu[...]
    down = wd[...].astype(F32)
    rest = [down[:, c * D : (c + 1) * D] for c in range(CHUNKS)] + [wo[...].astype(F32), vec2]
    own2[UROWS:SECOND, :] = jnp.concatenate(rest, axis=0).astype(BF16)


def forward_kernel(planes, side, rows, *refs):
    if planes:
        wq, wo, wu, wd, small, b_up, *refs = refs
    else:
        first_ref, full2, *refs = refs
    (hid_ref, emb_ref, seg_ref, packed_ref, mixed_ref, mid_ref, norm_ref, total_ref, vec_ref, w_qkv, w_out, scaled_ref,
     *refs) = refs
    if planes:
        full2, *refs = refs
    first, tail, bias_col, mask_q, mask_k, load, *refs = refs
    step = pl.program_id(0)
    begin = 2 * rows
    leave = begin + 7 * rows
    row, phase = (step - begin) // 7, (step - begin) % 7
    attending = (step >= begin) & (step < leave)
    tail_copy = pltpu.make_async_copy(full2.at[:, pl.ds(2 * UROWS, 32)], tail, load.at[0])

    if planes:
        own1, own2, send1, recv1, send2, recv2 = refs
        place = Place(planes, side)
        gather1 = Gather(place, own1, first, send1, recv1)
        gather2 = Gather(place, own2, full2, send2, recv2)

        @pl.when(step == 0)
        def _():
            own_blocks(place, wq, wo, wu, wd, small, b_up, own1, own2)
            place.greet()
            gather1.start_z(range(1, planes))
            gather1.start_ab()

        @pl.when(step == begin)
        def _():
            for which, kind, k in FIRST_SCHED:
                (gather1, gather2)[which].event(kind, k)

        for at, kind, k in SCHED:
            @pl.when(step == begin + at)
            def _(kind=kind, k=k):
                gather2.event(kind, k)

        @pl.when(step == begin + SCHED[-1][0])
        def _():
            tail_copy.start()
    else:
        @pl.when(step == 0)
        def _():
            tail_copy.start()
            c = pltpu.make_async_copy(first_ref, first, load.at[1])
            c.start()
            c.wait()

    @pl.when(step < begin)
    def _():
        scaled, _ = normalise(hid_ref[...].astype(F32) + emb_ref[...].astype(F32))
        mixed_ref[pl.ds(pl.multiple_of(step * TOKB, TOKB), TOKB), :] = scaled
        scaled_ref[...] = scaled.astype(BF16)

    @pl.when(step == begin)
    def _():
        join_rows(first, 0, QROWS, w_qkv, BLOCKS // 2)
        vec_ref[0] = sum_rows(first, QROWS)
        bias_col[0:D] = column(vec_ref[0, 2:3, :])
        bias_col[D : 2 * D] = jnp.zeros((D, 1), F32)
        bias_col[2 * D : 3 * D] = column(vec_ref[0, 3:4, :])

    tokens = pl.ds(pl.multiple_of(row * ROW, ROW), ROW)

    @pl.when(attending & (phase == 0))
    def _():
        normed = (mixed_ref[tokens, :] * vec_ref[0, 0:1, :] + vec_ref[0, 1:2, :]).astype(BF16)
        packed_ref[...] = (mm(w_qkv[...], normed, 1, 1) + bias_col[...]).astype(BF16)
        query_side, key_side = mask_rows(seg_ref[0])
        mask_q[...] = query_side
        mask_k[...] = key_side

    @pl.when(attending & (phase >= 1))
    def _():
        base = pl.multiple_of((phase - 1) * 128, 128)
        ones_rows = jnp.where(lax.broadcasted_iota(jnp.int32, (HEAD, ROW), 0) == 0, 1.0, 0.0).astype(BF16)
        sides = []
        for h in range(2):
            at = base + HEAD * h
            high, low = scaled_query(packed_ref[pl.ds(at, HEAD), :])
            keys = packed_ref[pl.ds(D + at, HEAD), :]
            sides.append((
                jnp.concatenate([high, low, mask_q[...]], axis=0),
                jnp.concatenate([keys, keys, mask_k[...]], axis=0),
                jnp.concatenate([packed_ref[pl.ds(2 * D + at, HEAD), :], ones_rows], axis=0),
            ))
        all_scores = [mm(sides[h][1], sides[h][0], 0, 0) for h in range(2)]
        mixed = []
        for h in range(2):
            scores = all_scores[h]
            top = jnp.max(scores, axis=0, keepdims=True)
            weights = jnp.exp2(scores - top).astype(BF16)
            summed = mm(sides[h][2], weights, 1, 0)
            total = summed[HEAD : HEAD + 1, :]
            mixed.append(summed[:HEAD, :] / total)
            total_ref[0, h : h + 1, :] = top + jnp.log2(total)
        mixed_ref[tokens, pl.ds(base, 128)] = jnp.concatenate(mixed, axis=0).T

    @pl.when(step == leave)
    def _():
        tail_copy.wait()
        join_rows(tail, 0, OROWS, w_out, BLOCKS // 2)
        vec_ref[1] = sum_rows(tail, OROWS)

    @pl.when(step >= leave)
    def _():
        half = pl.ds(pl.multiple_of((step - leave) * TOKB, TOKB), TOKB)
        entered = hid_ref[...].astype(F32) + emb_ref[...].astype(F32)
        middle = entered + mm(mixed_ref[half, :].astype(BF16), w_out[...], 1, 1) + vec_ref[0, 4:5, :]
        scaled, _ = normalise(middle)
        mid_ref[...] = middle
        norm_ref[...] = (scaled * vec_ref[0, 5:6, :] + vec_ref[0, 6:7, :]).astype(BF16)


def forward(planes, side, weights, hidden, embed, segment):
    n = hidden.shape[0]
    rows = n // ROW
    begin = 2 * rows
    leave_at = begin + 7 * rows
    one = pl.Buffered(1)
    hbm = pl.BlockSpec(memory_space=pl.ANY)

    def row(s):
        return jnp.clip((s - begin) // 7, 0, rows - 1)

    def entry(s):
        return (jnp.where(s < leave_at, jnp.minimum(s, begin - 1), s - leave_at), 0)

    def leave(s):
        return (jnp.maximum(s - leave_at, 0), 0)

    def pair(s):
        return jnp.where(s < leave_at, jnp.maximum((s - begin) % 7 - 1, 0) * (s >= begin), 5)

    entering = pl.BlockSpec((TOKB, D), entry)
    leaving = pl.BlockSpec((TOKB, D), leave)
    out_specs = [
        pl.BlockSpec((3 * D, ROW), lambda s: (0, row(s))),
        pl.BlockSpec((n, D), lambda s: (0, 0), pipeline_mode=one),
        leaving,
        leaving,
        pl.BlockSpec((1, 8, ROW), lambda s: (pair(s), 0, row(s))),
        pl.BlockSpec((2, 8, D), lambda s: (0, 0, 0)),
        pl.BlockSpec((3 * D, D), lambda s: (0, 0), pipeline_mode=one),
        pl.BlockSpec((D, D), lambda s: (0, 0), pipeline_mode=one),
        pl.BlockSpec((TOKB, D), lambda s: (jnp.minimum(s, begin - 1), 0)),
    ]
    out_shape = [
        jax.ShapeDtypeStruct((3 * D, n), BF16),
        jax.ShapeDtypeStruct((n, D), F32),
        jax.ShapeDtypeStruct((n, D), F32),
        jax.ShapeDtypeStruct((n, D), BF16),
        jax.ShapeDtypeStruct((HEADS // 2, 8, n), F32),
        jax.ShapeDtypeStruct((2, 8, D), F32),
        jax.ShapeDtypeStruct((3 * D, D), BF16),
        jax.ShapeDtypeStruct((D, D), BF16),
        jax.ShapeDtypeStruct((n, D), BF16),
    ]
    scratch = [
        pltpu.VMEM((BLOCKS, FIRST, D), BF16),
        pltpu.VMEM((BLOCKS, 32, D), BF16),
        pltpu.VMEM((3 * D, 1), F32),
        pltpu.VMEM((32, ROW), BF16),
        pltpu.VMEM((32, ROW), BF16),
        pltpu.SemaphoreType.DMA((2,)),
    ]
    params = dict(vmem_limit_bytes=56 * MIB)
    if planes:
        in_specs = [pl.BlockSpec(w.shape, lambda s: (0, 0), pipeline_mode=one) for w in weights]
        out_specs.append(hbm)
        out_shape.append(jax.ShapeDtypeStruct((BLOCKS, SECOND, D), BF16))
        scratch += [pltpu.VMEM((FIRST, D), BF16), pltpu.VMEM((SECOND, D), BF16)]
        scratch += [Gather.semaphores(planes)] * 4
        params.update(collective_id=1, has_side_effects=True)
    else:
        in_specs = [hbm, hbm]
    outs = pl.pallas_call(
        partial(forward_kernel, planes, side, rows),
        grid=(leave_at + begin,),
        in_specs=in_specs + [entering, entering, pl.BlockSpec((1, 1, ROW), lambda s: (row(s), 0, 0))],
        out_specs=out_specs,
        out_shape=out_shape,
        scratch_shapes=scratch,
        compiler_params=pltpu.CompilerParams(**params),
        name="attention_forward",
    )(*weights, hidden, embed, segment.reshape(rows, 1, ROW))
    return outs if planes else list(outs) + [weights[1]]


def feed_kernel(
    rows,
    up_ref, down_ref, vec_ref, norm_ref, mid_ref, cot_ref, seg_ref,
    out_ref, gmid_ref, gup_ref, gdown_ref, gvec_ref,
    w_down, result, back, live, active, pre, hold,
):
    step = pl.program_id(0)
    working = step < CHUNKS * rows
    j, i = step // rows, step % rows
    at = pl.ds(pl.multiple_of(i * ROW, ROW), ROW)

    @pl.when(step == 0)
    def _():
        gvec_ref[...] = jnp.zeros_like(gvec_ref)

    for chunk in range(CHUNKS):
        @pl.when(step == chunk * rows)
        def _():
            join_rows(down_ref, chunk % 2 * OROWS, OROWS, w_down, BLOCKS // 2)

    @pl.when(step < rows)
    def _():
        keep = column(jnp.where(seg_ref[0] >= 0, 1.0, 0.0))
        grad_result = cot_ref[...].astype(F32) * keep
        live[at, :] = grad_result.astype(BF16)
        gvec_ref[4:5, :] += jnp.sum(grad_result, axis=0, keepdims=True)

    @pl.when(working)
    def _():
        up = up_ref[...].reshape(D, D)
        down = w_down[...]
        x = mm(norm_ref[at, :], up, 1, 1) + vec_ref[1, pl.ds(j, 1), :]
        grad_act = mm(live[at, :], down, 1, 0)
        c0 = math.sqrt(2.0 / math.pi)
        c1 = 0.044715
        square = x * x
        th = jnp.tanh(x * (c0 + (c0 * c1) * square))
        half = 0.5 + 0.5 * th
        slope = half + (0.5 * x) * ((1.0 - th * th) * (c0 + (3 * c0 * c1) * square))
        activated = (x * half).astype(BF16)
        grad_pre = (grad_act * slope).astype(BF16)
        active[at, :] = activated
        pre[at, :] = grad_pre
        gvec_ref[pl.ds(j, 1), :] += jnp.sum(grad_pre.astype(F32), axis=0, keepdims=True)

        @pl.when(j == 0)
        def _():
            result[at, :] = mm(activated, down, 1, 1)
            back[at, :] = mm(grad_pre, up, 1, 0)

        @pl.when(j > 0)
        def _():
            result[at, :] += mm(activated, down, 1, 1)
            back[at, :] += mm(grad_pre, up, 1, 0)

    @pl.when(working & (i == rows - 1))
    def _():
        gup_ref[...] = mm(pre[...], norm_ref[...], 0, 0).astype(BF16)
        part_down = mm(live[...], active[...], 0, 0)

        hold[...] = part_down

        @pl.when(j % 2 == 0)
        def _():
            def pack(d, _):
                own = pl.ds(pl.multiple_of(d * OROWS, 8), OROWS)
                gdown_ref[d] = jnp.concatenate([hold[own], jnp.zeros((OROWS, D), F32)], axis=0).astype(BF16)
                return 0

            lax.fori_loop(0, BLOCKS, pack, 0)

        @pl.when(j % 2 == 1)
        def _():
            def pack(d, _):
                own = pl.ds(pl.multiple_of(d * OROWS, 8), OROWS)
                kept = gdown_ref[d].astype(F32)[:OROWS]
                gdown_ref[d] = jnp.concatenate([kept, hold[own]], axis=0).astype(BF16)
                return 0

            lax.fori_loop(0, BLOCKS, pack, 0)

    @pl.when(step >= CHUNKS * rows)
    def _():
        tokens = pl.ds(pl.multiple_of((step - CHUNKS * rows) * TOKB, TOKB), TOKB)
        middle = mid_ref[...]
        out_ref[...] = (middle + (result[tokens, :] + vec_ref[0, 7:8, :])).astype(BF16)
        grad = back[tokens, :]
        scaled, inverse = normalise(middle)
        gvec_ref[5:6, :] += jnp.sum(grad * scaled, axis=0, keepdims=True)
        gvec_ref[6:7, :] += jnp.sum(grad, axis=0, keepdims=True)
        gmid_ref[...] = live[tokens, :].astype(F32) + norm_back(grad, scaled, inverse, vec_ref[0, 5:6, :])


def feed(second, vec, normed, middle, cotangent, segment):
    n = normed.shape[0]
    rows = n // ROW
    one = pl.Buffered(1)

    def chunk(s):
        return jnp.minimum(s // rows, CHUNKS - 1)

    def late(s):
        return (jnp.maximum(s - CHUNKS * rows, 0), 0)

    leaving = pl.BlockSpec((TOKB, D), late)
    return pl.pallas_call(
        partial(feed_kernel, rows),
        grid=(CHUNKS * rows + n // TOKB,),
        in_specs=[
            pl.BlockSpec((BLOCKS // CHUNKS, UROWS, D), lambda s: (chunk(s), 0, 0)),
            pl.BlockSpec((BLOCKS, 2 * OROWS, D), lambda s: (0, 2 + chunk(s) // 2, 0), pipeline_mode=one),
            pl.BlockSpec((2, 8, D), lambda s: (0, 0, 0)),
            pl.BlockSpec((n, D), lambda s: (0, 0), pipeline_mode=one),
            leaving,
            pl.BlockSpec((ROW, D), lambda s: (jnp.minimum(s, rows - 1), 0), pipeline_mode=one),
            pl.BlockSpec((1, 1, ROW), lambda s: (jnp.minimum(s, rows - 1), 0, 0)),
        ],
        out_specs=[
            leaving,
            leaving,
            pl.BlockSpec((D, D), lambda s: (chunk(s), 0)),
            pl.BlockSpec((BLOCKS, 2 * OROWS, D), lambda s: (0, chunk(s) // 2, 0), pipeline_mode=one),
            pl.BlockSpec((8, D), lambda s: (0, 0)),
        ],
        out_shape=[
            jax.ShapeDtypeStruct((n, D), BF16),
            jax.ShapeDtypeStruct((n, D), F32),
            jax.ShapeDtypeStruct((FF, D), BF16),
            jax.ShapeDtypeStruct((BLOCKS, UROWS, D), BF16),
            jax.ShapeDtypeStruct((8, D), F32),
        ],
        scratch_shapes=[
            pltpu.VMEM((D, D), BF16),
            pltpu.VMEM((n, D), F32),
            pltpu.VMEM((n, D), F32),
            pltpu.VMEM((n, D), BF16),
            pltpu.VMEM((n, D), BF16),
            pltpu.VMEM((n, D), BF16),
            pltpu.VMEM((D, D), F32),
        ],
        compiler_params=pltpu.CompilerParams(vmem_limit_bytes=60 * MIB),
        name="feed_forward",
    )(second, second, vec, normed, middle, cotangent, segment.reshape(rows, 1, ROW))


def three_parts(row):
    r = lax.broadcasted_iota(jnp.int32, (16, row.shape[1]), 0)
    a = row.astype(BF16).astype(F32)
    b = (row - a).astype(BF16).astype(F32)
    c = row - a - b
    return jnp.where(r == 0, -a, jnp.where(r == 1, -b, jnp.where(r == 2, -c, 0.0))).astype(BF16)


def backward_kernel(
    planes, side, rows,
    w_out, seg_ref, packed_q, packed_k, packed_v, mixed_ref, total_ref, gmid_ref, gvec_ref, gup_ref, gdown_ref,
    gpacked_ref, sums_ref, *rest,
):
    if planes:
        mine, mask_q, mask_k, grad_mixed, delta, sum_out, sum_bias, tail, *transfer = rest
    else:
        tail, mask_q, mask_k, grad_mixed, delta, sum_out, sum_bias = rest
    step = pl.program_id(0)
    entry = 2 * rows
    heads = step >= entry

    if planes:
        place = Place(planes, side)
        scatter = Scatter(place, (gup_ref, gdown_ref, tail), *transfer[:5], mine, *transfer[5:])

        @pl.when(step == 0)
        def _():
            place.greet()
            scatter.start(0)
            scatter.start(1)

        @pl.when(step == entry)
        def _():
            scatter.start(2)
            scatter.load_first()

        for at, t, act in BACK:
            @pl.when(step == entry + at)
            def _(t=t, act=act):
                getattr(scatter, act)(t)

    @pl.when(step == 0)
    def _():
        sum_out[...] = jnp.zeros_like(sum_out)
        sum_bias[...] = jnp.zeros_like(sum_bias)

    @pl.when(step < entry)
    def _():
        at = pl.ds(pl.multiple_of(step * TOKB, TOKB), TOKB)
        mixed = mixed_ref[...]
        branch = gmid_ref[...].astype(BF16)
        sum_bias[0:1, :] += jnp.sum(branch.astype(F32), axis=0, keepdims=True)
        sum_out[...] += mm(branch, mixed.astype(BF16), 0, 0)
        grad = mm(branch, w_out[...], 1, 0).astype(BF16).astype(F32)
        grad_mixed[:, at] = grad.T.astype(BF16)
        inner = (grad * mixed).T
        delta[:, at] = jnp.concatenate(
            [jnp.sum(inner[HEAD * h : HEAD * (h + 1)], axis=0, keepdims=True) for h in range(HEADS)]
            + [jnp.zeros((16 - HEADS, TOKB), F32)],
            axis=0,
        )

    @pl.when(step == entry - 1)
    def _():
        r = lax.broadcasted_iota(jnp.int32, (8, D), 0)
        vectors = jnp.where(r == 7, sum_bias[0:1, :], gvec_ref[...])

        def pack(d, _):
            at = pl.ds(pl.multiple_of(d * OROWS, 8), OROWS)
            tail[d] = jnp.concatenate([sum_out[at, :], vectors], axis=0).astype(BF16)
            return 0

        lax.fori_loop(0, BLOCKS, pack, 0)

    row, pair = (step - entry) // 6, (step - entry) % 6

    @pl.when(heads & (pair == 0))
    def _():
        query_side, key_side = mask_rows(seg_ref[0])
        mask_q[...] = query_side
        mask_k[...] = key_side

    @pl.when(heads)
    def _():
        tokens = pl.ds(pl.multiple_of(row * ROW, ROW), ROW)
        r = lax.broadcasted_iota(jnp.int32, (16, ROW), 0)
        ones_rows = jnp.where(r < 3, 1.0, 0.0).astype(BF16)
        base = pl.multiple_of(pair * 128, 128)
        column_sums = []
        for h in range(2):
            at_rows = slice(HEAD * h, HEAD * (h + 1))
            queries, keys, values = packed_q[at_rows, :], packed_k[at_rows, :], packed_v[at_rows, :]
            grad = grad_mixed[pl.ds(base + HEAD * h, HEAD), tokens]
            high, low = scaled_query(queries)
            wide_q = jnp.concatenate([high, low, mask_q[...], three_parts(total_ref[0, h : h + 1, :])], axis=0)
            wide_k = jnp.concatenate([keys, keys, mask_k[...], ones_rows], axis=0)
            wide_g = jnp.concatenate([grad, three_parts(delta[pl.ds(2 * pair + h, 1), tokens])], axis=0)
            wide_v = jnp.concatenate([values, ones_rows], axis=0)
            grad_v = jnp.zeros((HEAD, ROW), F32)
            grad_k = jnp.zeros((HEAD, ROW), F32)
            grad_q = []
            for half in range(2):
                at = slice(half * (ROW // 2), (half + 1) * (ROW // 2))
                probs = jnp.exp2(mm(wide_q[:, at], wide_k, 0, 0))
                grad_probs = mm(wide_g[:, at], wide_v, 0, 0)
                grad_scores = (probs * grad_probs).astype(BF16)
                grad_v = grad_v + mm(grad[:, at], probs.astype(BF16), 1, 0)
                grad_k = grad_k + mm(queries[:, at], grad_scores, 1, 0)
                grad_q.append(mm(keys, grad_scores, 1, 1))
            grads = (
                (jnp.concatenate(grad_q, axis=1) * 0.125).astype(BF16),
                (grad_k * 0.125).astype(BF16),
                grad_v.astype(BF16),
            )
            for part in range(3):
                gpacked_ref[pl.ds(part * D + base + HEAD * h, HEAD), :] = grads[part]
            column_sums.append([jnp.sum(g.astype(F32), axis=1, keepdims=True) for g in grads])
        for part in range(3):
            both = jnp.concatenate([column_sums[0][part], column_sums[1][part]], axis=0)
            at = pl.ds(part * D + base, 128)

            @pl.when(row == 0)
            def _():
                sums_ref[at, :] = both

            @pl.when(row > 0)
            def _():
                sums_ref[at, :] += both

    if planes:
        @pl.when(step == entry + 6 * rows - 1)
        def _():
            scatter.finish()


def backward(planes, side, w_out, segment, packed, mixed, totals, gmid, gvec, gup, gdown):
    n = mixed.shape[0]
    rows = n // ROW
    entry = 2 * rows
    one = pl.Buffered(1)
    hbm = pl.BlockSpec(memory_space=pl.ANY)

    def early(s):
        return (jnp.minimum(s, entry - 1), 0)

    def row(s):
        return jnp.maximum(s - entry, 0) // 6

    def pair(s):
        return jnp.maximum(s - entry, 0) % 6

    def heads(part):
        return pl.BlockSpec((128, ROW), lambda s: (6 * part + pair(s), row(s)))

    out_specs = [
        pl.BlockSpec((3 * D, ROW), lambda s: (0, row(s))),
        pl.BlockSpec((3 * D, 1), lambda s: (0, 0), pipeline_mode=one),
    ]
    out_shape = [jax.ShapeDtypeStruct((3 * D, n), BF16), jax.ShapeDtypeStruct((3 * D, 1), F32)]
    scratch = [
        pltpu.VMEM((32, ROW), BF16),
        pltpu.VMEM((32, ROW), BF16),
        pltpu.VMEM((D, n), BF16),
        pltpu.VMEM((16, n), F32),
        pltpu.VMEM((D, D), F32),
        pltpu.VMEM((8, D), F32),
    ]
    params = dict(vmem_limit_bytes=56 * MIB)
    if planes:
        rows1 = 2 * UROWS + 32
        out_specs.append(pl.BlockSpec((rows1, D), lambda s: (0, 0), pipeline_mode=one))
        out_shape.append(jax.ShapeDtypeStruct((rows1, D), F32))
        scratch.append(pltpu.VMEM((BLOCKS, 32, D), BF16))
        scratch += Scatter.scratch(planes, side, 3, rows1)
        params.update(collective_id=2, has_side_effects=True)
    else:
        out_specs.append(pl.BlockSpec((BLOCKS, 32, D), lambda s: (0, 0, 0), pipeline_mode=one))
        out_shape.append(jax.ShapeDtypeStruct((BLOCKS, 32, D), BF16))
    return pl.pallas_call(
        partial(backward_kernel, planes, side, rows),
        grid=(entry + 6 * rows,),
        in_specs=[
            pl.BlockSpec((D, D), lambda s: (0, 0), pipeline_mode=one),
            pl.BlockSpec((1, 1, ROW), lambda s: (row(s), 0, 0)),
            heads(0),
            heads(1),
            heads(2),
            pl.BlockSpec((TOKB, D), early),
            pl.BlockSpec((1, 8, ROW), lambda s: (pair(s), 0, row(s))),
            pl.BlockSpec((TOKB, D), early),
            pl.BlockSpec((8, D), lambda s: (0, 0)),
            hbm,
            hbm,
        ],
        out_specs=out_specs,
        out_shape=out_shape,
        scratch_shapes=scratch,
        compiler_params=pltpu.CompilerParams(**params),
        name="attention_backward",
    )(w_out, segment.reshape(rows, 1, ROW), packed, packed, packed, mixed, totals, gmid, gvec, gup, gdown)


def enter_kernel(
    planes, side, blocks,
    w_hbm, vec_ref, hid_ref, emb_ref, gmid_ref, grad_hbm, sums_ref, scaled_hbm,
    ghid_ref, out_ref, *rest,
):
    if planes:
        mine, (scaled_all, w_qkv, grad_packed, totals, load, packed, *transfer) = out_ref, rest
    else:
        packed, (scaled_all, w_qkv, grad_packed, totals, load) = out_ref, rest
    step = pl.program_id(0)
    chunks = 4
    size = 3 * D // chunks
    begin, late = 0, chunks
    if planes:
        place = Place(planes, side)

    def chunk_of(t):
        return place.plane(t + 1) if planes else t

    def grad_load(t):
        rows = pl.ds(pl.multiple_of(chunk_of(t) * size, size), size)
        return pltpu.make_async_copy(grad_hbm.at[rows], grad_packed.at[rows], load.at[t])

    loads = [
        pltpu.make_async_copy(scaled_hbm, scaled_all, load.at[chunks]),
        pltpu.make_async_copy(w_hbm, w_qkv, load.at[chunks + 1]),
    ]

    if planes:
        rider = Rider(place, *transfer[:4])
        scatter = Scatter(place, (packed,), *transfer[4:9], mine, *transfer[9:])

    @pl.when(step == 0)
    def _():
        loads[0].start()
        grad_load(0).start()
        loads[1].start()
        for t in range(1, chunks):
            grad_load(t).start()
        totals[...] = jnp.zeros_like(totals)
        if planes:
            place.greet()

    def entering():
        return normalise(hid_ref[...].astype(F32) + emb_ref[...].astype(F32))

    @pl.when(step == begin)
    def _():
        for c in loads:
            c.wait()

    for t in range(chunks):
        @pl.when(step == t)
        def _(t=t):
            grad_load(t).wait()

    if planes:
        for at, t, act in ENTER:
            @pl.when(step == begin + at)
            def _(t=t, act=act):
                getattr(scatter, act)(t)
                if t == planes - 1:
                    rider.arrive(("arrive_core", "arrive_b", "arrive_a").index(act))

    @pl.when((step >= begin) & (step < late))
    def _():
        t = step - begin
        chunk = chunk_of(t)
        at = pl.ds(pl.multiple_of(chunk * size, size), size)
        product = mm(grad_packed[at, :], scaled_all[...], 1, 0)
        weight = w_qkv[at, :].astype(F32)
        sums = sums_ref[at, :]
        totals[0:1, :] += jnp.sum(weight * product, axis=0, keepdims=True)
        totals[1:2, :] += jnp.sum(weight * sums, axis=0, keepdims=True)
        grad_w = product * vec_ref[0, 0:1, :] + sums * vec_ref[0, 1:2, :]
        count = BLOCKS // chunks
        for i in range(count):
            rows = [grad_w[i * QROWS : (i + 1) * QROWS], jnp.zeros((8, D), F32)]
            packed[chunk * count + i] = jnp.concatenate(rows, axis=0).astype(BF16)

    if planes:
        for t in range(planes):
            @pl.when(step == begin + t)
            def _(t=t):
                scatter.start_one(t)
                if t == 0:
                    scatter.load_first()

    @pl.when(step == late - 1)
    def _():
        ends = [jnp.broadcast_to(sums_ref[at : at + D, :], (D, 128)).T[0:1, :] for at in (0, 2 * D)]
        vectors = jnp.concatenate([totals[0:2, :]] + ends + [jnp.zeros((4, D), F32)], axis=0)
        if planes:
            rider.stages[0] = vectors
            rider.start()
        else:
            kept = packed[0, QROWS - 8 : QROWS + 8, :].astype(F32)[:8]
            packed[0, QROWS - 8 : QROWS + 8, :] = jnp.concatenate([kept, vectors], axis=0).astype(BF16)

    @pl.when(step >= late)
    def _():
        at = pl.ds(pl.multiple_of((step - late) * TOKB, TOKB), TOKB)
        scaled, inverse = entering()
        grad = mm(grad_packed[:, at], w_qkv[...], 0, 0)
        ghid_ref[...] = (gmid_ref[...] + norm_back(grad, scaled, inverse, vec_ref[0, 0:1, :])).astype(BF16)

    if planes:
        @pl.when(step == late + blocks - 1)
        def _():
            for t, act in ENTER_LAST:
                getattr(scatter, act)(t)
                if t == planes - 1:
                    rider.arrive(("arrive_core", "arrive_b", "arrive_a").index(act))
            scatter.finish()
            mine[QROWS : QROWS + 8, :] = rider.finish()


def enter(planes, side, w_qkv, vec, hidden, embed, gmid, gpacked, sums, scaled):
    n = hidden.shape[0]
    blocks = n // TOKB
    late_at = 4
    one = pl.Buffered(1)
    hbm = pl.BlockSpec(memory_space=pl.ANY)

    def late(s):
        return (jnp.maximum(s - late_at, 0), 0)

    tokens = pl.BlockSpec((TOKB, D), late)
    out_specs = [pl.BlockSpec((TOKB, D), late)]
    out_shape = [jax.ShapeDtypeStruct((n, D), BF16)]
    scratch = [
        pltpu.VMEM((n, D), BF16),
        pltpu.VMEM((3 * D, D), BF16),
        pltpu.VMEM((3 * D, n), BF16),
        pltpu.VMEM((8, D), F32),
        pltpu.SemaphoreType.DMA((6,)),
    ]
    params = dict(vmem_limit_bytes=56 * MIB)
    if planes:
        out_specs.append(pl.BlockSpec((FIRST, D), lambda s: (0, 0), pipeline_mode=one))
        out_shape.append(jax.ShapeDtypeStruct((FIRST, D), F32))
        scratch.append(pltpu.VMEM((BLOCKS, FIRST, D), BF16))
        scratch += Rider.scratch(planes) + Scatter.scratch(planes, side, 1, FIRST)
        params.update(collective_id=3, has_side_effects=True)
    else:
        out_specs.append(pl.BlockSpec((BLOCKS, FIRST, D), lambda s: (0, 0, 0), pipeline_mode=one))
        out_shape.append(jax.ShapeDtypeStruct((BLOCKS, FIRST, D), BF16))
    return pl.pallas_call(
        partial(enter_kernel, planes, side, blocks),
        grid=(late_at + blocks,),
        in_specs=[
            hbm,
            pl.BlockSpec((2, 8, D), lambda s: (0, 0, 0)),
            tokens,
            tokens,
            pl.BlockSpec((TOKB, D), late),
            hbm,
            pl.BlockSpec((3 * D, 1), lambda s: (0, 0), pipeline_mode=one),
            hbm,
        ],
        out_specs=out_specs,
        out_shape=out_shape,
        scratch_shapes=scratch,
        compiler_params=pltpu.CompilerParams(**params),
        name="projection_backward",
    )(w_qkv, vec, hidden, embed, gmid, gpacked, sums, scaled)


def body(
    planes, side, devices,
    hidden, time_embed, segment_ids,
    ln1_gain, ln1_bias, w_qkv, b_query, b_value, w_out, b_out, ln2_gain, ln2_bias, w_up, b_up, w_down, b_down,
    cotangent,
):
    index = lax.axis_index("dp") * lax.axis_size("fsdp") + lax.axis_index("fsdp")
    axes = ("dp", "fsdp")
    small = (ln1_gain, ln1_bias, b_query, b_value, b_out, ln2_gain, ln2_bias, b_down)
    if planes:
        weights = (w_qkv.T, w_out.T, w_up.T, w_down.T, jnp.stack(small), b_up[None, :])
    else:
        def whole(a, dim):
            return lax.all_gather(a, axes, axis=dim, tiled=True)

        def only_first(rows):
            return jnp.concatenate([rows[None], jnp.zeros((BLOCKS - 1,) + rows.shape, BF16)], axis=0)

        vec1 = jnp.stack([whole(v, 0) for v in small])
        vec2 = jnp.concatenate([whole(b_up, 0).reshape(CHUNKS, D), jnp.zeros((8 - CHUNKS, D), BF16)], axis=0)
        down_rows = whole(w_down, 1).T.reshape(BLOCKS, OROWS, CHUNKS, D).transpose(0, 2, 1, 3)
        first = jnp.concatenate([whole(w_qkv, 1).T.reshape(BLOCKS, QROWS, D), only_first(vec1)], axis=1)
        second = jnp.concatenate(
            [
                whole(w_up, 1).T.reshape(BLOCKS, UROWS, D),
                down_rows.reshape(BLOCKS, UROWS, D),
                whole(w_out, 1).T.reshape(BLOCKS, OROWS, D),
                only_first(vec2),
            ],
            axis=1,
        )
        weights = (first, second)
    packed, mixed, middle, normed, totals, vec, full_qkv, full_out, scaled, second = forward(
        planes, side, weights, hidden, time_embed, segment_ids
    )
    output, gmid, gup, gdown, gvec = feed(second, vec, normed, middle, cotangent, segment_ids)
    gup = gup.reshape(BLOCKS, UROWS, D)
    gpacked, sums, late = backward(
        planes, side, full_out, segment_ids, packed, mixed, totals, gmid, gvec, gup, gdown
    )
    ghid, last = enter(planes, side, full_qkv, vec, hidden, time_embed, gmid, gpacked, sums, scaled)
    if planes:
        part_up = late[:UROWS]
        part_down = late[UROWS : 2 * UROWS].reshape(CHUNKS, OROWS, D).transpose(1, 0, 2).reshape(OROWS, FF)
        part_out = late[2 * UROWS : 2 * UROWS + OROWS]
        part_qkv = last[:QROWS]
        vectors = jnp.concatenate([late[2 * UROWS + OROWS :], last[QROWS:]], axis=0)
        short = lax.dynamic_slice(vectors, (0, index * OROWS), (16, OROWS))
        part_bup = lax.dynamic_slice(vectors[:CHUNKS].reshape(-1), (index * UROWS,), (UROWS,))
    else:
        def shared(a, dim):
            return lax.psum_scatter(a.astype(F32), axes, scatter_dimension=dim, tiled=True)

        part_up = shared(gup.reshape(FF, D), 0)
        part_down = shared(gdown.reshape(BLOCKS, CHUNKS, OROWS, D).transpose(0, 2, 1, 3).reshape(D, FF), 0)
        part_out = shared(late[:, :OROWS].reshape(D, D), 0)
        part_qkv = shared(last[:, :QROWS].reshape(3 * D, D), 0)
        vectors = jnp.concatenate([late[0, OROWS:], last[0, QROWS:]], axis=0)
        short = shared(vectors, 1)
        part_bup = shared(vectors[:CHUNKS].reshape(-1), 0)
    return (
        output, ghid,
        short[8], short[9], part_qkv.T, short[10], short[11], part_out.T, short[7],
        short[5], short[6], part_up.T, part_bup, part_down.T, short[4],
    )


def solution(mesh):
    groups, cells = mesh.shape["dp"], mesh.shape["fsdp"]
    side = math.isqrt(cells)
    own_transfers = groups * cells == BLOCKS and side == 2 and cells == 4 and groups % 2 == 0
    split = ("dp", "fsdp")
    rows, flat, cols = P(split, None), P(split), P(None, split)
    return jax.shard_map(
        partial(body, groups // 2 if own_transfers else 0, side, groups * cells),
        mesh=mesh,
        in_specs=(
            rows, rows, flat, flat, flat, cols, flat, flat, cols, flat, flat, flat, cols, flat, cols, flat, rows,
        ),
        out_specs=(
            rows, rows, flat, flat, cols, flat, flat, cols, flat, flat, flat, cols, flat, cols, flat,
        ),
        check_vma=False,
    )
```

```python
from functools import partial
import math

import jax
import jax.numpy as jnp
from jax import lax
from jax.experimental import pallas as pl
from jax.experimental.pallas import tpu as pltpu
from jax.sharding import PartitionSpec as P

D = 768
HEADS = 12
HEAD = 64
FF = 3072
ROW = 1024
BLOCKS = 32
QROWS = 3 * D // BLOCKS
OROWS = D // BLOCKS
UROWS = FF // BLOCKS
CHUNKS = FF // D
FIRST = QROWS + 8
SECOND = 2 * UROWS + OROWS + 8
TOKB = 512
MIB = 2**20
MESH = pl.DeviceIdType.MESH
F32 = jnp.float32
BF16 = jnp.bfloat16
LOG2E = math.log2(math.e)
EPS = 1e-05
FIRST_SCHED = (
    (0, "z", 1), (0, "a", 0), (0, "z", 2), (0, "a", 1), (0, "z", 3), (1, "s", 1), (1, "s", 2), (0, "b", 0), (0, "a", 2),
    (0, "b", 1), (0, "a", 3), (1, "o", 0), (0, "b", 2), (0, "b", 3), (0, "end", 0),
)
SCHED = (
    (0, "z", 1), (0, "s", 3), (1, "a", 0), (2, "a", 1), (2, "z", 2), (3, "b", 0), (5, "a", 2), (6, "z", 3), (6, "b", 1),
    (9, "a", 3), (9, "b", 2), (12, "b", 3), (13, "end", 0),
)
BACK = (
    (1, 0, "arrive_core"), (2, 1, "arrive_core"), (3, 0, "arrive_b"), (4, 2, "arrive_core"), (5, 1, "arrive_b"),
    (5, 0, "arrive_a"), (6, 3, "arrive_core"), (7, 2, "arrive_b"), (8, 1, "arrive_a"), (9, 3, "arrive_b"),
    (9, 2, "arrive_a"), (11, 3, "arrive_a"),
)
ENTER = (
    (2, 0, "arrive_core"), (3, 1, "arrive_core"), (4, 0, "arrive_b"), (4, 2, "arrive_core"), (5, 1, "arrive_b"),
    (5, 3, "arrive_core"), (6, 0, "arrive_a"), (6, 2, "arrive_b"), (7, 1, "arrive_a"), (7, 3, "arrive_b"),
)
ENTER_LAST = ((2, "arrive_a"), (3, "arrive_a"))


def mm(a, b, ca, cb):
    return lax.dot_general(a, b, (((ca,), (cb,)), ((), ())), preferred_element_type=F32)


def normalise(values):
    centred = values - jnp.mean(values, axis=-1, keepdims=True)
    inverse = lax.rsqrt(jnp.mean(centred * centred, axis=-1, keepdims=True) + EPS)
    return centred * inverse, inverse


def norm_back(grad, scaled, inverse, gain):
    u = grad * gain
    return inverse * (
        u
        - jnp.mean(u, axis=-1, keepdims=True)
        - scaled * jnp.mean(u * scaled, axis=-1, keepdims=True)
    )


def column(row):
    return jnp.broadcast_to(row, (128, row.shape[1])).T[:, :1]


def join_rows(source, start, rows, target, pairs):
    low = start // 16 * 16
    high = -(-(start + rows) // 16) * 16

    def step(p, _):
        parts = [
            source[2 * p + i, low:high, :].astype(F32)[start - low : start - low + rows]
            for i in range(2)
        ]
        at = pl.multiple_of(2 * rows * p, 2 * rows)
        target[pl.ds(at, 2 * rows), :] = jnp.concatenate(parts, axis=0).astype(BF16)
        return 0

    lax.fori_loop(0, pairs, step, 0)


def sum_rows(source, start):
    low = start // 16 * 16

    def step(d, total):
        return total + source[d, low : low + 16, :].astype(F32)[start - low : start - low + 8]

    return lax.fori_loop(0, BLOCKS, step, jnp.zeros((8, D), F32))


def mask_rows(segment):
    r = lax.broadcasted_iota(jnp.int32, (32, ROW), 0)
    hit = r == segment + 1
    query_side = jnp.where(hit, 1.0, 0.0).astype(BF16)
    key_side = jnp.where(hit | (r >= 17), 0.0, -1e30).astype(BF16)
    return query_side, key_side


def scaled_query(queries):
    wide = queries.astype(F32) * (LOG2E / 8)
    high = wide.astype(BF16)
    low = (wide - high.astype(F32)).astype(BF16)
    return high, low


class Place:
    def __init__(self, planes, side):
        self.planes, self.side = planes, side
        group, cell = lax.axis_index("dp"), lax.axis_index("fsdp")
        self.z, self.core = group // 2, group % 2
        y, x = cell // side, cell % side
        self.step_a = 1 + self.core * (side - 1)
        self.step_b = side - self.core * (side - 1)
        self.a = x + self.core * (y - x)
        self.b = y + self.core * (x - y)

    def plane(self, k):
        return lax.rem(self.z + k + self.planes, self.planes)

    def paired(self, k):
        plane, bit = self.z, 1
        while bit <= k:
            if k & bit:
                plane = plane + bit - 2 * bit * (self.z // bit % 2)
            bit *= 2
        return plane

    def at(self, z, core, a, b):
        return (z * 2 + core, a * self.step_a + b * self.step_b)

    def block(self, z, a, b):
        return (z * 2 + self.core) * (self.side * self.side) + a * self.step_a + b * self.step_b

    def run(self, z, core):
        return (z * 2 + core) * (self.side * self.side)

    def across_a(self):
        return self.at(self.z, self.core, 1 - self.a, self.b)

    def across_b(self):
        return self.at(self.z, self.core, self.a, 1 - self.b)

    def other_core(self):
        return (self.z * 2 + 1 - self.core, self.a * self.step_a + self.b * self.step_b)

    def along_z(self, k):
        return self.at(self.plane(k), self.core, self.a, self.b)

    def arrive(self):
        barrier = pltpu.get_barrier_semaphore()
        peers = [self.along_z(k) for k in range(1, self.planes)]
        peers += [self.across_a(), self.across_b(), self.other_core()]
        for peer in peers:
            pl.semaphore_signal(barrier, inc=1, device_id=peer, device_id_type=MESH)

    def meet(self):
        pl.semaphore_wait(pltpu.get_barrier_semaphore(), self.planes + 2)


class Gather:
    def __init__(self, place, own, full, send, recv):
        self.place, self.own, self.full, self.send, self.recv = place, own, full, send, recv
        self.planes = place.planes

    @staticmethod
    def semaphores(planes):
        return pltpu.SemaphoreType.DMA((5 * planes + 1,))

    def copy(self, kind, k):
        place, full = self.place, self.full
        plane = place.paired(k)
        column = full.at[place.block(plane, place.a, place.b)]
        if kind == "z":
            source, target = self.own, full.at[place.block(place.z, place.a, place.b)]
            to = place.at(plane, place.core, place.a, place.b)
        elif kind == "a" or kind == "b":
            source, target = (column if k else self.own), column
            to = place.across_a() if kind == "a" else place.across_b()
        elif kind == "d":
            source = target = full.at[place.block(plane, 1 - place.a, place.b)]
            to = place.across_b()
        else:
            cells = place.side * place.side
            source = target = full.at[pl.ds(place.run(plane, place.core), cells)]
            to = place.other_core()
        i = "zabdc".index(kind) * self.planes + k
        return pltpu.make_async_remote_copy(
            src_ref=source, dst_ref=target, send_sem=self.send.at[i], recv_sem=self.recv.at[i],
            device_id=to, device_id_type=MESH,
        )

    def keep(self):
        place = self.place
        return pltpu.make_async_copy(
            self.own, self.full.at[place.block(place.z, place.a, place.b)], self.send.at[5 * self.planes]
        )

    def start_z(self, ways):
        for k in ways:
            self.copy("z", k).start()

    def start_ab(self):
        self.keep().start()
        self.copy("a", 0).start()
        self.copy("b", 0).start()

    def event(self, kind, k):
        if kind == "s":
            self.start_z((k,))
        elif kind == "o":
            self.start_ab()
        elif kind == "z":
            self.copy("z", k).wait_recv()
            self.copy("a", k).start()
            self.copy("b", k).start()
        elif kind == "a":
            self.copy("a", k).wait_recv()
            self.copy("d", k).start()
        elif kind == "b":
            self.copy("b", k).wait_recv()
            self.copy("d", k).wait_recv()
            if k == 0:
                self.keep().wait()
            self.copy("c", k).start()
        else:
            for k in range(self.planes):
                self.copy("c", k).wait_recv()
            for k in range(self.planes):
                for kind in "zabdc" if k else "abdc":
                    self.copy(kind, k).wait_send()


class Rider:
    def __init__(self, place, stages, got, send, recv):
        self.place, self.stages, self.got, self.send, self.recv = place, stages, got, send, recv

    @staticmethod
    def scratch(planes):
        count = 3 + planes
        return [
            pltpu.VMEM((4, 8, D), F32),
            pltpu.VMEM((count, 8, D), F32),
            pltpu.SemaphoreType.DMA((count,)),
            pltpu.SemaphoreType.DMA((count,)),
        ]

    def copy(self, i):
        place = self.place
        to = (place.other_core, place.across_b, place.across_a)[i]() if i < 3 else place.along_z(i - 3)
        return pltpu.make_async_remote_copy(
            src_ref=self.stages.at[min(i, 3)], dst_ref=self.got.at[i], send_sem=self.send.at[i], recv_sem=self.recv.at[i],
            device_id=to, device_id_type=MESH,
        )

    def start(self):
        self.copy(0).start()

    def arrive(self, i):
        self.copy(i).wait_recv()
        self.stages[i + 1] = self.stages[i] + self.got[i]
        if i < 2:
            self.copy(i + 1).start()
        else:
            for k in range(1, self.place.planes):
                self.copy(3 + k).start()

    def finish(self):
        total = self.stages[3]
        for k in range(1, self.place.planes):
            self.copy(3 + k).wait_recv()
            total = total + self.got[3 + k]
        for i in (0, 1, 2):
            self.copy(i).wait_send()
        for k in range(1, self.place.planes):
            self.copy(3 + k).wait_send()
        return total


class Scatter:
    def __init__(self, place, sources, land, ours, got_b, got_a, got_z, mine, load, send, recv):
        self.place, self.sources, self.land, self.ours = place, sources, land, ours
        self.got_b, self.got_a, self.got_z, self.mine = got_b, got_a, got_z, mine
        self.load, self.send, self.recv = load, send, recv
        self.planes, self.side = place.planes, place.side
        self.cells = place.side * place.side
        self.parts = len(sources)
        self.order = list(range(1, self.planes)) + [0]
        self.offsets = [sum(s.shape[1] for s in sources[:i]) for i in range(self.parts + 1)]

    @staticmethod
    def scratch(planes, side, parts, rows):
        cells = side * side
        count = planes * (parts + 4)
        return [
            pltpu.VMEM((planes, cells, rows, D), BF16),
            pltpu.VMEM((2, cells, rows, D), BF16),
            pltpu.VMEM((planes, side, rows, D), BF16),
            pltpu.VMEM((planes, rows, D), BF16),
            pltpu.VMEM((planes, rows, D), BF16),
            pltpu.SemaphoreType.DMA((2, parts)),
            pltpu.SemaphoreType.DMA((count,)),
            pltpu.SemaphoreType.DMA((count,)),
        ]

    def remote(self, slot, source, target, to):
        return pltpu.make_async_remote_copy(
            src_ref=source, dst_ref=target, send_sem=self.send.at[slot], recv_sem=self.recv.at[slot],
            device_id=to, device_id_type=MESH,
        )

    def rows(self, part):
        return pl.ds(self.offsets[part], self.offsets[part + 1] - self.offsets[part])

    def cell(self, a, b):
        return a * self.place.step_a + b * self.place.step_b

    def core_copy(self, k, part):
        place = self.place
        group = pl.ds(place.run(place.plane(k), 1 - place.core), self.cells)
        return self.remote(
            k * self.parts + part, self.sources[part].at[group], self.land.at[k, :, self.rows(part)],
            place.other_core(),
        )

    def load_copy(self, t, part):
        place = self.place
        group = pl.ds(place.run(place.plane(self.order[t]), place.core), self.cells)
        return pltpu.make_async_copy(
            self.sources[part].at[group], self.ours.at[t % 2, :, self.rows(part)], self.load.at[t % 2, part]
        )

    def b_copy(self, k, a):
        place = self.place
        base = self.planes * self.parts
        return self.remote(
            base + 2 * k + a, self.land.at[k, self.cell(a, 1 - place.b)], self.got_b.at[k, a], place.across_b()
        )

    def a_copy(self, k):
        place = self.place
        base = self.planes * (self.parts + 2)
        return self.remote(
            base + k, self.land.at[k, self.cell(1 - place.a, place.b)], self.got_a.at[k], place.across_a()
        )

    def z_copy(self, k):
        place = self.place
        base = self.planes * (self.parts + 3)
        return self.remote(
            base + k, self.land.at[k, self.cell(place.a, place.b)], self.got_z.at[k], place.along_z(k)
        )

    def start(self, part):
        for k in self.order:
            self.core_copy(k, part).start()

    def start_one(self, t):
        self.core_copy(self.order[t], 0).start()

    def load_first(self):
        for part in range(self.parts):
            self.load_copy(0, part).start()

    def arrive_core(self, t):
        k = self.order[t]
        if t + 1 < self.planes:
            for part in range(self.parts):
                self.load_copy(t + 1, part).start()
        for part in range(self.parts):
            self.load_copy(t, part).wait()
            self.core_copy(k, part).wait_recv()

        def add(cell, _):
            self.land[k, cell] = self.land[k, cell] + self.ours[t % 2, cell]
            return 0

        lax.fori_loop(0, self.cells, add, 0)
        for a in range(self.side):
            self.b_copy(k, a).start()

    def arrive_b(self, t):
        k = self.order[t]
        for a in range(self.side):
            self.b_copy(k, a).wait_recv()
            at = self.cell(a, self.place.b)
            self.land[k, at] = self.land[k, at] + self.got_b[k, a]
        self.a_copy(k).start()

    def arrive_a(self, t):
        k = self.order[t]
        self.a_copy(k).wait_recv()
        at = self.cell(self.place.a, self.place.b)
        if k:
            self.land[k, at] = self.land[k, at] + self.got_a[k]
            self.z_copy(k).start()
        else:
            self.mine[...] = self.land[k, at].astype(F32) + self.got_a[k].astype(F32)

    def finish(self):
        for k in range(1, self.planes):
            self.z_copy(k).wait_recv()
            self.mine[...] += self.got_z[k].astype(F32)
        for k in range(self.planes):
            for part in range(self.parts):
                self.core_copy(k, part).wait_send()
            for a in range(self.side):
                self.b_copy(k, a).wait_send()
            self.a_copy(k).wait_send()
            if k:
                self.z_copy(k).wait_send()


def own_blocks(place, wq, wo, wu, wd, small, b_up, own1, own2):
    index = place.run(place.z, place.core) + place.a * place.step_a + place.b * place.step_b

    def spread(size, first):
        lane = lax.broadcasted_iota(jnp.int32, (size, D), 1)
        return jnp.where(lane == first + lax.broadcasted_iota(jnp.int32, (size, D), 0), 1.0, 0.0).astype(BF16)

    per_row = D // UROWS
    vec1 = mm(small[...], spread(OROWS, index * OROWS), 1, 0)
    whole_row = jnp.broadcast_to(b_up[...].astype(F32), (8, UROWS))
    here = lax.broadcasted_iota(jnp.int32, (8, UROWS), 0) == index // per_row
    vec2 = mm(jnp.where(here, whole_row, 0.0).astype(BF16), spread(UROWS, index % per_row * UROWS), 1, 0)
    own1[...] = jnp.concatenate([wq[...].astype(F32), vec1], axis=0).astype(BF16)
    own2[0:UROWS, :] = wu[...]
    down = wd[...].astype(F32)
    rest = [down[:, c * D : (c + 1) * D] for c in range(CHUNKS)] + [wo[...].astype(F32), vec2]
    own2[UROWS:SECOND, :] = jnp.concatenate(rest, axis=0).astype(BF16)


def forward_kernel(planes, side, rows, *refs):
    if planes:
        wq, wo, wu, wd, small, b_up, *refs = refs
    else:
        first_ref, full2, *refs = refs
    (hid_ref, emb_ref, seg_ref, packed_ref, mixed_ref, mid_ref, norm_ref, total_ref, vec_ref, w_qkv, w_out, scaled_ref,
     *refs) = refs
    if planes:
        full2, *refs = refs
    first, tail, bias_col, mask_q, mask_k, load, *refs = refs
    step = pl.program_id(0)
    begin = 2 * rows
    leave = begin + 7 * rows
    row, phase = (step - begin) // 7, (step - begin) % 7
    attending = (step >= begin) & (step < leave)
    tail_copy = pltpu.make_async_copy(full2.at[:, pl.ds(2 * UROWS, 32)], tail, load.at[0])

    if planes:
        own1, own2, send1, recv1, send2, recv2 = refs
        place = Place(planes, side)
        gather1 = Gather(place, own1, first, send1, recv1)
        gather2 = Gather(place, own2, full2, send2, recv2)

        @pl.when(step == 0)
        def _():
            place.arrive()
            own_blocks(place, wq, wo, wu, wd, small, b_up, own1, own2)
            place.meet()
            gather1.start_z(range(1, planes))
            gather1.start_ab()

        @pl.when(step == begin)
        def _():
            for which, kind, k in FIRST_SCHED:
                (gather1, gather2)[which].event(kind, k)

        for at, kind, k in SCHED:
            @pl.when(step == begin + at)
            def _(kind=kind, k=k):
                gather2.event(kind, k)

        @pl.when(step == begin + SCHED[-1][0])
        def _():
            tail_copy.start()
    else:
        @pl.when(step == 0)
        def _():
            tail_copy.start()
            c = pltpu.make_async_copy(first_ref, first, load.at[1])
            c.start()
            c.wait()

    @pl.when(step < begin)
    def _():
        scaled, _ = normalise(hid_ref[...].astype(F32) + emb_ref[...].astype(F32))
        mixed_ref[pl.ds(pl.multiple_of(step * TOKB, TOKB), TOKB), :] = scaled
        scaled_ref[...] = scaled.astype(BF16)

    @pl.when(step == begin)
    def _():
        join_rows(first, 0, QROWS, w_qkv, BLOCKS // 2)
        vec_ref[0] = sum_rows(first, QROWS)
        bias_col[0:D] = column(vec_ref[0, 2:3, :])
        bias_col[D : 2 * D] = jnp.zeros((D, 1), F32)
        bias_col[2 * D : 3 * D] = column(vec_ref[0, 3:4, :])

    tokens = pl.ds(pl.multiple_of(row * ROW, ROW), ROW)

    @pl.when(attending & (phase == 0))
    def _():
        normed = (mixed_ref[tokens, :] * vec_ref[0, 0:1, :] + vec_ref[0, 1:2, :]).astype(BF16)
        packed_ref[...] = (mm(w_qkv[...], normed, 1, 1) + bias_col[...]).astype(BF16)
        query_side, key_side = mask_rows(seg_ref[0])
        mask_q[...] = query_side
        mask_k[...] = key_side

    @pl.when(attending & (phase >= 1))
    def _():
        base = pl.multiple_of((phase - 1) * 128, 128)
        ones_rows = jnp.where(lax.broadcasted_iota(jnp.int32, (HEAD, ROW), 0) == 0, 1.0, 0.0).astype(BF16)
        sides = []
        for h in range(2):
            at = base + HEAD * h
            high, low = scaled_query(packed_ref[pl.ds(at, HEAD), :])
            keys = packed_ref[pl.ds(D + at, HEAD), :]
            sides.append((
                jnp.concatenate([high, low, mask_q[...]], axis=0),
                jnp.concatenate([keys, keys, mask_k[...]], axis=0),
                jnp.concatenate([packed_ref[pl.ds(2 * D + at, HEAD), :], ones_rows], axis=0),
            ))
        all_scores = [mm(sides[h][1], sides[h][0], 0, 0) for h in range(2)]
        mixed = []
        for h in range(2):
            scores = all_scores[h]
            top = jnp.max(scores, axis=0, keepdims=True)
            weights = jnp.exp2(scores - top).astype(BF16)
            summed = mm(sides[h][2], weights, 1, 0)
            total = summed[HEAD : HEAD + 1, :]
            mixed.append(summed[:HEAD, :] / total)
            total_ref[0, h : h + 1, :] = top + jnp.log2(total)
        mixed_ref[tokens, pl.ds(base, 128)] = jnp.concatenate(mixed, axis=0).T

    @pl.when(step == leave)
    def _():
        tail_copy.wait()
        join_rows(tail, 0, OROWS, w_out, BLOCKS // 2)
        vec_ref[1] = sum_rows(tail, OROWS)

    @pl.when(step >= leave)
    def _():
        half = pl.ds(pl.multiple_of((step - leave) * TOKB, TOKB), TOKB)
        entered = hid_ref[...].astype(F32) + emb_ref[...].astype(F32)
        middle = entered + mm(mixed_ref[half, :].astype(BF16), w_out[...], 1, 1) + vec_ref[0, 4:5, :]
        scaled, _ = normalise(middle)
        mid_ref[...] = middle
        norm_ref[...] = (scaled * vec_ref[0, 5:6, :] + vec_ref[0, 6:7, :]).astype(BF16)


def forward(planes, side, weights, hidden, embed, segment):
    n = hidden.shape[0]
    rows = n // ROW
    begin = 2 * rows
    leave_at = begin + 7 * rows
    one = pl.Buffered(1)
    hbm = pl.BlockSpec(memory_space=pl.ANY)

    def row(s):
        return jnp.clip((s - begin) // 7, 0, rows - 1)

    def entry(s):
        return (jnp.where(s < leave_at, jnp.minimum(s, begin - 1), s - leave_at), 0)

    def leave(s):
        return (jnp.maximum(s - leave_at, 0), 0)

    def pair(s):
        return jnp.where(s < leave_at, jnp.maximum((s - begin) % 7 - 1, 0) * (s >= begin), 5)

    entering = pl.BlockSpec((TOKB, D), entry)
    leaving = pl.BlockSpec((TOKB, D), leave)
    out_specs = [
        pl.BlockSpec((3 * D, ROW), lambda s: (0, row(s))),
        pl.BlockSpec((n, D), lambda s: (0, 0), pipeline_mode=one),
        leaving,
        leaving,
        pl.BlockSpec((1, 8, ROW), lambda s: (pair(s), 0, row(s))),
        pl.BlockSpec((2, 8, D), lambda s: (0, 0, 0)),
        pl.BlockSpec((3 * D, D), lambda s: (0, 0), pipeline_mode=one),
        pl.BlockSpec((D, D), lambda s: (0, 0), pipeline_mode=one),
        pl.BlockSpec((TOKB, D), lambda s: (jnp.minimum(s, begin - 1), 0)),
    ]
    out_shape = [
        jax.ShapeDtypeStruct((3 * D, n), BF16),
        jax.ShapeDtypeStruct((n, D), F32),
        jax.ShapeDtypeStruct((n, D), F32),
        jax.ShapeDtypeStruct((n, D), BF16),
        jax.ShapeDtypeStruct((HEADS // 2, 8, n), F32),
        jax.ShapeDtypeStruct((2, 8, D), F32),
        jax.ShapeDtypeStruct((3 * D, D), BF16),
        jax.ShapeDtypeStruct((D, D), BF16),
        jax.ShapeDtypeStruct((n, D), BF16),
    ]
    scratch = [
        pltpu.VMEM((BLOCKS, FIRST, D), BF16),
        pltpu.VMEM((BLOCKS, 32, D), BF16),
        pltpu.VMEM((3 * D, 1), F32),
        pltpu.VMEM((32, ROW), BF16),
        pltpu.VMEM((32, ROW), BF16),
        pltpu.SemaphoreType.DMA((2,)),
    ]
    params = dict(vmem_limit_bytes=56 * MIB)
    if planes:
        in_specs = [pl.BlockSpec(w.shape, lambda s: (0, 0), pipeline_mode=one) for w in weights]
        out_specs.append(hbm)
        out_shape.append(jax.ShapeDtypeStruct((BLOCKS, SECOND, D), BF16))
        scratch += [pltpu.VMEM((FIRST, D), BF16), pltpu.VMEM((SECOND, D), BF16)]
        scratch += [Gather.semaphores(planes)] * 4
        params.update(collective_id=1, has_side_effects=True)
    else:
        in_specs = [hbm, hbm]
    outs = pl.pallas_call(
        partial(forward_kernel, planes, side, rows),
        grid=(leave_at + begin,),
        in_specs=in_specs + [entering, entering, pl.BlockSpec((1, 1, ROW), lambda s: (row(s), 0, 0))],
        out_specs=out_specs,
        out_shape=out_shape,
        scratch_shapes=scratch,
        compiler_params=pltpu.CompilerParams(**params),
        name="attention_forward",
    )(*weights, hidden, embed, segment.reshape(rows, 1, ROW))
    return outs if planes else list(outs) + [weights[1]]


def feed_kernel(
    rows,
    up_ref, down_ref, vec_ref, norm_ref, mid_ref, cot_ref, seg_ref,
    out_ref, gmid_ref, gup_ref, gdown_ref, gvec_ref,
    w_down, result, back, live, active, pre, hold,
):
    step = pl.program_id(0)
    working = step < CHUNKS * rows
    j, i = step // rows, step % rows
    at = pl.ds(pl.multiple_of(i * ROW, ROW), ROW)

    @pl.when(step == 0)
    def _():
        gvec_ref[...] = jnp.zeros_like(gvec_ref)

    for chunk in range(CHUNKS):
        @pl.when(step == chunk * rows)
        def _():
            join_rows(down_ref, chunk % 2 * OROWS, OROWS, w_down, BLOCKS // 2)

    @pl.when(step < rows)
    def _():
        keep = column(jnp.where(seg_ref[0] >= 0, 1.0, 0.0))
        grad_result = cot_ref[...].astype(F32) * keep
        live[at, :] = grad_result.astype(BF16)
        gvec_ref[4:5, :] += jnp.sum(grad_result, axis=0, keepdims=True)

    @pl.when(working)
    def _():
        up = up_ref[...].reshape(D, D)
        down = w_down[...]
        x = mm(norm_ref[at, :], up, 1, 1) + vec_ref[1, pl.ds(j, 1), :]
        grad_act = mm(live[at, :], down, 1, 0)
        c0 = math.sqrt(2.0 / math.pi)
        c1 = 0.044715
        square = x * x
        th = jnp.tanh(x * (c0 + (c0 * c1) * square))
        half = 0.5 + 0.5 * th
        slope = half + (0.5 * x) * ((1.0 - th * th) * (c0 + (3 * c0 * c1) * square))
        activated = (x * half).astype(BF16)
        grad_pre = (grad_act * slope).astype(BF16)
        active[at, :] = activated
        pre[at, :] = grad_pre
        gvec_ref[pl.ds(j, 1), :] += jnp.sum(grad_pre.astype(F32), axis=0, keepdims=True)

        @pl.when(j == 0)
        def _():
            result[at, :] = mm(activated, down, 1, 1)
            back[at, :] = mm(grad_pre, up, 1, 0)

        @pl.when(j > 0)
        def _():
            result[at, :] += mm(activated, down, 1, 1)
            back[at, :] += mm(grad_pre, up, 1, 0)

    @pl.when(working & (i == rows - 1))
    def _():
        gup_ref[...] = mm(pre[...], norm_ref[...], 0, 0).astype(BF16)
        part_down = mm(live[...], active[...], 0, 0)

        hold[...] = part_down

        @pl.when(j % 2 == 0)
        def _():
            def pack(d, _):
                own = pl.ds(pl.multiple_of(d * OROWS, 8), OROWS)
                gdown_ref[d] = jnp.concatenate([hold[own], jnp.zeros((OROWS, D), F32)], axis=0).astype(BF16)
                return 0

            lax.fori_loop(0, BLOCKS, pack, 0)

        @pl.when(j % 2 == 1)
        def _():
            def pack(d, _):
                own = pl.ds(pl.multiple_of(d * OROWS, 8), OROWS)
                kept = gdown_ref[d].astype(F32)[:OROWS]
                gdown_ref[d] = jnp.concatenate([kept, hold[own]], axis=0).astype(BF16)
                return 0

            lax.fori_loop(0, BLOCKS, pack, 0)

    @pl.when(step >= CHUNKS * rows)
    def _():
        tokens = pl.ds(pl.multiple_of((step - CHUNKS * rows) * TOKB, TOKB), TOKB)
        middle = mid_ref[...]
        out_ref[...] = (middle + (result[tokens, :] + vec_ref[0, 7:8, :])).astype(BF16)
        grad = back[tokens, :]
        scaled, inverse = normalise(middle)
        gvec_ref[5:6, :] += jnp.sum(grad * scaled, axis=0, keepdims=True)
        gvec_ref[6:7, :] += jnp.sum(grad, axis=0, keepdims=True)
        gmid_ref[...] = live[tokens, :].astype(F32) + norm_back(grad, scaled, inverse, vec_ref[0, 5:6, :])


def feed(second, vec, normed, middle, cotangent, segment):
    n = normed.shape[0]
    rows = n // ROW
    one = pl.Buffered(1)

    def chunk(s):
        return jnp.minimum(s // rows, CHUNKS - 1)

    def late(s):
        return (jnp.maximum(s - CHUNKS * rows, 0), 0)

    leaving = pl.BlockSpec((TOKB, D), late)
    return pl.pallas_call(
        partial(feed_kernel, rows),
        grid=(CHUNKS * rows + n // TOKB,),
        in_specs=[
            pl.BlockSpec((BLOCKS // CHUNKS, UROWS, D), lambda s: (chunk(s), 0, 0)),
            pl.BlockSpec((BLOCKS, 2 * OROWS, D), lambda s: (0, 2 + chunk(s) // 2, 0), pipeline_mode=one),
            pl.BlockSpec((2, 8, D), lambda s: (0, 0, 0)),
            pl.BlockSpec((n, D), lambda s: (0, 0), pipeline_mode=one),
            leaving,
            pl.BlockSpec((ROW, D), lambda s: (jnp.minimum(s, rows - 1), 0), pipeline_mode=one),
            pl.BlockSpec((1, 1, ROW), lambda s: (jnp.minimum(s, rows - 1), 0, 0)),
        ],
        out_specs=[
            leaving,
            leaving,
            pl.BlockSpec((D, D), lambda s: (chunk(s), 0)),
            pl.BlockSpec((BLOCKS, 2 * OROWS, D), lambda s: (0, chunk(s) // 2, 0), pipeline_mode=one),
            pl.BlockSpec((8, D), lambda s: (0, 0)),
        ],
        out_shape=[
            jax.ShapeDtypeStruct((n, D), BF16),
            jax.ShapeDtypeStruct((n, D), F32),
            jax.ShapeDtypeStruct((FF, D), BF16),
            jax.ShapeDtypeStruct((BLOCKS, UROWS, D), BF16),
            jax.ShapeDtypeStruct((8, D), F32),
        ],
        scratch_shapes=[
            pltpu.VMEM((D, D), BF16),
            pltpu.VMEM((n, D), F32),
            pltpu.VMEM((n, D), F32),
            pltpu.VMEM((n, D), BF16),
            pltpu.VMEM((n, D), BF16),
            pltpu.VMEM((n, D), BF16),
            pltpu.VMEM((D, D), F32),
        ],
        compiler_params=pltpu.CompilerParams(vmem_limit_bytes=60 * MIB),
        name="feed_forward",
    )(second, second, vec, normed, middle, cotangent, segment.reshape(rows, 1, ROW))


def three_parts(row):
    r = lax.broadcasted_iota(jnp.int32, (16, row.shape[1]), 0)
    a = row.astype(BF16).astype(F32)
    b = (row - a).astype(BF16).astype(F32)
    c = row - a - b
    return jnp.where(r == 0, -a, jnp.where(r == 1, -b, jnp.where(r == 2, -c, 0.0))).astype(BF16)


def backward_kernel(
    planes, side, rows,
    w_out, seg_ref, packed_q, packed_k, packed_v, mixed_ref, total_ref, gmid_ref, gvec_ref, gup_ref, gdown_ref,
    gpacked_ref, sums_ref, *rest,
):
    if planes:
        up_out, down_out, out_out, vec_out, mask_q, mask_k, grad_mixed, delta, sum_out, sum_bias, tail, mine, *transfer = rest
    else:
        tail, mask_q, mask_k, grad_mixed, delta, sum_out, sum_bias = rest
    step = pl.program_id(0)
    entry = 2 * rows
    heads = step >= entry

    if planes:
        place = Place(planes, side)
        scatter = Scatter(place, (gup_ref, gdown_ref, tail), *transfer[:5], mine, *transfer[5:])

        @pl.when(step == 0)
        def _():
            place.arrive()

        @pl.when(step == 1)
        def _():
            place.meet()
            scatter.start(0)
            scatter.start(1)

        @pl.when(step == entry)
        def _():
            scatter.start(2)
            scatter.load_first()

        for at, t, act in BACK:
            @pl.when(step == entry + at)
            def _(t=t, act=act):
                getattr(scatter, act)(t)

    @pl.when(step == 0)
    def _():
        sum_out[...] = jnp.zeros_like(sum_out)
        sum_bias[...] = jnp.zeros_like(sum_bias)

    @pl.when(step < entry)
    def _():
        at = pl.ds(pl.multiple_of(step * TOKB, TOKB), TOKB)
        mixed = mixed_ref[...]
        branch = gmid_ref[...].astype(BF16)
        sum_bias[0:1, :] += jnp.sum(branch.astype(F32), axis=0, keepdims=True)
        sum_out[...] += mm(branch, mixed.astype(BF16), 0, 0)
        grad = mm(branch, w_out[...], 1, 0).astype(BF16).astype(F32)
        grad_mixed[:, at] = grad.T.astype(BF16)
        inner = (grad * mixed).T
        delta[:, at] = jnp.concatenate(
            [jnp.sum(inner[HEAD * h : HEAD * (h + 1)], axis=0, keepdims=True) for h in range(HEADS)]
            + [jnp.zeros((16 - HEADS, TOKB), F32)],
            axis=0,
        )

    @pl.when(step == entry - 1)
    def _():
        r = lax.broadcasted_iota(jnp.int32, (8, D), 0)
        vectors = jnp.where(r == 7, sum_bias[0:1, :], gvec_ref[...])

        def pack(d, _):
            at = pl.ds(pl.multiple_of(d * OROWS, 8), OROWS)
            tail[d] = jnp.concatenate([sum_out[at, :], vectors], axis=0).astype(BF16)
            return 0

        lax.fori_loop(0, BLOCKS, pack, 0)

    row, pair = (step - entry) // 6, (step - entry) % 6

    @pl.when(heads & (pair == 0))
    def _():
        query_side, key_side = mask_rows(seg_ref[0])
        mask_q[...] = query_side
        mask_k[...] = key_side

    @pl.when(heads)
    def _():
        tokens = pl.ds(pl.multiple_of(row * ROW, ROW), ROW)
        r = lax.broadcasted_iota(jnp.int32, (16, ROW), 0)
        ones_rows = jnp.where(r < 3, 1.0, 0.0).astype(BF16)
        base = pl.multiple_of(pair * 128, 128)
        column_sums = []
        for h in range(2):
            at_rows = slice(HEAD * h, HEAD * (h + 1))
            queries, keys, values = packed_q[at_rows, :], packed_k[at_rows, :], packed_v[at_rows, :]
            grad = grad_mixed[pl.ds(base + HEAD * h, HEAD), tokens]
            high, low = scaled_query(queries)
            wide_q = jnp.concatenate([high, low, mask_q[...], three_parts(total_ref[0, h : h + 1, :])], axis=0)
            wide_k = jnp.concatenate([keys, keys, mask_k[...], ones_rows], axis=0)
            wide_g = jnp.concatenate([grad, three_parts(delta[pl.ds(2 * pair + h, 1), tokens])], axis=0)
            wide_v = jnp.concatenate([values, ones_rows], axis=0)
            grad_v = jnp.zeros((HEAD, ROW), F32)
            grad_k = jnp.zeros((HEAD, ROW), F32)
            grad_q = []
            for half in range(2):
                at = slice(half * (ROW // 2), (half + 1) * (ROW // 2))
                probs = jnp.exp2(mm(wide_q[:, at], wide_k, 0, 0))
                grad_probs = mm(wide_g[:, at], wide_v, 0, 0)
                grad_scores = (probs * grad_probs).astype(BF16)
                grad_v = grad_v + mm(grad[:, at], probs.astype(BF16), 1, 0)
                grad_k = grad_k + mm(queries[:, at], grad_scores, 1, 0)
                grad_q.append(mm(keys, grad_scores, 1, 1))
            grads = (
                (jnp.concatenate(grad_q, axis=1) * 0.125).astype(BF16),
                (grad_k * 0.125).astype(BF16),
                grad_v.astype(BF16),
            )
            for part in range(3):
                gpacked_ref[pl.ds(part * D + base + HEAD * h, HEAD), :] = grads[part]
            column_sums.append([jnp.sum(g.astype(F32), axis=1, keepdims=True) for g in grads])
        for part in range(3):
            both = jnp.concatenate([column_sums[0][part], column_sums[1][part]], axis=0)
            at = pl.ds(part * D + base, 128)

            @pl.when(row == 0)
            def _():
                sums_ref[at, :] = both

            @pl.when(row > 0)
            def _():
                sums_ref[at, :] += both

    if planes:
        @pl.when(step == entry + 6 * rows - 1)
        def _():
            scatter.finish()
            up_out[...] = mine[0:UROWS, :]
            for c in range(CHUNKS):
                down_out[:, c * D : (c + 1) * D] = mine[UROWS + c * OROWS : UROWS + (c + 1) * OROWS, :]
            out_out[...] = mine[2 * UROWS : 2 * UROWS + OROWS, :]
            vec_out[...] = mine[2 * UROWS + OROWS : 2 * UROWS + 32, :]


def backward(planes, side, w_out, segment, packed, mixed, totals, gmid, gvec, gup, gdown):
    n = mixed.shape[0]
    rows = n // ROW
    entry = 2 * rows
    one = pl.Buffered(1)
    hbm = pl.BlockSpec(memory_space=pl.ANY)

    def early(s):
        return (jnp.minimum(s, entry - 1), 0)

    def row(s):
        return jnp.maximum(s - entry, 0) // 6

    def pair(s):
        return jnp.maximum(s - entry, 0) % 6

    def heads(part):
        return pl.BlockSpec((128, ROW), lambda s: (6 * part + pair(s), row(s)))

    out_specs = [
        pl.BlockSpec((3 * D, ROW), lambda s: (0, row(s))),
        pl.BlockSpec((3 * D, 1), lambda s: (0, 0), pipeline_mode=one),
    ]
    out_shape = [jax.ShapeDtypeStruct((3 * D, n), BF16), jax.ShapeDtypeStruct((3 * D, 1), F32)]
    scratch = [
        pltpu.VMEM((32, ROW), BF16),
        pltpu.VMEM((32, ROW), BF16),
        pltpu.VMEM((D, n), BF16),
        pltpu.VMEM((16, n), F32),
        pltpu.VMEM((D, D), F32),
        pltpu.VMEM((8, D), F32),
    ]
    params = dict(vmem_limit_bytes=56 * MIB)
    if planes:
        rows1 = 2 * UROWS + 32
        for shape in ((UROWS, D), (OROWS, FF), (OROWS, D), (8, D)):
            out_specs.append(pl.BlockSpec(shape, lambda s: (0, 0), pipeline_mode=one))
            out_shape.append(jax.ShapeDtypeStruct(shape, F32))
        scratch += [pltpu.VMEM((BLOCKS, 32, D), BF16), pltpu.VMEM((rows1, D), F32)]
        scratch += Scatter.scratch(planes, side, 3, rows1)
        params.update(collective_id=2, has_side_effects=True)
    else:
        out_specs.append(pl.BlockSpec((BLOCKS, 32, D), lambda s: (0, 0, 0), pipeline_mode=one))
        out_shape.append(jax.ShapeDtypeStruct((BLOCKS, 32, D), BF16))
    return pl.pallas_call(
        partial(backward_kernel, planes, side, rows),
        grid=(entry + 6 * rows,),
        in_specs=[
            pl.BlockSpec((D, D), lambda s: (0, 0), pipeline_mode=one),
            pl.BlockSpec((1, 1, ROW), lambda s: (row(s), 0, 0)),
            heads(0),
            heads(1),
            heads(2),
            pl.BlockSpec((TOKB, D), early),
            pl.BlockSpec((1, 8, ROW), lambda s: (pair(s), 0, row(s))),
            pl.BlockSpec((TOKB, D), early),
            pl.BlockSpec((8, D), lambda s: (0, 0)),
            hbm,
            hbm,
        ],
        out_specs=out_specs,
        out_shape=out_shape,
        scratch_shapes=scratch,
        compiler_params=pltpu.CompilerParams(**params),
        name="attention_backward",
    )(w_out, segment.reshape(rows, 1, ROW), packed, packed, packed, mixed, totals, gmid, gvec, gup, gdown)


def enter_kernel(
    planes, side, blocks,
    w_hbm, vec_ref, hid_ref, emb_ref, gmid_ref, grad_hbm, sums_ref, scaled_hbm,
    ghid_ref, out_ref, *rest,
):
    if planes:
        vec_out, scaled_all, w_qkv, grad_packed, totals, load, packed, mine, *transfer = rest
    else:
        packed, (scaled_all, w_qkv, grad_packed, totals, load) = out_ref, rest
    step = pl.program_id(0)
    chunks = 4
    size = 3 * D // chunks
    begin, late = 0, chunks
    if planes:
        place = Place(planes, side)

    def chunk_of(t):
        return place.plane(t + 1) if planes else t

    def grad_load(t):
        rows = pl.ds(pl.multiple_of(chunk_of(t) * size, size), size)
        return pltpu.make_async_copy(grad_hbm.at[rows], grad_packed.at[rows], load.at[t])

    loads = [
        pltpu.make_async_copy(scaled_hbm, scaled_all, load.at[chunks]),
        pltpu.make_async_copy(w_hbm, w_qkv, load.at[chunks + 1]),
    ]

    if planes:
        rider = Rider(place, *transfer[:4])
        scatter = Scatter(place, (packed,), *transfer[4:9], mine, *transfer[9:])

    @pl.when(step == 0)
    def _():
        loads[0].start()
        grad_load(0).start()
        loads[1].start()
        for t in range(1, chunks):
            grad_load(t).start()
        totals[...] = jnp.zeros_like(totals)
        if planes:
            place.arrive()

    def entering():
        return normalise(hid_ref[...].astype(F32) + emb_ref[...].astype(F32))

    @pl.when(step == begin)
    def _():
        for c in loads:
            c.wait()
        if planes:
            place.meet()

    for t in range(chunks):
        @pl.when(step == t)
        def _(t=t):
            grad_load(t).wait()

    if planes:
        for at, t, act in ENTER:
            @pl.when(step == begin + at)
            def _(t=t, act=act):
                getattr(scatter, act)(t)
                if t == planes - 1:
                    rider.arrive(("arrive_core", "arrive_b", "arrive_a").index(act))

    @pl.when((step >= begin) & (step < late))
    def _():
        t = step - begin
        chunk = chunk_of(t)
        at = pl.ds(pl.multiple_of(chunk * size, size), size)
        product = mm(grad_packed[at, :], scaled_all[...], 1, 0)
        weight = w_qkv[at, :].astype(F32)
        sums = sums_ref[at, :]
        totals[0:1, :] += jnp.sum(weight * product, axis=0, keepdims=True)
        totals[1:2, :] += jnp.sum(weight * sums, axis=0, keepdims=True)
        grad_w = product * vec_ref[0, 0:1, :] + sums * vec_ref[0, 1:2, :]
        count = BLOCKS // chunks
        for i in range(count):
            rows = [grad_w[i * QROWS : (i + 1) * QROWS], jnp.zeros((8, D), F32)]
            packed[chunk * count + i] = jnp.concatenate(rows, axis=0).astype(BF16)

    if planes:
        for t in range(planes):
            @pl.when(step == begin + t)
            def _(t=t):
                if t == 0:
                    scatter.load_first()
                scatter.start_one(t)

    @pl.when(step == late - 1)
    def _():
        ends = [jnp.broadcast_to(sums_ref[at : at + D, :], (D, 128)).T[0:1, :] for at in (0, 2 * D)]
        vectors = jnp.concatenate([totals[0:2, :]] + ends + [jnp.zeros((4, D), F32)], axis=0)
        if planes:
            rider.stages[0] = vectors
            rider.start()
        else:
            kept = packed[0, QROWS - 8 : QROWS + 8, :].astype(F32)[:8]
            packed[0, QROWS - 8 : QROWS + 8, :] = jnp.concatenate([kept, vectors], axis=0).astype(BF16)

    @pl.when(step >= late)
    def _():
        at = pl.ds(pl.multiple_of((step - late) * TOKB, TOKB), TOKB)
        scaled, inverse = entering()
        grad = mm(grad_packed[:, at], w_qkv[...], 0, 0)
        ghid_ref[...] = (gmid_ref[...] + norm_back(grad, scaled, inverse, vec_ref[0, 0:1, :])).astype(BF16)

    if planes:
        @pl.when(step == late + blocks - 1)
        def _():
            for t, act in ENTER_LAST:
                getattr(scatter, act)(t)
                if t == planes - 1:
                    rider.arrive(("arrive_core", "arrive_b", "arrive_a").index(act))
            scatter.finish()
            out_ref[...] = mine[0:QROWS, :]
            vec_out[...] = rider.finish()


def enter(planes, side, w_qkv, vec, hidden, embed, gmid, gpacked, sums, scaled):
    n = hidden.shape[0]
    blocks = n // TOKB
    late_at = 4
    one = pl.Buffered(1)
    hbm = pl.BlockSpec(memory_space=pl.ANY)

    def late(s):
        return (jnp.maximum(s - late_at, 0), 0)

    tokens = pl.BlockSpec((TOKB, D), late)
    out_specs = [pl.BlockSpec((TOKB, D), late)]
    out_shape = [jax.ShapeDtypeStruct((n, D), BF16)]
    scratch = [
        pltpu.VMEM((n, D), BF16),
        pltpu.VMEM((3 * D, D), BF16),
        pltpu.VMEM((3 * D, n), BF16),
        pltpu.VMEM((8, D), F32),
        pltpu.SemaphoreType.DMA((6,)),
    ]
    params = dict(vmem_limit_bytes=56 * MIB)
    if planes:
        for shape in ((QROWS, D), (8, D)):
            out_specs.append(pl.BlockSpec(shape, lambda s: (0, 0), pipeline_mode=one))
            out_shape.append(jax.ShapeDtypeStruct(shape, F32))
        scratch += [pltpu.VMEM((BLOCKS, FIRST, D), BF16), pltpu.VMEM((FIRST, D), F32)]
        scratch += Rider.scratch(planes) + Scatter.scratch(planes, side, 1, FIRST)
        params.update(collective_id=3, has_side_effects=True)
    else:
        out_specs.append(pl.BlockSpec((BLOCKS, FIRST, D), lambda s: (0, 0, 0), pipeline_mode=one))
        out_shape.append(jax.ShapeDtypeStruct((BLOCKS, FIRST, D), BF16))
    return pl.pallas_call(
        partial(enter_kernel, planes, side, blocks),
        grid=(late_at + blocks,),
        in_specs=[
            hbm,
            pl.BlockSpec((2, 8, D), lambda s: (0, 0, 0)),
            tokens,
            tokens,
            pl.BlockSpec((TOKB, D), late),
            hbm,
            pl.BlockSpec((3 * D, 1), lambda s: (0, 0), pipeline_mode=one),
            hbm,
        ],
        out_specs=out_specs,
        out_shape=out_shape,
        scratch_shapes=scratch,
        compiler_params=pltpu.CompilerParams(**params),
        name="projection_backward",
    )(w_qkv, vec, hidden, embed, gmid, gpacked, sums, scaled)


def body(
    planes, side, devices,
    hidden, time_embed, segment_ids,
    ln1_gain, ln1_bias, w_qkv, b_query, b_value, w_out, b_out, ln2_gain, ln2_bias, w_up, b_up, w_down, b_down,
    cotangent,
):
    index = lax.axis_index("dp") * lax.axis_size("fsdp") + lax.axis_index("fsdp")
    axes = ("dp", "fsdp")
    small = (ln1_gain, ln1_bias, b_query, b_value, b_out, ln2_gain, ln2_bias, b_down)
    if planes:
        weights = (w_qkv.T, w_out.T, w_up.T, w_down.T, jnp.stack(small), b_up[None, :])
    else:
        def whole(a, dim):
            return lax.all_gather(a, axes, axis=dim, tiled=True)

        def only_first(rows):
            return jnp.concatenate([rows[None], jnp.zeros((BLOCKS - 1,) + rows.shape, BF16)], axis=0)

        vec1 = jnp.stack([whole(v, 0) for v in small])
        vec2 = jnp.concatenate([whole(b_up, 0).reshape(CHUNKS, D), jnp.zeros((8 - CHUNKS, D), BF16)], axis=0)
        down_rows = whole(w_down, 1).T.reshape(BLOCKS, OROWS, CHUNKS, D).transpose(0, 2, 1, 3)
        first = jnp.concatenate([whole(w_qkv, 1).T.reshape(BLOCKS, QROWS, D), only_first(vec1)], axis=1)
        second = jnp.concatenate(
            [
                whole(w_up, 1).T.reshape(BLOCKS, UROWS, D),
                down_rows.reshape(BLOCKS, UROWS, D),
                whole(w_out, 1).T.reshape(BLOCKS, OROWS, D),
                only_first(vec2),
            ],
            axis=1,
        )
        weights = (first, second)
    packed, mixed, middle, normed, totals, vec, full_qkv, full_out, scaled, second = forward(
        planes, side, weights, hidden, time_embed, segment_ids
    )
    output, gmid, gup, gdown, gvec = feed(second, vec, normed, middle, cotangent, segment_ids)
    gup = gup.reshape(BLOCKS, UROWS, D)
    gpacked, sums, *late = backward(
        planes, side, full_out, segment_ids, packed, mixed, totals, gmid, gvec, gup, gdown
    )
    ghid, *last = enter(planes, side, full_qkv, vec, hidden, time_embed, gmid, gpacked, sums, scaled)
    if planes:
        part_up, part_down, part_out, vectors = late
        part_qkv, vectors_qkv = last
        vectors = jnp.concatenate([vectors, vectors_qkv], axis=0)
        short = lax.dynamic_slice(vectors, (0, index * OROWS), (16, OROWS))
        part_bup = lax.dynamic_slice(vectors[:CHUNKS].reshape(-1), (index * UROWS,), (UROWS,))
    else:
        def shared(a, dim):
            return lax.psum_scatter(a.astype(F32), axes, scatter_dimension=dim, tiled=True)

        (late,), (last,) = late, last
        part_up = shared(gup.reshape(FF, D), 0)
        part_down = shared(gdown.reshape(BLOCKS, CHUNKS, OROWS, D).transpose(0, 2, 1, 3).reshape(D, FF), 0)
        part_out = shared(late[:, :OROWS].reshape(D, D), 0)
        part_qkv = shared(last[:, :QROWS].reshape(3 * D, D), 0)
        vectors = jnp.concatenate([late[0, OROWS:], last[0, QROWS:]], axis=0)
        short = shared(vectors, 1)
        part_bup = shared(vectors[:CHUNKS].reshape(-1), 0)
    return (
        output, ghid,
        short[8], short[9], part_qkv.T, short[10], short[11], part_out.T, short[7],
        short[5], short[6], part_up.T, part_bup, part_down.T, short[4],
    )


def solution(mesh):
    groups, cells = mesh.shape["dp"], mesh.shape["fsdp"]
    side = math.isqrt(cells)
    own_transfers = groups * cells == BLOCKS and side == 2 and cells == 4 and groups % 2 == 0
    split = ("dp", "fsdp")
    rows, flat, cols = P(split, None), P(split), P(None, split)
    return jax.shard_map(
        partial(body, groups // 2 if own_transfers else 0, side, groups * cells),
        mesh=mesh,
        in_specs=(
            rows, rows, flat, flat, flat, cols, flat, flat, cols, flat, flat, flat, cols, flat, cols, flat, rows,
        ),
        out_specs=(
            rows, rows, flat, flat, cols, flat, flat, cols, flat, flat, flat, cols, flat, cols, flat,
        ),
        check_vma=False,
    )
```

```python
from functools import partial
import math

import jax
import jax.numpy as jnp
from jax import lax
from jax.experimental import pallas as pl
from jax.experimental.pallas import tpu as pltpu
from jax.sharding import PartitionSpec as P

D = 768
HEADS = 12
HEAD = 64
FF = 3072
ROW = 1024
BLOCKS = 32
QROWS = 3 * D // BLOCKS
OROWS = D // BLOCKS
UROWS = FF // BLOCKS
CHUNKS = FF // D
FIRST = QROWS + 8
SECOND = 2 * UROWS + OROWS + 8
TOKB = 512
MIB = 2**20
MESH = pl.DeviceIdType.MESH
F32 = jnp.float32
BF16 = jnp.bfloat16
LOG2E = math.log2(math.e)
EPS = 1e-05
FIRST_SCHED = (
    (0, "z", 1), (0, "a", 0), (0, "z", 2), (0, "a", 1), (0, "z", 3), (1, "s", 1), (1, "s", 2), (0, "b", 0), (0, "a", 2),
    (0, "b", 1), (0, "a", 3), (1, "o", 0), (0, "b", 2), (0, "b", 3), (0, "end", 0),
)
SCHED = (
    (0, "z", 1), (0, "s", 3), (1, "a", 0), (2, "a", 1), (2, "z", 2), (3, "b", 0), (5, "a", 2), (6, "z", 3), (6, "b", 1),
    (9, "a", 3), (9, "b", 2), (12, "b", 3), (13, "end", 0),
)
BACK = (
    (1, 0, "arrive_core"), (2, 1, "arrive_core"), (3, 0, "arrive_b"), (4, 2, "arrive_core"), (5, 1, "arrive_b"),
    (5, 0, "arrive_a"), (6, 3, "arrive_core"), (7, 2, "arrive_b"), (8, 1, "arrive_a"), (9, 3, "arrive_b"),
    (9, 2, "arrive_a"), (11, 3, "arrive_a"),
)
ENTER = (
    (2, 0, "arrive_core"), (3, 1, "arrive_core"), (4, 0, "arrive_b"), (4, 2, "arrive_core"), (5, 1, "arrive_b"),
    (5, 3, "arrive_core"), (6, 0, "arrive_a"), (6, 2, "arrive_b"), (7, 1, "arrive_a"), (7, 3, "arrive_b"),
)
ENTER_LAST = ((2, "arrive_a"), (3, "arrive_a"))


def mm(a, b, ca, cb):
    return lax.dot_general(a, b, (((ca,), (cb,)), ((), ())), preferred_element_type=F32)


def normalise(values):
    centred = values - jnp.mean(values, axis=-1, keepdims=True)
    inverse = lax.rsqrt(jnp.mean(centred * centred, axis=-1, keepdims=True) + EPS)
    return centred * inverse, inverse


def norm_back(grad, scaled, inverse, gain):
    u = grad * gain
    return inverse * (
        u
        - jnp.mean(u, axis=-1, keepdims=True)
        - scaled * jnp.mean(u * scaled, axis=-1, keepdims=True)
    )


def column(row):
    return jnp.broadcast_to(row, (128, row.shape[1])).T[:, :1]


def join_rows(source, start, rows, target, pairs):
    low = start // 16 * 16
    high = -(-(start + rows) // 16) * 16

    def step(p, _):
        parts = [
            source[2 * p + i, low:high, :].astype(F32)[start - low : start - low + rows]
            for i in range(2)
        ]
        at = pl.multiple_of(2 * rows * p, 2 * rows)
        target[pl.ds(at, 2 * rows), :] = jnp.concatenate(parts, axis=0).astype(BF16)
        return 0

    lax.fori_loop(0, pairs, step, 0)


def sum_rows(source, start):
    low = start // 16 * 16

    def step(d, total):
        return total + source[d, low : low + 16, :].astype(F32)[start - low : start - low + 8]

    return lax.fori_loop(0, BLOCKS, step, jnp.zeros((8, D), F32))


def mask_rows(segment):
    r = lax.broadcasted_iota(jnp.int32, (32, ROW), 0)
    hit = r == segment + 1
    query_side = jnp.where(hit, 1.0, 0.0).astype(BF16)
    key_side = jnp.where(hit | (r >= 17), 0.0, -1e30).astype(BF16)
    return query_side, key_side


def scaled_query(queries):
    wide = queries.astype(F32) * (LOG2E / 8)
    high = wide.astype(BF16)
    rest = wide - high.astype(F32)
    low = rest.astype(BF16)
    return [high, low, (rest - low.astype(F32)).astype(BF16)]


class Place:
    def __init__(self, planes, side):
        self.planes, self.side = planes, side
        group, cell = lax.axis_index("dp"), lax.axis_index("fsdp")
        self.z, self.core = group // 2, group % 2
        y, x = cell // side, cell % side
        self.step_a = 1 + self.core * (side - 1)
        self.step_b = side - self.core * (side - 1)
        self.a = x + self.core * (y - x)
        self.b = y + self.core * (x - y)

    def plane(self, k):
        return lax.rem(self.z + k + self.planes, self.planes)

    def paired(self, k):
        plane, bit = self.z, 1
        while bit <= k:
            if k & bit:
                plane = plane + bit - 2 * bit * (self.z // bit % 2)
            bit *= 2
        return plane

    def at(self, z, core, a, b):
        return (z * 2 + core, a * self.step_a + b * self.step_b)

    def block(self, z, a, b):
        return (z * 2 + self.core) * (self.side * self.side) + a * self.step_a + b * self.step_b

    def run(self, z, core):
        return (z * 2 + core) * (self.side * self.side)

    def across_a(self):
        return self.at(self.z, self.core, 1 - self.a, self.b)

    def across_b(self):
        return self.at(self.z, self.core, self.a, 1 - self.b)

    def other_core(self):
        return (self.z * 2 + 1 - self.core, self.a * self.step_a + self.b * self.step_b)

    def along_z(self, k):
        return self.at(self.plane(k), self.core, self.a, self.b)

    def arrive(self):
        barrier = pltpu.get_barrier_semaphore()
        peers = [self.along_z(k) for k in range(1, self.planes)]
        peers += [self.across_a(), self.across_b(), self.other_core()]
        for peer in peers:
            pl.semaphore_signal(barrier, inc=1, device_id=peer, device_id_type=MESH)

    def meet(self):
        pl.semaphore_wait(pltpu.get_barrier_semaphore(), self.planes + 2)


class Gather:
    def __init__(self, place, own, full, send, recv):
        self.place, self.own, self.full, self.send, self.recv = place, own, full, send, recv
        self.planes = place.planes

    @staticmethod
    def semaphores(planes):
        return pltpu.SemaphoreType.DMA((5 * planes + 1,))

    def copy(self, kind, k):
        place, full = self.place, self.full
        plane = place.paired(k)
        column = full.at[place.block(plane, place.a, place.b)]
        if kind == "z":
            source, target = self.own, full.at[place.block(place.z, place.a, place.b)]
            to = place.at(plane, place.core, place.a, place.b)
        elif kind == "a" or kind == "b":
            source, target = (column if k else self.own), column
            to = place.across_a() if kind == "a" else place.across_b()
        elif kind == "d":
            source = target = full.at[place.block(plane, 1 - place.a, place.b)]
            to = place.across_b()
        else:
            cells = place.side * place.side
            source = target = full.at[pl.ds(place.run(plane, place.core), cells)]
            to = place.other_core()
        i = "zabdc".index(kind) * self.planes + k
        return pltpu.make_async_remote_copy(
            src_ref=source, dst_ref=target, send_sem=self.send.at[i], recv_sem=self.recv.at[i],
            device_id=to, device_id_type=MESH,
        )

    def keep(self):
        place = self.place
        return pltpu.make_async_copy(
            self.own, self.full.at[place.block(place.z, place.a, place.b)], self.send.at[5 * self.planes]
        )

    def start_z(self, ways):
        for k in ways:
            self.copy("z", k).start()

    def start_ab(self):
        self.keep().start()
        self.copy("a", 0).start()
        self.copy("b", 0).start()

    def event(self, kind, k):
        if kind == "s":
            self.start_z((k,))
        elif kind == "o":
            self.start_ab()
        elif kind == "z":
            self.copy("z", k).wait_recv()
            self.copy("a", k).start()
            self.copy("b", k).start()
        elif kind == "a":
            self.copy("a", k).wait_recv()
            self.copy("d", k).start()
        elif kind == "b":
            self.copy("b", k).wait_recv()
            self.copy("d", k).wait_recv()
            if k == 0:
                self.keep().wait()
            self.copy("c", k).start()
        else:
            for k in range(self.planes):
                self.copy("c", k).wait_recv()
            for k in range(self.planes):
                for kind in "zabdc" if k else "abdc":
                    self.copy(kind, k).wait_send()


class Rider:
    def __init__(self, place, stages, got, send, recv):
        self.place, self.stages, self.got, self.send, self.recv = place, stages, got, send, recv

    @staticmethod
    def scratch(planes):
        count = 3 + planes
        return [
            pltpu.VMEM((4, 8, D), F32),
            pltpu.VMEM((count, 8, D), F32),
            pltpu.SemaphoreType.DMA((count,)),
            pltpu.SemaphoreType.DMA((count,)),
        ]

    def copy(self, i):
        place = self.place
        to = (place.other_core, place.across_b, place.across_a)[i]() if i < 3 else place.along_z(i - 3)
        return pltpu.make_async_remote_copy(
            src_ref=self.stages.at[min(i, 3)], dst_ref=self.got.at[i], send_sem=self.send.at[i], recv_sem=self.recv.at[i],
            device_id=to, device_id_type=MESH,
        )

    def start(self):
        self.copy(0).start()

    def arrive(self, i):
        self.copy(i).wait_recv()
        self.stages[i + 1] = self.stages[i] + self.got[i]
        if i < 2:
            self.copy(i + 1).start()
        else:
            for k in range(1, self.place.planes):
                self.copy(3 + k).start()

    def finish(self):
        total = self.stages[3]
        for k in range(1, self.place.planes):
            self.copy(3 + k).wait_recv()
            total = total + self.got[3 + k]
        for i in (0, 1, 2):
            self.copy(i).wait_send()
        for k in range(1, self.place.planes):
            self.copy(3 + k).wait_send()
        return total


class Scatter:
    def __init__(self, place, sources, land, ours, got_b, got_a, got_z, mine, load, send, recv):
        self.place, self.sources, self.land, self.ours = place, sources, land, ours
        self.got_b, self.got_a, self.got_z, self.mine = got_b, got_a, got_z, mine
        self.load, self.send, self.recv = load, send, recv
        self.planes, self.side = place.planes, place.side
        self.cells = place.side * place.side
        self.parts = len(sources)
        self.order = list(range(1, self.planes)) + [0]
        self.offsets = [sum(s.shape[1] for s in sources[:i]) for i in range(self.parts + 1)]

    @staticmethod
    def scratch(planes, side, parts, rows):
        cells = side * side
        count = planes * (parts + 4)
        return [
            pltpu.VMEM((planes, cells, rows, D), BF16),
            pltpu.VMEM((2, cells, rows, D), BF16),
            pltpu.VMEM((planes, side, rows, D), BF16),
            pltpu.VMEM((planes, rows, D), BF16),
            pltpu.VMEM((planes, rows, D), BF16),
            pltpu.SemaphoreType.DMA((2, parts)),
            pltpu.SemaphoreType.DMA((count,)),
            pltpu.SemaphoreType.DMA((count,)),
        ]

    def remote(self, slot, source, target, to):
        return pltpu.make_async_remote_copy(
            src_ref=source, dst_ref=target, send_sem=self.send.at[slot], recv_sem=self.recv.at[slot],
            device_id=to, device_id_type=MESH,
        )

    def rows(self, part):
        return pl.ds(self.offsets[part], self.offsets[part + 1] - self.offsets[part])

    def cell(self, a, b):
        return a * self.place.step_a + b * self.place.step_b

    def core_copy(self, k, part):
        place = self.place
        group = pl.ds(place.run(place.plane(k), 1 - place.core), self.cells)
        return self.remote(
            k * self.parts + part, self.sources[part].at[group], self.land.at[k, :, self.rows(part)],
            place.other_core(),
        )

    def load_copy(self, t, part):
        place = self.place
        group = pl.ds(place.run(place.plane(self.order[t]), place.core), self.cells)
        return pltpu.make_async_copy(
            self.sources[part].at[group], self.ours.at[t % 2, :, self.rows(part)], self.load.at[t % 2, part]
        )

    def b_copy(self, k, a):
        place = self.place
        base = self.planes * self.parts
        return self.remote(
            base + 2 * k + a, self.land.at[k, self.cell(a, 1 - place.b)], self.got_b.at[k, a], place.across_b()
        )

    def a_copy(self, k):
        place = self.place
        base = self.planes * (self.parts + 2)
        return self.remote(
            base + k, self.land.at[k, self.cell(1 - place.a, place.b)], self.got_a.at[k], place.across_a()
        )

    def z_copy(self, k):
        place = self.place
        base = self.planes * (self.parts + 3)
        return self.remote(
            base + k, self.land.at[k, self.cell(place.a, place.b)], self.got_z.at[k], place.along_z(k)
        )

    def start(self, part):
        for k in self.order:
            self.core_copy(k, part).start()

    def start_one(self, t):
        self.core_copy(self.order[t], 0).start()

    def load_first(self):
        for part in range(self.parts):
            self.load_copy(0, part).start()

    def arrive_core(self, t):
        k = self.order[t]
        if t + 1 < self.planes:
            for part in range(self.parts):
                self.load_copy(t + 1, part).start()
        for part in range(self.parts):
            self.load_copy(t, part).wait()
            self.core_copy(k, part).wait_recv()

        def add(cell, _):
            self.land[k, cell] = self.land[k, cell] + self.ours[t % 2, cell]
            return 0

        lax.fori_loop(0, self.cells, add, 0)
        for a in range(self.side):
            self.b_copy(k, a).start()

    def arrive_b(self, t):
        k = self.order[t]
        for a in range(self.side):
            self.b_copy(k, a).wait_recv()
            at = self.cell(a, self.place.b)
            self.land[k, at] = self.land[k, at] + self.got_b[k, a]
        self.a_copy(k).start()

    def arrive_a(self, t):
        k = self.order[t]
        self.a_copy(k).wait_recv()
        at = self.cell(self.place.a, self.place.b)
        if k:
            self.land[k, at] = self.land[k, at] + self.got_a[k]
            self.z_copy(k).start()
        else:
            self.mine[...] = self.land[k, at].astype(F32) + self.got_a[k].astype(F32)

    def finish(self):
        for k in range(1, self.planes):
            self.z_copy(k).wait_recv()
            self.mine[...] += self.got_z[k].astype(F32)
        for k in range(self.planes):
            for part in range(self.parts):
                self.core_copy(k, part).wait_send()
            for a in range(self.side):
                self.b_copy(k, a).wait_send()
            self.a_copy(k).wait_send()
            if k:
                self.z_copy(k).wait_send()


def own_blocks(place, wq, wo, wu, wd, small, b_up, own1, own2):
    index = place.run(place.z, place.core) + place.a * place.step_a + place.b * place.step_b

    def spread(size, first):
        lane = lax.broadcasted_iota(jnp.int32, (size, D), 1)
        return jnp.where(lane == first + lax.broadcasted_iota(jnp.int32, (size, D), 0), 1.0, 0.0).astype(BF16)

    per_row = D // UROWS
    vec1 = mm(small[...], spread(OROWS, index * OROWS), 1, 0)
    whole_row = jnp.broadcast_to(b_up[...].astype(F32), (8, UROWS))
    here = lax.broadcasted_iota(jnp.int32, (8, UROWS), 0) == index // per_row
    vec2 = mm(jnp.where(here, whole_row, 0.0).astype(BF16), spread(UROWS, index % per_row * UROWS), 1, 0)
    own1[...] = jnp.concatenate([wq[...].astype(F32), vec1], axis=0).astype(BF16)
    own2[0:UROWS, :] = wu[...]
    down = wd[...].astype(F32)
    rest = [down[:, c * D : (c + 1) * D] for c in range(CHUNKS)] + [wo[...].astype(F32), vec2]
    own2[UROWS:SECOND, :] = jnp.concatenate(rest, axis=0).astype(BF16)


def forward_kernel(planes, side, rows, *refs):
    if planes:
        wq, wo, wu, wd, small, b_up, *refs = refs
    else:
        first_ref, full2, *refs = refs
    (hid_ref, emb_ref, seg_ref, packed_ref, mixed_ref, mid_ref, norm_ref, total_ref, vec_ref, w_qkv, w_out, scaled_ref,
     *refs) = refs
    if planes:
        full2, *refs = refs
    first, tail, bias_col, mask_q, mask_k, load, *refs = refs
    step = pl.program_id(0)
    begin = 2 * rows
    leave = begin + 7 * rows
    row, phase = (step - begin) // 7, (step - begin) % 7
    attending = (step >= begin) & (step < leave)
    tail_copy = pltpu.make_async_copy(full2.at[:, pl.ds(2 * UROWS, 32)], tail, load.at[0])

    if planes:
        own1, own2, send1, recv1, send2, recv2 = refs
        place = Place(planes, side)
        gather1 = Gather(place, own1, first, send1, recv1)
        gather2 = Gather(place, own2, full2, send2, recv2)

        @pl.when(step == 0)
        def _():
            place.arrive()
            own_blocks(place, wq, wo, wu, wd, small, b_up, own1, own2)
            place.meet()
            gather1.start_z(range(1, planes))
            gather1.start_ab()

        @pl.when(step == begin)
        def _():
            for which, kind, k in FIRST_SCHED:
                (gather1, gather2)[which].event(kind, k)

        for at, kind, k in SCHED:
            @pl.when(step == begin + at)
            def _(kind=kind, k=k):
                gather2.event(kind, k)

        @pl.when(step == begin + SCHED[-1][0])
        def _():
            tail_copy.start()
    else:
        @pl.when(step == 0)
        def _():
            tail_copy.start()
            c = pltpu.make_async_copy(first_ref, first, load.at[1])
            c.start()
            c.wait()

    @pl.when(step < begin)
    def _():
        scaled, _ = normalise(hid_ref[...].astype(F32) + emb_ref[...].astype(F32))
        mixed_ref[pl.ds(pl.multiple_of(step * TOKB, TOKB), TOKB), :] = scaled
        scaled_ref[...] = scaled.astype(BF16)

    @pl.when(step == begin)
    def _():
        join_rows(first, 0, QROWS, w_qkv, BLOCKS // 2)
        vec_ref[0] = sum_rows(first, QROWS)
        bias_col[0:D] = column(vec_ref[0, 2:3, :])
        bias_col[D : 2 * D] = jnp.zeros((D, 1), F32)
        bias_col[2 * D : 3 * D] = column(vec_ref[0, 3:4, :])

    tokens = pl.ds(pl.multiple_of(row * ROW, ROW), ROW)

    @pl.when(attending & (phase == 0))
    def _():
        normed = (mixed_ref[tokens, :] * vec_ref[0, 0:1, :] + vec_ref[0, 1:2, :]).astype(BF16)
        packed_ref[...] = (mm(w_qkv[...], normed, 1, 1) + bias_col[...]).astype(BF16)
        query_side, key_side = mask_rows(seg_ref[0])
        mask_q[...] = query_side
        mask_k[...] = key_side

    @pl.when(attending & (phase >= 1))
    def _():
        base = pl.multiple_of((phase - 1) * 128, 128)
        ones_rows = jnp.where(lax.broadcasted_iota(jnp.int32, (HEAD, ROW), 0) == 0, 1.0, 0.0).astype(BF16)
        sides = []
        for h in range(2):
            at = base + HEAD * h
            query_parts = scaled_query(packed_ref[pl.ds(at, HEAD), :])
            keys = packed_ref[pl.ds(D + at, HEAD), :]
            sides.append((
                jnp.concatenate(query_parts + [mask_q[...]], axis=0),
                jnp.concatenate([keys, keys, keys, mask_k[...]], axis=0),
                jnp.concatenate([packed_ref[pl.ds(2 * D + at, HEAD), :], ones_rows], axis=0),
            ))
        all_scores = [mm(sides[h][1], sides[h][0], 0, 0) for h in range(2)]
        mixed = []
        for h in range(2):
            scores = all_scores[h]
            top = jnp.max(scores, axis=0, keepdims=True)
            weights = jnp.exp2(scores - top).astype(BF16)
            summed = mm(sides[h][2], weights, 1, 0)
            total = summed[HEAD : HEAD + 1, :]
            mixed.append(summed[:HEAD, :] / total)
            total_ref[0, h : h + 1, :] = top + jnp.log2(total)
        mixed_ref[tokens, pl.ds(base, 128)] = jnp.concatenate(mixed, axis=0).T

    @pl.when(step == leave)
    def _():
        tail_copy.wait()
        join_rows(tail, 0, OROWS, w_out, BLOCKS // 2)
        vec_ref[1] = sum_rows(tail, OROWS)

    @pl.when(step >= leave)
    def _():
        half = pl.ds(pl.multiple_of((step - leave) * TOKB, TOKB), TOKB)
        entered = hid_ref[...].astype(F32) + emb_ref[...].astype(F32)
        middle = entered + mm(mixed_ref[half, :].astype(BF16), w_out[...], 1, 1) + vec_ref[0, 4:5, :]
        scaled, _ = normalise(middle)
        mid_ref[...] = middle
        norm_ref[...] = (scaled * vec_ref[0, 5:6, :] + vec_ref[0, 6:7, :]).astype(BF16)


def forward(planes, side, weights, hidden, embed, segment):
    n = hidden.shape[0]
    rows = n // ROW
    begin = 2 * rows
    leave_at = begin + 7 * rows
    one = pl.Buffered(1)
    hbm = pl.BlockSpec(memory_space=pl.ANY)

    def row(s):
        return jnp.clip((s - begin) // 7, 0, rows - 1)

    def entry(s):
        return (jnp.where(s < leave_at, jnp.minimum(s, begin - 1), s - leave_at), 0)

    def leave(s):
        return (jnp.maximum(s - leave_at, 0), 0)

    def pair(s):
        return jnp.where(s < leave_at, jnp.maximum((s - begin) % 7 - 1, 0) * (s >= begin), 5)

    entering = pl.BlockSpec((TOKB, D), entry)
    leaving = pl.BlockSpec((TOKB, D), leave)
    out_specs = [
        pl.BlockSpec((3 * D, ROW), lambda s: (0, row(s))),
        pl.BlockSpec((n, D), lambda s: (0, 0), pipeline_mode=one),
        leaving,
        leaving,
        pl.BlockSpec((1, 8, ROW), lambda s: (pair(s), 0, row(s))),
        pl.BlockSpec((2, 8, D), lambda s: (0, 0, 0)),
        pl.BlockSpec((3 * D, D), lambda s: (0, 0), pipeline_mode=one),
        pl.BlockSpec((D, D), lambda s: (0, 0), pipeline_mode=one),
        pl.BlockSpec((TOKB, D), lambda s: (jnp.minimum(s, begin - 1), 0)),
    ]
    out_shape = [
        jax.ShapeDtypeStruct((3 * D, n), BF16),
        jax.ShapeDtypeStruct((n, D), F32),
        jax.ShapeDtypeStruct((n, D), F32),
        jax.ShapeDtypeStruct((n, D), BF16),
        jax.ShapeDtypeStruct((HEADS // 2, 8, n), F32),
        jax.ShapeDtypeStruct((2, 8, D), F32),
        jax.ShapeDtypeStruct((3 * D, D), BF16),
        jax.ShapeDtypeStruct((D, D), BF16),
        jax.ShapeDtypeStruct((n, D), BF16),
    ]
    scratch = [
        pltpu.VMEM((BLOCKS, FIRST, D), BF16),
        pltpu.VMEM((BLOCKS, 32, D), BF16),
        pltpu.VMEM((3 * D, 1), F32),
        pltpu.VMEM((32, ROW), BF16),
        pltpu.VMEM((32, ROW), BF16),
        pltpu.SemaphoreType.DMA((2,)),
    ]
    params = dict(vmem_limit_bytes=56 * MIB)
    if planes:
        in_specs = [pl.BlockSpec(w.shape, lambda s: (0, 0), pipeline_mode=one) for w in weights]
        out_specs.append(hbm)
        out_shape.append(jax.ShapeDtypeStruct((BLOCKS, SECOND, D), BF16))
        scratch += [pltpu.VMEM((FIRST, D), BF16), pltpu.VMEM((SECOND, D), BF16)]
        scratch += [Gather.semaphores(planes)] * 4
        params.update(collective_id=1, has_side_effects=True)
    else:
        in_specs = [hbm, hbm]
    outs = pl.pallas_call(
        partial(forward_kernel, planes, side, rows),
        grid=(leave_at + begin,),
        in_specs=in_specs + [entering, entering, pl.BlockSpec((1, 1, ROW), lambda s: (row(s), 0, 0))],
        out_specs=out_specs,
        out_shape=out_shape,
        scratch_shapes=scratch,
        compiler_params=pltpu.CompilerParams(**params),
        name="attention_forward",
    )(*weights, hidden, embed, segment.reshape(rows, 1, ROW))
    return outs if planes else list(outs) + [weights[1]]


def feed_kernel(
    rows,
    up_ref, down_ref, vec_ref, norm_ref, mid_ref, cot_ref, seg_ref,
    out_ref, gmid_ref, gup_ref, gdown_ref, gvec_ref,
    w_down, result, back, live, active, pre, hold,
):
    step = pl.program_id(0)
    working = step < CHUNKS * rows
    j, i = step // rows, step % rows
    at = pl.ds(pl.multiple_of(i * ROW, ROW), ROW)

    @pl.when(step == 0)
    def _():
        gvec_ref[...] = jnp.zeros_like(gvec_ref)

    for chunk in range(CHUNKS):
        @pl.when(step == chunk * rows)
        def _():
            join_rows(down_ref, chunk % 2 * OROWS, OROWS, w_down, BLOCKS // 2)

    @pl.when(step < rows)
    def _():
        keep = column(jnp.where(seg_ref[0] >= 0, 1.0, 0.0))
        grad_result = cot_ref[...].astype(F32) * keep
        live[at, :] = grad_result.astype(BF16)
        gvec_ref[4:5, :] += jnp.sum(grad_result, axis=0, keepdims=True)

    @pl.when(working)
    def _():
        up = up_ref[...].reshape(D, D)
        down = w_down[...]
        x = mm(norm_ref[at, :], up, 1, 1) + vec_ref[1, pl.ds(j, 1), :]
        grad_act = mm(live[at, :], down, 1, 0)
        c0 = math.sqrt(2.0 / math.pi)
        c1 = 0.044715
        square = x * x
        th = jnp.tanh(x * (c0 + (c0 * c1) * square))
        half = 0.5 + 0.5 * th
        slope = half + (0.5 * x) * ((1.0 - th * th) * (c0 + (3 * c0 * c1) * square))
        activated = (x * half).astype(BF16)
        grad_pre = (grad_act * slope).astype(BF16)
        active[at, :] = activated
        pre[at, :] = grad_pre
        gvec_ref[pl.ds(j, 1), :] += jnp.sum(grad_pre.astype(F32), axis=0, keepdims=True)

        @pl.when(j == 0)
        def _():
            result[at, :] = mm(activated, down, 1, 1)
            back[at, :] = mm(grad_pre, up, 1, 0)

        @pl.when(j > 0)
        def _():
            result[at, :] += mm(activated, down, 1, 1)
            back[at, :] += mm(grad_pre, up, 1, 0)

    @pl.when(working & (i == rows - 1))
    def _():
        gup_ref[...] = mm(pre[...], norm_ref[...], 0, 0).astype(BF16)
        part_down = mm(live[...], active[...], 0, 0)

        hold[...] = part_down

        @pl.when(j % 2 == 0)
        def _():
            def pack(d, _):
                own = pl.ds(pl.multiple_of(d * OROWS, 8), OROWS)
                gdown_ref[d] = jnp.concatenate([hold[own], jnp.zeros((OROWS, D), F32)], axis=0).astype(BF16)
                return 0

            lax.fori_loop(0, BLOCKS, pack, 0)

        @pl.when(j % 2 == 1)
        def _():
            def pack(d, _):
                own = pl.ds(pl.multiple_of(d * OROWS, 8), OROWS)
                kept = gdown_ref[d].astype(F32)[:OROWS]
                gdown_ref[d] = jnp.concatenate([kept, hold[own]], axis=0).astype(BF16)
                return 0

            lax.fori_loop(0, BLOCKS, pack, 0)

    @pl.when(step >= CHUNKS * rows)
    def _():
        tokens = pl.ds(pl.multiple_of((step - CHUNKS * rows) * TOKB, TOKB), TOKB)
        middle = mid_ref[...]
        out_ref[...] = (middle + (result[tokens, :] + vec_ref[0, 7:8, :])).astype(BF16)
        grad = back[tokens, :]
        scaled, inverse = normalise(middle)
        gvec_ref[5:6, :] += jnp.sum(grad * scaled, axis=0, keepdims=True)
        gvec_ref[6:7, :] += jnp.sum(grad, axis=0, keepdims=True)
        gmid_ref[...] = live[tokens, :].astype(F32) + norm_back(grad, scaled, inverse, vec_ref[0, 5:6, :])


def feed(second, vec, normed, middle, cotangent, segment):
    n = normed.shape[0]
    rows = n // ROW
    one = pl.Buffered(1)

    def chunk(s):
        return jnp.minimum(s // rows, CHUNKS - 1)

    def late(s):
        return (jnp.maximum(s - CHUNKS * rows, 0), 0)

    leaving = pl.BlockSpec((TOKB, D), late)
    return pl.pallas_call(
        partial(feed_kernel, rows),
        grid=(CHUNKS * rows + n // TOKB,),
        in_specs=[
            pl.BlockSpec((BLOCKS // CHUNKS, UROWS, D), lambda s: (chunk(s), 0, 0)),
            pl.BlockSpec((BLOCKS, 2 * OROWS, D), lambda s: (0, 2 + chunk(s) // 2, 0), pipeline_mode=one),
            pl.BlockSpec((2, 8, D), lambda s: (0, 0, 0)),
            pl.BlockSpec((n, D), lambda s: (0, 0), pipeline_mode=one),
            leaving,
            pl.BlockSpec((ROW, D), lambda s: (jnp.minimum(s, rows - 1), 0), pipeline_mode=one),
            pl.BlockSpec((1, 1, ROW), lambda s: (jnp.minimum(s, rows - 1), 0, 0)),
        ],
        out_specs=[
            leaving,
            leaving,
            pl.BlockSpec((D, D), lambda s: (chunk(s), 0)),
            pl.BlockSpec((BLOCKS, 2 * OROWS, D), lambda s: (0, chunk(s) // 2, 0), pipeline_mode=one),
            pl.BlockSpec((8, D), lambda s: (0, 0)),
        ],
        out_shape=[
            jax.ShapeDtypeStruct((n, D), BF16),
            jax.ShapeDtypeStruct((n, D), F32),
            jax.ShapeDtypeStruct((FF, D), BF16),
            jax.ShapeDtypeStruct((BLOCKS, UROWS, D), BF16),
            jax.ShapeDtypeStruct((8, D), F32),
        ],
        scratch_shapes=[
            pltpu.VMEM((D, D), BF16),
            pltpu.VMEM((n, D), F32),
            pltpu.VMEM((n, D), F32),
            pltpu.VMEM((n, D), BF16),
            pltpu.VMEM((n, D), BF16),
            pltpu.VMEM((n, D), BF16),
            pltpu.VMEM((D, D), F32),
        ],
        compiler_params=pltpu.CompilerParams(vmem_limit_bytes=60 * MIB),
        name="feed_forward",
    )(second, second, vec, normed, middle, cotangent, segment.reshape(rows, 1, ROW))


def three_parts(row):
    r = lax.broadcasted_iota(jnp.int32, (16, row.shape[1]), 0)
    a = row.astype(BF16).astype(F32)
    b = (row - a).astype(BF16).astype(F32)
    c = row - a - b
    return jnp.where(r == 0, -a, jnp.where(r == 1, -b, jnp.where(r == 2, -c, 0.0))).astype(BF16)


def backward_kernel(
    planes, side, rows,
    w_out, seg_ref, packed_q, packed_k, packed_v, mixed_ref, total_ref, gmid_ref, gvec_ref, gup_ref, gdown_ref,
    gpacked_ref, sums_ref, *rest,
):
    if planes:
        up_out, down_out, out_out, vec_out, mask_q, mask_k, grad_mixed, delta, sum_out, sum_bias, tail, mine, *transfer = rest
    else:
        tail, mask_q, mask_k, grad_mixed, delta, sum_out, sum_bias = rest
    step = pl.program_id(0)
    entry = 2 * rows
    heads = step >= entry

    if planes:
        place = Place(planes, side)
        scatter = Scatter(place, (gup_ref, gdown_ref, tail), *transfer[:5], mine, *transfer[5:])

        @pl.when(step == 0)
        def _():
            place.arrive()

        @pl.when(step == 1)
        def _():
            place.meet()
            scatter.start(0)
            scatter.start(1)

        @pl.when(step == entry)
        def _():
            scatter.start(2)
            scatter.load_first()

        for at, t, act in BACK:
            @pl.when(step == entry + at)
            def _(t=t, act=act):
                getattr(scatter, act)(t)

    @pl.when(step == 0)
    def _():
        sum_out[...] = jnp.zeros_like(sum_out)
        sum_bias[...] = jnp.zeros_like(sum_bias)

    @pl.when(step < entry)
    def _():
        at = pl.ds(pl.multiple_of(step * TOKB, TOKB), TOKB)
        mixed = mixed_ref[...]
        branch = gmid_ref[...].astype(BF16)
        sum_bias[0:1, :] += jnp.sum(branch.astype(F32), axis=0, keepdims=True)
        sum_out[...] += mm(branch, mixed.astype(BF16), 0, 0)
        grad = mm(branch, w_out[...], 1, 0).astype(BF16).astype(F32)
        grad_mixed[:, at] = grad.T.astype(BF16)
        inner = (grad * mixed).T
        delta[:, at] = jnp.concatenate(
            [jnp.sum(inner[HEAD * h : HEAD * (h + 1)], axis=0, keepdims=True) for h in range(HEADS)]
            + [jnp.zeros((16 - HEADS, TOKB), F32)],
            axis=0,
        )

    @pl.when(step == entry - 1)
    def _():
        r = lax.broadcasted_iota(jnp.int32, (8, D), 0)
        vectors = jnp.where(r == 7, sum_bias[0:1, :], gvec_ref[...])

        def pack(d, _):
            at = pl.ds(pl.multiple_of(d * OROWS, 8), OROWS)
            tail[d] = jnp.concatenate([sum_out[at, :], vectors], axis=0).astype(BF16)
            return 0

        lax.fori_loop(0, BLOCKS, pack, 0)

    row, pair = (step - entry) // 6, (step - entry) % 6

    @pl.when(heads & (pair == 0))
    def _():
        query_side, key_side = mask_rows(seg_ref[0])
        mask_q[...] = query_side
        mask_k[...] = key_side

    @pl.when(heads)
    def _():
        tokens = pl.ds(pl.multiple_of(row * ROW, ROW), ROW)
        r = lax.broadcasted_iota(jnp.int32, (16, ROW), 0)
        ones_rows = jnp.where(r < 3, 1.0, 0.0).astype(BF16)
        base = pl.multiple_of(pair * 128, 128)
        column_sums = []
        for h in range(2):
            at_rows = slice(HEAD * h, HEAD * (h + 1))
            queries, keys, values = packed_q[at_rows, :], packed_k[at_rows, :], packed_v[at_rows, :]
            grad = grad_mixed[pl.ds(base + HEAD * h, HEAD), tokens]
            wide_q = jnp.concatenate(scaled_query(queries) + [mask_q[...], three_parts(total_ref[0, h : h + 1, :])], axis=0)
            wide_k = jnp.concatenate([keys, keys, keys, mask_k[...], ones_rows], axis=0)
            wide_g = jnp.concatenate([grad, three_parts(delta[pl.ds(2 * pair + h, 1), tokens])], axis=0)
            wide_v = jnp.concatenate([values, ones_rows], axis=0)
            grad_v = jnp.zeros((HEAD, ROW), F32)
            grad_k = jnp.zeros((HEAD, ROW), F32)
            grad_q = []
            for half in range(2):
                at = slice(half * (ROW // 2), (half + 1) * (ROW // 2))
                probs = jnp.exp2(mm(wide_q[:, at], wide_k, 0, 0))
                grad_probs = mm(wide_g[:, at], wide_v, 0, 0)
                grad_scores = (probs * grad_probs).astype(BF16)
                grad_v = grad_v + mm(grad[:, at], probs.astype(BF16), 1, 0)
                grad_k = grad_k + mm(queries[:, at], grad_scores, 1, 0)
                grad_q.append(mm(keys, grad_scores, 1, 1))
            grads = (
                (jnp.concatenate(grad_q, axis=1) * 0.125).astype(BF16),
                (grad_k * 0.125).astype(BF16),
                grad_v.astype(BF16),
            )
            for part in range(3):
                gpacked_ref[pl.ds(part * D + base + HEAD * h, HEAD), :] = grads[part]
            column_sums.append([jnp.sum(g.astype(F32), axis=1, keepdims=True) for g in grads])
        for part in range(3):
            both = jnp.concatenate([column_sums[0][part], column_sums[1][part]], axis=0)
            at = pl.ds(part * D + base, 128)

            @pl.when(row == 0)
            def _():
                sums_ref[at, :] = both

            @pl.when(row > 0)
            def _():
                sums_ref[at, :] += both

    if planes:
        @pl.when(step == entry + 6 * rows - 1)
        def _():
            scatter.finish()
            up_out[...] = mine[0:UROWS, :]
            for c in range(CHUNKS):
                down_out[:, c * D : (c + 1) * D] = mine[UROWS + c * OROWS : UROWS + (c + 1) * OROWS, :]
            out_out[...] = mine[2 * UROWS : 2 * UROWS + OROWS, :]
            vec_out[...] = mine[2 * UROWS + OROWS : 2 * UROWS + 32, :]


def backward(planes, side, w_out, segment, packed, mixed, totals, gmid, gvec, gup, gdown):
    n = mixed.shape[0]
    rows = n // ROW
    entry = 2 * rows
    one = pl.Buffered(1)
    hbm = pl.BlockSpec(memory_space=pl.ANY)

    def early(s):
        return (jnp.minimum(s, entry - 1), 0)

    def row(s):
        return jnp.maximum(s - entry, 0) // 6

    def pair(s):
        return jnp.maximum(s - entry, 0) % 6

    def heads(part):
        return pl.BlockSpec((128, ROW), lambda s: (6 * part + pair(s), row(s)))

    out_specs = [
        pl.BlockSpec((3 * D, ROW), lambda s: (0, row(s))),
        pl.BlockSpec((3 * D, 1), lambda s: (0, 0), pipeline_mode=one),
    ]
    out_shape = [jax.ShapeDtypeStruct((3 * D, n), BF16), jax.ShapeDtypeStruct((3 * D, 1), F32)]
    scratch = [
        pltpu.VMEM((32, ROW), BF16),
        pltpu.VMEM((32, ROW), BF16),
        pltpu.VMEM((D, n), BF16),
        pltpu.VMEM((16, n), F32),
        pltpu.VMEM((D, D), F32),
        pltpu.VMEM((8, D), F32),
    ]
    params = dict(vmem_limit_bytes=56 * MIB)
    if planes:
        rows1 = 2 * UROWS + 32
        for shape in ((UROWS, D), (OROWS, FF), (OROWS, D), (8, D)):
            out_specs.append(pl.BlockSpec(shape, lambda s: (0, 0), pipeline_mode=one))
            out_shape.append(jax.ShapeDtypeStruct(shape, F32))
        scratch += [pltpu.VMEM((BLOCKS, 32, D), BF16), pltpu.VMEM((rows1, D), F32)]
        scratch += Scatter.scratch(planes, side, 3, rows1)
        params.update(collective_id=2, has_side_effects=True)
    else:
        out_specs.append(pl.BlockSpec((BLOCKS, 32, D), lambda s: (0, 0, 0), pipeline_mode=one))
        out_shape.append(jax.ShapeDtypeStruct((BLOCKS, 32, D), BF16))
    return pl.pallas_call(
        partial(backward_kernel, planes, side, rows),
        grid=(entry + 6 * rows,),
        in_specs=[
            pl.BlockSpec((D, D), lambda s: (0, 0), pipeline_mode=one),
            pl.BlockSpec((1, 1, ROW), lambda s: (row(s), 0, 0)),
            heads(0),
            heads(1),
            heads(2),
            pl.BlockSpec((TOKB, D), early),
            pl.BlockSpec((1, 8, ROW), lambda s: (pair(s), 0, row(s))),
            pl.BlockSpec((TOKB, D), early),
            pl.BlockSpec((8, D), lambda s: (0, 0)),
            hbm,
            hbm,
        ],
        out_specs=out_specs,
        out_shape=out_shape,
        scratch_shapes=scratch,
        compiler_params=pltpu.CompilerParams(**params),
        name="attention_backward",
    )(w_out, segment.reshape(rows, 1, ROW), packed, packed, packed, mixed, totals, gmid, gvec, gup, gdown)


def enter_kernel(
    planes, side, blocks,
    w_hbm, vec_ref, hid_ref, emb_ref, gmid_ref, grad_hbm, sums_ref, scaled_hbm,
    ghid_ref, out_ref, *rest,
):
    if planes:
        vec_out, scaled_all, w_qkv, grad_packed, totals, load, packed, mine, *transfer = rest
    else:
        packed, (scaled_all, w_qkv, grad_packed, totals, load) = out_ref, rest
    step = pl.program_id(0)
    chunks = 4
    size = 3 * D // chunks
    begin, late = 0, chunks
    if planes:
        place = Place(planes, side)

    def chunk_of(t):
        return place.plane(t + 1) if planes else t

    def grad_load(t):
        rows = pl.ds(pl.multiple_of(chunk_of(t) * size, size), size)
        return pltpu.make_async_copy(grad_hbm.at[rows], grad_packed.at[rows], load.at[t])

    loads = [
        pltpu.make_async_copy(scaled_hbm, scaled_all, load.at[chunks]),
        pltpu.make_async_copy(w_hbm, w_qkv, load.at[chunks + 1]),
    ]

    if planes:
        rider = Rider(place, *transfer[:4])
        scatter = Scatter(place, (packed,), *transfer[4:9], mine, *transfer[9:])

    @pl.when(step == 0)
    def _():
        loads[0].start()
        grad_load(0).start()
        loads[1].start()
        for t in range(1, chunks):
            grad_load(t).start()
        totals[...] = jnp.zeros_like(totals)
        if planes:
            place.arrive()

    def entering():
        return normalise(hid_ref[...].astype(F32) + emb_ref[...].astype(F32))

    @pl.when(step == begin)
    def _():
        for c in loads:
            c.wait()
        if planes:
            place.meet()

    for t in range(chunks):
        @pl.when(step == t)
        def _(t=t):
            grad_load(t).wait()

    if planes:
        for at, t, act in ENTER:
            @pl.when(step == begin + at)
            def _(t=t, act=act):
                getattr(scatter, act)(t)
                if t == planes - 1:
                    rider.arrive(("arrive_core", "arrive_b", "arrive_a").index(act))

    @pl.when((step >= begin) & (step < late))
    def _():
        t = step - begin
        chunk = chunk_of(t)
        at = pl.ds(pl.multiple_of(chunk * size, size), size)
        product = mm(grad_packed[at, :], scaled_all[...], 1, 0)
        weight = w_qkv[at, :].astype(F32)
        sums = sums_ref[at, :]
        totals[0:1, :] += jnp.sum(weight * product, axis=0, keepdims=True)
        totals[1:2, :] += jnp.sum(weight * sums, axis=0, keepdims=True)
        grad_w = product * vec_ref[0, 0:1, :] + sums * vec_ref[0, 1:2, :]
        count = BLOCKS // chunks
        for i in range(count):
            rows = [grad_w[i * QROWS : (i + 1) * QROWS], jnp.zeros((8, D), F32)]
            packed[chunk * count + i] = jnp.concatenate(rows, axis=0).astype(BF16)

    if planes:
        for t in range(planes):
            @pl.when(step == begin + t)
            def _(t=t):
                if t == 0:
                    scatter.load_first()
                scatter.start_one(t)

    @pl.when(step == late - 1)
    def _():
        ends = [jnp.broadcast_to(sums_ref[at : at + D, :], (D, 128)).T[0:1, :] for at in (0, 2 * D)]
        vectors = jnp.concatenate([totals[0:2, :]] + ends + [jnp.zeros((4, D), F32)], axis=0)
        if planes:
            rider.stages[0] = vectors
            rider.start()
        else:
            kept = packed[0, QROWS - 8 : QROWS + 8, :].astype(F32)[:8]
            packed[0, QROWS - 8 : QROWS + 8, :] = jnp.concatenate([kept, vectors], axis=0).astype(BF16)

    @pl.when(step >= late)
    def _():
        at = pl.ds(pl.multiple_of((step - late) * TOKB, TOKB), TOKB)
        scaled, inverse = entering()
        grad = mm(grad_packed[:, at], w_qkv[...], 0, 0)
        ghid_ref[...] = (gmid_ref[...] + norm_back(grad, scaled, inverse, vec_ref[0, 0:1, :])).astype(BF16)

    if planes:
        @pl.when(step == late + blocks - 1)
        def _():
            for t, act in ENTER_LAST:
                getattr(scatter, act)(t)
                if t == planes - 1:
                    rider.arrive(("arrive_core", "arrive_b", "arrive_a").index(act))
            scatter.finish()
            out_ref[...] = mine[0:QROWS, :]
            vec_out[...] = rider.finish()


def enter(planes, side, w_qkv, vec, hidden, embed, gmid, gpacked, sums, scaled):
    n = hidden.shape[0]
    blocks = n // TOKB
    late_at = 4
    one = pl.Buffered(1)
    hbm = pl.BlockSpec(memory_space=pl.ANY)

    def late(s):
        return (jnp.maximum(s - late_at, 0), 0)

    tokens = pl.BlockSpec((TOKB, D), late)
    out_specs = [pl.BlockSpec((TOKB, D), late)]
    out_shape = [jax.ShapeDtypeStruct((n, D), BF16)]
    scratch = [
        pltpu.VMEM((n, D), BF16),
        pltpu.VMEM((3 * D, D), BF16),
        pltpu.VMEM((3 * D, n), BF16),
        pltpu.VMEM((8, D), F32),
        pltpu.SemaphoreType.DMA((6,)),
    ]
    params = dict(vmem_limit_bytes=56 * MIB)
    if planes:
        for shape in ((QROWS, D), (8, D)):
            out_specs.append(pl.BlockSpec(shape, lambda s: (0, 0), pipeline_mode=one))
            out_shape.append(jax.ShapeDtypeStruct(shape, F32))
        scratch += [pltpu.VMEM((BLOCKS, FIRST, D), BF16), pltpu.VMEM((FIRST, D), F32)]
        scratch += Rider.scratch(planes) + Scatter.scratch(planes, side, 1, FIRST)
        params.update(collective_id=3, has_side_effects=True)
    else:
        out_specs.append(pl.BlockSpec((BLOCKS, FIRST, D), lambda s: (0, 0, 0), pipeline_mode=one))
        out_shape.append(jax.ShapeDtypeStruct((BLOCKS, FIRST, D), BF16))
    return pl.pallas_call(
        partial(enter_kernel, planes, side, blocks),
        grid=(late_at + blocks,),
        in_specs=[
            hbm,
            pl.BlockSpec((2, 8, D), lambda s: (0, 0, 0)),
            tokens,
            tokens,
            pl.BlockSpec((TOKB, D), late),
            hbm,
            pl.BlockSpec((3 * D, 1), lambda s: (0, 0), pipeline_mode=one),
            hbm,
        ],
        out_specs=out_specs,
        out_shape=out_shape,
        scratch_shapes=scratch,
        compiler_params=pltpu.CompilerParams(**params),
        name="projection_backward",
    )(w_qkv, vec, hidden, embed, gmid, gpacked, sums, scaled)


def body(
    planes, side, devices,
    hidden, time_embed, segment_ids,
    ln1_gain, ln1_bias, w_qkv, b_query, b_value, w_out, b_out, ln2_gain, ln2_bias, w_up, b_up, w_down, b_down,
    cotangent,
):
    index = lax.axis_index("dp") * lax.axis_size("fsdp") + lax.axis_index("fsdp")
    axes = ("dp", "fsdp")
    small = (ln1_gain, ln1_bias, b_query, b_value, b_out, ln2_gain, ln2_bias, b_down)
    if planes:
        weights = (w_qkv.T, w_out.T, w_up.T, w_down.T, jnp.stack(small), b_up[None, :])
    else:
        def whole(a, dim):
            return lax.all_gather(a, axes, axis=dim, tiled=True)

        def only_first(rows):
            return jnp.concatenate([rows[None], jnp.zeros((BLOCKS - 1,) + rows.shape, BF16)], axis=0)

        vec1 = jnp.stack([whole(v, 0) for v in small])
        vec2 = jnp.concatenate([whole(b_up, 0).reshape(CHUNKS, D), jnp.zeros((8 - CHUNKS, D), BF16)], axis=0)
        down_rows = whole(w_down, 1).T.reshape(BLOCKS, OROWS, CHUNKS, D).transpose(0, 2, 1, 3)
        first = jnp.concatenate([whole(w_qkv, 1).T.reshape(BLOCKS, QROWS, D), only_first(vec1)], axis=1)
        second = jnp.concatenate(
            [
                whole(w_up, 1).T.reshape(BLOCKS, UROWS, D),
                down_rows.reshape(BLOCKS, UROWS, D),
                whole(w_out, 1).T.reshape(BLOCKS, OROWS, D),
                only_first(vec2),
            ],
            axis=1,
        )
        weights = (first, second)
    packed, mixed, middle, normed, totals, vec, full_qkv, full_out, scaled, second = forward(
        planes, side, weights, hidden, time_embed, segment_ids
    )
    output, gmid, gup, gdown, gvec = feed(second, vec, normed, middle, cotangent, segment_ids)
    gup = gup.reshape(BLOCKS, UROWS, D)
    gpacked, sums, *late = backward(
        planes, side, full_out, segment_ids, packed, mixed, totals, gmid, gvec, gup, gdown
    )
    ghid, *last = enter(planes, side, full_qkv, vec, hidden, time_embed, gmid, gpacked, sums, scaled)
    if planes:
        part_up, part_down, part_out, vectors = late
        part_qkv, vectors_qkv = last
        vectors = jnp.concatenate([vectors, vectors_qkv], axis=0)
        short = lax.dynamic_slice(vectors, (0, index * OROWS), (16, OROWS))
        part_bup = lax.dynamic_slice(vectors[:CHUNKS].reshape(-1), (index * UROWS,), (UROWS,))
    else:
        def shared(a, dim):
            return lax.psum_scatter(a.astype(F32), axes, scatter_dimension=dim, tiled=True)

        (late,), (last,) = late, last
        part_up = shared(gup.reshape(FF, D), 0)
        part_down = shared(gdown.reshape(BLOCKS, CHUNKS, OROWS, D).transpose(0, 2, 1, 3).reshape(D, FF), 0)
        part_out = shared(late[:, :OROWS].reshape(D, D), 0)
        part_qkv = shared(last[:, :QROWS].reshape(3 * D, D), 0)
        vectors = jnp.concatenate([late[0, OROWS:], last[0, QROWS:]], axis=0)
        short = shared(vectors, 1)
        part_bup = shared(vectors[:CHUNKS].reshape(-1), 0)
    return (
        output, ghid,
        short[8], short[9], part_qkv.T, short[10], short[11], part_out.T, short[7],
        short[5], short[6], part_up.T, part_bup, part_down.T, short[4],
    )


def solution(mesh):
    groups, cells = mesh.shape["dp"], mesh.shape["fsdp"]
    side = math.isqrt(cells)
    own_transfers = groups * cells == BLOCKS and side == 2 and cells == 4 and groups % 2 == 0
    split = ("dp", "fsdp")
    rows, flat, cols = P(split, None), P(split), P(None, split)
    return jax.shard_map(
        partial(body, groups // 2 if own_transfers else 0, side, groups * cells),
        mesh=mesh,
        in_specs=(
            rows, rows, flat, flat, flat, cols, flat, flat, cols, flat, flat, flat, cols, flat, cols, flat, rows,
        ),
        out_specs=(
            rows, rows, flat, flat, cols, flat, flat, cols, flat, flat, flat, cols, flat, cols, flat,
        ),
        check_vma=False,
    )
```

```python
from functools import partial
import math

import jax
import jax.numpy as jnp
from jax import lax
from jax.experimental import pallas as pl
from jax.experimental.pallas import tpu as pltpu
from jax.sharding import PartitionSpec as P

D = 768
HEADS = 12
HEAD = 64
FF = 3072
ROW = 1024
BLOCKS = 32
QROWS = 3 * D // BLOCKS
OROWS = D // BLOCKS
UROWS = FF // BLOCKS
CHUNKS = FF // D
FIRST = QROWS + 8
SECOND = 2 * UROWS + OROWS + 8
TOKB = 512
MIB = 2**20
MESH = pl.DeviceIdType.MESH
F32 = jnp.float32
BF16 = jnp.bfloat16
LOG2E = math.log2(math.e)
EPS = 1e-05
FIRST_SCHED = (
    (0, "z", 1), (0, "a", 0), (0, "z", 2), (0, "a", 1), (0, "z", 3), (1, "s", 1), (1, "s", 2), (0, "b", 0), (0, "a", 2),
    (0, "b", 1), (0, "a", 3), (1, "o", 0), (0, "b", 2), (0, "b", 3), (0, "end", 0),
)
SCHED = (
    (0, "z", 1), (0, "s", 3), (1, "a", 0), (2, "a", 1), (2, "z", 2), (3, "b", 0), (5, "a", 2), (6, "z", 3), (6, "b", 1),
    (9, "a", 3), (9, "b", 2), (12, "b", 3), (13, "end", 0),
)
BACK = (
    (1, 0, "arrive_core"), (2, 1, "arrive_core"), (3, 0, "arrive_b"), (4, 2, "arrive_core"), (5, 1, "arrive_b"),
    (5, 0, "arrive_a"), (6, 3, "arrive_core"), (7, 2, "arrive_b"), (8, 1, "arrive_a"), (9, 3, "arrive_b"),
    (9, 2, "arrive_a"), (11, 3, "arrive_a"),
)
ENTER = (
    (2, 0, "arrive_core"), (3, 1, "arrive_core"), (4, 0, "arrive_b"), (4, 2, "arrive_core"), (5, 1, "arrive_b"),
    (5, 3, "arrive_core"), (6, 0, "arrive_a"), (6, 2, "arrive_b"), (7, 1, "arrive_a"), (7, 3, "arrive_b"),
)
ENTER_LAST = ((2, "arrive_a"), (3, "arrive_a"))


def mm(a, b, ca, cb):
    return lax.dot_general(a, b, (((ca,), (cb,)), ((), ())), preferred_element_type=F32)


def normalise(values):
    centred = values - jnp.mean(values, axis=-1, keepdims=True)
    inverse = lax.rsqrt(jnp.mean(centred * centred, axis=-1, keepdims=True) + EPS)
    return centred * inverse, inverse


def norm_back(grad, scaled, inverse, gain):
    u = grad * gain
    return inverse * (
        u
        - jnp.mean(u, axis=-1, keepdims=True)
        - scaled * jnp.mean(u * scaled, axis=-1, keepdims=True)
    )


def column(row):
    return jnp.broadcast_to(row, (128, row.shape[1])).T[:, :1]


def join_rows(source, start, rows, target, pairs):
    low = start // 16 * 16
    high = -(-(start + rows) // 16) * 16

    def step(p, _):
        parts = [
            source[2 * p + i, low:high, :].astype(F32)[start - low : start - low + rows]
            for i in range(2)
        ]
        at = pl.multiple_of(2 * rows * p, 2 * rows)
        target[pl.ds(at, 2 * rows), :] = jnp.concatenate(parts, axis=0).astype(BF16)
        return 0

    lax.fori_loop(0, pairs, step, 0)


def sum_rows(source, start):
    low = start // 16 * 16

    def step(d, total):
        return total + source[d, low : low + 16, :].astype(F32)[start - low : start - low + 8]

    return lax.fori_loop(0, BLOCKS, step, jnp.zeros((8, D), F32))


def mask_rows(segment):
    r = lax.broadcasted_iota(jnp.int32, (32, ROW), 0)
    hit = r == segment + 1
    query_side = jnp.where(hit, 1.0, 0.0).astype(BF16)
    key_side = jnp.where(hit | (r >= 17), 0.0, -1e30).astype(BF16)
    return query_side, key_side


def scaled_query(queries):
    wide = queries.astype(F32) * (LOG2E / 8)
    high = wide.astype(BF16)
    rest = wide - high.astype(F32)
    low = rest.astype(BF16)
    return [high, low, (rest - low.astype(F32)).astype(BF16)]


class Place:
    def __init__(self, planes, side):
        self.planes, self.side = planes, side
        group, cell = lax.axis_index("dp"), lax.axis_index("fsdp")
        self.z, self.core = group // 2, group % 2
        y, x = cell // side, cell % side
        self.step_a = 1 + self.core * (side - 1)
        self.step_b = side - self.core * (side - 1)
        self.a = x + self.core * (y - x)
        self.b = y + self.core * (x - y)

    def plane(self, k):
        return lax.rem(self.z + k + self.planes, self.planes)

    def paired(self, k):
        plane, bit = self.z, 1
        while bit <= k:
            if k & bit:
                plane = plane + bit - 2 * bit * (self.z // bit % 2)
            bit *= 2
        return plane

    def at(self, z, core, a, b):
        return (z * 2 + core, a * self.step_a + b * self.step_b)

    def block(self, z, a, b):
        return (z * 2 + self.core) * (self.side * self.side) + a * self.step_a + b * self.step_b

    def run(self, z, core):
        return (z * 2 + core) * (self.side * self.side)

    def across_a(self):
        return self.at(self.z, self.core, 1 - self.a, self.b)

    def across_b(self):
        return self.at(self.z, self.core, self.a, 1 - self.b)

    def other_core(self):
        return (self.z * 2 + 1 - self.core, self.a * self.step_a + self.b * self.step_b)

    def along_z(self, k):
        return self.at(self.plane(k), self.core, self.a, self.b)

    def arrive(self):
        barrier = pltpu.get_barrier_semaphore()
        peers = [self.along_z(k) for k in range(1, self.planes)]
        peers += [self.across_a(), self.across_b(), self.other_core()]
        for peer in peers:
            pl.semaphore_signal(barrier, inc=1, device_id=peer, device_id_type=MESH)

    def meet(self):
        pl.semaphore_wait(pltpu.get_barrier_semaphore(), self.planes + 2)


class Gather:
    def __init__(self, place, own, full, send, recv):
        self.place, self.own, self.full, self.send, self.recv = place, own, full, send, recv
        self.planes = place.planes

    @staticmethod
    def semaphores(planes):
        return pltpu.SemaphoreType.DMA((5 * planes + 1,))

    def copy(self, kind, k):
        place, full = self.place, self.full
        plane = place.paired(k)
        column = full.at[place.block(plane, place.a, place.b)]
        if kind == "z":
            source, target = self.own, full.at[place.block(place.z, place.a, place.b)]
            to = place.at(plane, place.core, place.a, place.b)
        elif kind == "a" or kind == "b":
            source, target = (column if k else self.own), column
            to = place.across_a() if kind == "a" else place.across_b()
        elif kind == "d":
            source = target = full.at[place.block(plane, 1 - place.a, place.b)]
            to = place.across_b()
        else:
            cells = place.side * place.side
            source = target = full.at[pl.ds(place.run(plane, place.core), cells)]
            to = place.other_core()
        i = "zabdc".index(kind) * self.planes + k
        return pltpu.make_async_remote_copy(
            src_ref=source, dst_ref=target, send_sem=self.send.at[i], recv_sem=self.recv.at[i],
            device_id=to, device_id_type=MESH,
        )

    def keep(self):
        place = self.place
        return pltpu.make_async_copy(
            self.own, self.full.at[place.block(place.z, place.a, place.b)], self.send.at[5 * self.planes]
        )

    def start_z(self, ways):
        for k in ways:
            self.copy("z", k).start()

    def start_ab(self):
        self.keep().start()
        self.copy("a", 0).start()
        self.copy("b", 0).start()

    def event(self, kind, k):
        if kind == "s":
            self.start_z((k,))
        elif kind == "o":
            self.start_ab()
        elif kind == "z":
            self.copy("z", k).wait_recv()
            self.copy("a", k).start()
            self.copy("b", k).start()
        elif kind == "a":
            self.copy("a", k).wait_recv()
            self.copy("d", k).start()
        elif kind == "b":
            self.copy("b", k).wait_recv()
            self.copy("d", k).wait_recv()
            if k == 0:
                self.keep().wait()
            self.copy("c", k).start()
        else:
            for k in range(self.planes):
                self.copy("c", k).wait_recv()
            for k in range(self.planes):
                for kind in "zabdc" if k else "abdc":
                    self.copy(kind, k).wait_send()


class Rider:
    def __init__(self, place, stages, got, send, recv):
        self.place, self.stages, self.got, self.send, self.recv = place, stages, got, send, recv

    @staticmethod
    def scratch(planes):
        count = 3 + planes
        return [
            pltpu.VMEM((4, 8, D), F32),
            pltpu.VMEM((count, 8, D), F32),
            pltpu.SemaphoreType.DMA((count,)),
            pltpu.SemaphoreType.DMA((count,)),
        ]

    def copy(self, i):
        place = self.place
        to = (place.other_core, place.across_b, place.across_a)[i]() if i < 3 else place.along_z(i - 3)
        return pltpu.make_async_remote_copy(
            src_ref=self.stages.at[min(i, 3)], dst_ref=self.got.at[i], send_sem=self.send.at[i], recv_sem=self.recv.at[i],
            device_id=to, device_id_type=MESH,
        )

    def start(self):
        self.copy(0).start()

    def arrive(self, i):
        self.copy(i).wait_recv()
        self.stages[i + 1] = self.stages[i] + self.got[i]
        if i < 2:
            self.copy(i + 1).start()
        else:
            for k in range(1, self.place.planes):
                self.copy(3 + k).start()

    def finish(self):
        total = self.stages[3]
        for k in range(1, self.place.planes):
            self.copy(3 + k).wait_recv()
            total = total + self.got[3 + k]
        for i in (0, 1, 2):
            self.copy(i).wait_send()
        for k in range(1, self.place.planes):
            self.copy(3 + k).wait_send()
        return total


class Scatter:
    def __init__(self, place, sources, land, ours, got_b, got_a, got_z, mine, load, send, recv):
        self.place, self.sources, self.land, self.ours = place, sources, land, ours
        self.got_b, self.got_a, self.got_z, self.mine = got_b, got_a, got_z, mine
        self.load, self.send, self.recv = load, send, recv
        self.planes, self.side = place.planes, place.side
        self.cells = place.side * place.side
        self.parts = len(sources)
        self.order = list(range(1, self.planes)) + [0]
        self.offsets = [sum(s.shape[1] for s in sources[:i]) for i in range(self.parts + 1)]

    @staticmethod
    def scratch(planes, side, parts, rows):
        cells = side * side
        count = planes * (parts + 4)
        return [
            pltpu.VMEM((planes, cells, rows, D), BF16),
            pltpu.VMEM((2, cells, rows, D), BF16),
            pltpu.VMEM((planes, side, rows, D), BF16),
            pltpu.VMEM((planes, rows, D), BF16),
            pltpu.VMEM((planes, rows, D), BF16),
            pltpu.SemaphoreType.DMA((2, parts)),
            pltpu.SemaphoreType.DMA((count,)),
            pltpu.SemaphoreType.DMA((count,)),
        ]

    def remote(self, slot, source, target, to):
        return pltpu.make_async_remote_copy(
            src_ref=source, dst_ref=target, send_sem=self.send.at[slot], recv_sem=self.recv.at[slot],
            device_id=to, device_id_type=MESH,
        )

    def rows(self, part):
        return pl.ds(self.offsets[part], self.offsets[part + 1] - self.offsets[part])

    def cell(self, a, b):
        return a * self.place.step_a + b * self.place.step_b

    def core_copy(self, k, part):
        place = self.place
        group = pl.ds(place.run(place.plane(k), 1 - place.core), self.cells)
        return self.remote(
            k * self.parts + part, self.sources[part].at[group], self.land.at[k, :, self.rows(part)],
            place.other_core(),
        )

    def load_copy(self, t, part):
        place = self.place
        group = pl.ds(place.run(place.plane(self.order[t]), place.core), self.cells)
        return pltpu.make_async_copy(
            self.sources[part].at[group], self.ours.at[t % 2, :, self.rows(part)], self.load.at[t % 2, part]
        )

    def b_copy(self, k, a):
        place = self.place
        base = self.planes * self.parts
        return self.remote(
            base + 2 * k + a, self.land.at[k, self.cell(a, 1 - place.b)], self.got_b.at[k, a], place.across_b()
        )

    def a_copy(self, k):
        place = self.place
        base = self.planes * (self.parts + 2)
        return self.remote(
            base + k, self.land.at[k, self.cell(1 - place.a, place.b)], self.got_a.at[k], place.across_a()
        )

    def z_copy(self, k):
        place = self.place
        base = self.planes * (self.parts + 3)
        return self.remote(
            base + k, self.land.at[k, self.cell(place.a, place.b)], self.got_z.at[k], place.along_z(k)
        )

    def start(self, part):
        for k in self.order:
            self.core_copy(k, part).start()

    def start_one(self, t):
        self.core_copy(self.order[t], 0).start()

    def load_first(self):
        for part in range(self.parts):
            self.load_copy(0, part).start()

    def arrive_core(self, t):
        k = self.order[t]
        if t + 1 < self.planes:
            for part in range(self.parts):
                self.load_copy(t + 1, part).start()
        for part in range(self.parts):
            self.load_copy(t, part).wait()
            self.core_copy(k, part).wait_recv()

        def add(cell, _):
            self.land[k, cell] = self.land[k, cell] + self.ours[t % 2, cell]
            return 0

        lax.fori_loop(0, self.cells, add, 0)
        for a in range(self.side):
            self.b_copy(k, a).start()

    def arrive_b(self, t):
        k = self.order[t]
        for a in range(self.side):
            self.b_copy(k, a).wait_recv()
            at = self.cell(a, self.place.b)
            self.land[k, at] = self.land[k, at] + self.got_b[k, a]
        self.a_copy(k).start()

    def arrive_a(self, t):
        k = self.order[t]
        self.a_copy(k).wait_recv()
        at = self.cell(self.place.a, self.place.b)
        if k:
            self.land[k, at] = self.land[k, at] + self.got_a[k]
            self.z_copy(k).start()
        else:
            self.mine[...] = self.land[k, at].astype(F32) + self.got_a[k].astype(F32)

    def finish(self):
        for k in range(1, self.planes):
            self.z_copy(k).wait_recv()
            self.mine[...] += self.got_z[k].astype(F32)
        for k in range(self.planes):
            for part in range(self.parts):
                self.core_copy(k, part).wait_send()
            for a in range(self.side):
                self.b_copy(k, a).wait_send()
            self.a_copy(k).wait_send()
            if k:
                self.z_copy(k).wait_send()


def own_blocks(place, wq, wo, wu, wd, small, b_up, own1, own2):
    index = place.run(place.z, place.core) + place.a * place.step_a + place.b * place.step_b

    def spread(size, first):
        lane = lax.broadcasted_iota(jnp.int32, (size, D), 1)
        return jnp.where(lane == first + lax.broadcasted_iota(jnp.int32, (size, D), 0), 1.0, 0.0).astype(BF16)

    per_row = D // UROWS
    vec1 = mm(small[...], spread(OROWS, index * OROWS), 1, 0)
    whole_row = jnp.broadcast_to(b_up[...].astype(F32), (8, UROWS))
    here = lax.broadcasted_iota(jnp.int32, (8, UROWS), 0) == index // per_row
    vec2 = mm(jnp.where(here, whole_row, 0.0).astype(BF16), spread(UROWS, index % per_row * UROWS), 1, 0)
    own1[...] = jnp.concatenate([wq[...].astype(F32), vec1], axis=0).astype(BF16)
    own2[0:UROWS, :] = wu[...]
    down = wd[...].astype(F32)
    rest = [down[:, c * D : (c + 1) * D] for c in range(CHUNKS)] + [wo[...].astype(F32), vec2]
    own2[UROWS:SECOND, :] = jnp.concatenate(rest, axis=0).astype(BF16)


def forward_kernel(planes, side, rows, *refs):
    if planes:
        wq, wo, wu, wd, small, b_up, *refs = refs
    else:
        first_ref, full2, *refs = refs
    (hid_ref, emb_ref, seg_ref, packed_ref, mixed_ref, mid_ref, norm_ref, total_ref, vec_ref, w_qkv, w_out, scaled_ref,
     *refs) = refs
    if planes:
        full2, *refs = refs
    first, tail, bias_col, mask_q, mask_k, load, *refs = refs
    step = pl.program_id(0)
    begin = 2 * rows
    leave = begin + 7 * rows
    row, phase = (step - begin) // 7, (step - begin) % 7
    attending = (step >= begin) & (step < leave)
    tail_copy = pltpu.make_async_copy(full2.at[:, pl.ds(2 * UROWS, 32)], tail, load.at[0])

    if planes:
        own1, own2, send1, recv1, send2, recv2 = refs
        place = Place(planes, side)
        gather1 = Gather(place, own1, first, send1, recv1)
        gather2 = Gather(place, own2, full2, send2, recv2)

        @pl.when(step == 0)
        def _():
            place.arrive()
            own_blocks(place, wq, wo, wu, wd, small, b_up, own1, own2)
            place.meet()
            gather1.start_z(range(1, planes))
            gather1.start_ab()

        @pl.when(step == begin)
        def _():
            for which, kind, k in FIRST_SCHED:
                (gather1, gather2)[which].event(kind, k)

        for at, kind, k in SCHED:
            @pl.when(step == begin + at)
            def _(kind=kind, k=k):
                gather2.event(kind, k)

        @pl.when(step == begin + SCHED[-1][0])
        def _():
            tail_copy.start()
    else:
        @pl.when(step == 0)
        def _():
            tail_copy.start()
            c = pltpu.make_async_copy(first_ref, first, load.at[1])
            c.start()
            c.wait()

    @pl.when(step < begin)
    def _():
        scaled, _ = normalise(hid_ref[...].astype(F32) + emb_ref[...].astype(F32))
        mixed_ref[pl.ds(pl.multiple_of(step * TOKB, TOKB), TOKB), :] = scaled
        scaled_ref[...] = scaled.astype(BF16)

    @pl.when(step == begin)
    def _():
        join_rows(first, 0, QROWS, w_qkv, BLOCKS // 2)
        vec_ref[0] = sum_rows(first, QROWS)
        bias_col[0:D] = column(vec_ref[0, 2:3, :])
        bias_col[D : 2 * D] = jnp.zeros((D, 1), F32)
        bias_col[2 * D : 3 * D] = column(vec_ref[0, 3:4, :])

    tokens = pl.ds(pl.multiple_of(row * ROW, ROW), ROW)

    @pl.when(attending & (phase == 0))
    def _():
        normed = (mixed_ref[tokens, :] * vec_ref[0, 0:1, :] + vec_ref[0, 1:2, :]).astype(BF16)
        packed_ref[...] = (mm(w_qkv[...], normed, 1, 1) + bias_col[...]).astype(BF16)
        query_side, key_side = mask_rows(seg_ref[0])
        mask_q[...] = query_side
        mask_k[...] = key_side

    @pl.when(attending & (phase >= 1))
    def _():
        base = pl.multiple_of((phase - 1) * 128, 128)
        ones_rows = jnp.where(lax.broadcasted_iota(jnp.int32, (HEAD, ROW), 0) == 0, 1.0, 0.0).astype(BF16)
        sides = []
        for h in range(2):
            at = base + HEAD * h
            query_parts = scaled_query(packed_ref[pl.ds(at, HEAD), :])
            keys = packed_ref[pl.ds(D + at, HEAD), :]
            sides.append((
                jnp.concatenate(query_parts + [mask_q[...]], axis=0),
                jnp.concatenate([keys, keys, keys, mask_k[...]], axis=0),
                jnp.concatenate([packed_ref[pl.ds(2 * D + at, HEAD), :], ones_rows], axis=0),
            ))
        all_scores = [mm(sides[h][1], sides[h][0], 0, 0) for h in range(2)]
        mixed = []
        for h in range(2):
            scores = all_scores[h]
            top = jnp.max(scores, axis=0, keepdims=True)
            weights = jnp.exp2(scores - top).astype(BF16)
            summed = mm(sides[h][2], weights, 1, 0)
            total = summed[HEAD : HEAD + 1, :]
            mixed.append(summed[:HEAD, :] / total)
            total_ref[0, h : h + 1, :] = top + jnp.log2(total)
        mixed_ref[tokens, pl.ds(base, 128)] = jnp.concatenate(mixed, axis=0).T

    @pl.when(step == leave)
    def _():
        tail_copy.wait()
        join_rows(tail, 0, OROWS, w_out, BLOCKS // 2)
        vec_ref[1] = sum_rows(tail, OROWS)

    @pl.when(step >= leave)
    def _():
        half = pl.ds(pl.multiple_of((step - leave) * TOKB, TOKB), TOKB)
        entered = hid_ref[...].astype(F32) + emb_ref[...].astype(F32)
        middle = entered + mm(mixed_ref[half, :].astype(BF16), w_out[...], 1, 1) + vec_ref[0, 4:5, :]
        scaled, _ = normalise(middle)
        mid_ref[...] = middle
        norm_ref[...] = (scaled * vec_ref[0, 5:6, :] + vec_ref[0, 6:7, :]).astype(BF16)


def forward(planes, side, weights, hidden, embed, segment):
    n = hidden.shape[0]
    rows = n // ROW
    begin = 2 * rows
    leave_at = begin + 7 * rows
    one = pl.Buffered(1)
    hbm = pl.BlockSpec(memory_space=pl.ANY)

    def row(s):
        return jnp.clip((s - begin) // 7, 0, rows - 1)

    def entry(s):
        return (jnp.where(s < leave_at, jnp.minimum(s, begin - 1), s - leave_at), 0)

    def leave(s):
        return (jnp.maximum(s - leave_at, 0), 0)

    def pair(s):
        return jnp.where(s < leave_at, jnp.maximum((s - begin) % 7 - 1, 0) * (s >= begin), 5)

    entering = pl.BlockSpec((TOKB, D), entry)
    leaving = pl.BlockSpec((TOKB, D), leave)
    out_specs = [
        pl.BlockSpec((3 * D, ROW), lambda s: (0, row(s))),
        pl.BlockSpec((n, D), lambda s: (0, 0), pipeline_mode=one),
        leaving,
        leaving,
        pl.BlockSpec((1, 8, ROW), lambda s: (pair(s), 0, row(s))),
        pl.BlockSpec((2, 8, D), lambda s: (0, 0, 0)),
        pl.BlockSpec((3 * D, D), lambda s: (0, 0), pipeline_mode=one),
        pl.BlockSpec((D, D), lambda s: (0, 0), pipeline_mode=one),
        pl.BlockSpec((TOKB, D), lambda s: (jnp.minimum(s, begin - 1), 0)),
    ]
    out_shape = [
        jax.ShapeDtypeStruct((3 * D, n), BF16),
        jax.ShapeDtypeStruct((n, D), F32),
        jax.ShapeDtypeStruct((n, D), F32),
        jax.ShapeDtypeStruct((n, D), BF16),
        jax.ShapeDtypeStruct((HEADS // 2, 8, n), F32),
        jax.ShapeDtypeStruct((2, 8, D), F32),
        jax.ShapeDtypeStruct((3 * D, D), BF16),
        jax.ShapeDtypeStruct((D, D), BF16),
        jax.ShapeDtypeStruct((n, D), BF16),
    ]
    scratch = [
        pltpu.VMEM((BLOCKS, FIRST, D), BF16),
        pltpu.VMEM((BLOCKS, 32, D), BF16),
        pltpu.VMEM((3 * D, 1), F32),
        pltpu.VMEM((32, ROW), BF16),
        pltpu.VMEM((32, ROW), BF16),
        pltpu.SemaphoreType.DMA((2,)),
    ]
    params = dict(vmem_limit_bytes=56 * MIB)
    if planes:
        in_specs = [pl.BlockSpec(w.shape, lambda s: (0, 0), pipeline_mode=one) for w in weights]
        out_specs.append(hbm)
        out_shape.append(jax.ShapeDtypeStruct((BLOCKS, SECOND, D), BF16))
        scratch += [pltpu.VMEM((FIRST, D), BF16), pltpu.VMEM((SECOND, D), BF16)]
        scratch += [Gather.semaphores(planes)] * 4
        params.update(collective_id=1, has_side_effects=True)
    else:
        in_specs = [hbm, hbm]
    outs = pl.pallas_call(
        partial(forward_kernel, planes, side, rows),
        grid=(leave_at + begin,),
        in_specs=in_specs + [entering, entering, pl.BlockSpec((1, 1, ROW), lambda s: (row(s), 0, 0))],
        out_specs=out_specs,
        out_shape=out_shape,
        scratch_shapes=scratch,
        compiler_params=pltpu.CompilerParams(**params),
        name="attention_forward",
    )(*weights, hidden, embed, segment.reshape(rows, 1, ROW))
    return outs if planes else list(outs) + [weights[1]]


def feed_kernel(
    rows,
    up_ref, down_ref, vec_ref, norm_ref, mid_ref, cot_ref, seg_ref,
    out_ref, gmid_ref, gup_ref, gdown_ref, gvec_ref,
    w_down, result, back, live, active, pre, hold,
):
    step = pl.program_id(0)
    working = step < CHUNKS * rows
    j, i = step // rows, step % rows
    at = pl.ds(pl.multiple_of(i * ROW, ROW), ROW)

    @pl.when(step == 0)
    def _():
        gvec_ref[...] = jnp.zeros_like(gvec_ref)

    for chunk in range(CHUNKS):
        @pl.when(step == chunk * rows)
        def _():
            join_rows(down_ref, chunk % 2 * OROWS, OROWS, w_down, BLOCKS // 2)

    @pl.when(step < rows)
    def _():
        keep = column(jnp.where(seg_ref[0] >= 0, 1.0, 0.0))
        grad_result = cot_ref[...].astype(F32) * keep
        live[at, :] = grad_result.astype(BF16)
        gvec_ref[4:5, :] += jnp.sum(grad_result, axis=0, keepdims=True)

    @pl.when(working)
    def _():
        up = up_ref[...].reshape(D, D)
        down = w_down[...]
        x = mm(norm_ref[at, :], up, 1, 1) + vec_ref[1, pl.ds(j, 1), :]
        grad_act = mm(live[at, :], down, 1, 0)
        c0 = math.sqrt(2.0 / math.pi)
        c1 = 0.044715
        square = x * x
        th = jnp.tanh(x * (c0 + (c0 * c1) * square))
        half = 0.5 + 0.5 * th
        value = x * half
        slope = half + (half * (x - value)) * (2 * c0 + (6 * c0 * c1) * square)
        activated = value.astype(BF16)
        grad_pre = (grad_act * slope).astype(BF16)
        active[at, :] = activated
        pre[at, :] = grad_pre
        gvec_ref[pl.ds(j, 1), :] += jnp.sum(grad_pre.astype(F32), axis=0, keepdims=True)

        @pl.when(j == 0)
        def _():
            result[at, :] = mm(activated, down, 1, 1)
            back[at, :] = mm(grad_pre, up, 1, 0)

        @pl.when(j > 0)
        def _():
            result[at, :] += mm(activated, down, 1, 1)
            back[at, :] += mm(grad_pre, up, 1, 0)

    @pl.when(working & (i == rows - 1))
    def _():
        gup_ref[...] = mm(pre[...], norm_ref[...], 0, 0).astype(BF16)
        part_down = mm(live[...], active[...], 0, 0)

        hold[...] = part_down

        @pl.when(j % 2 == 0)
        def _():
            def pack(d, _):
                own = pl.ds(pl.multiple_of(d * OROWS, 8), OROWS)
                gdown_ref[d] = jnp.concatenate([hold[own], jnp.zeros((OROWS, D), F32)], axis=0).astype(BF16)
                return 0

            lax.fori_loop(0, BLOCKS, pack, 0)

        @pl.when(j % 2 == 1)
        def _():
            def pack(d, _):
                own = pl.ds(pl.multiple_of(d * OROWS, 8), OROWS)
                kept = gdown_ref[d].astype(F32)[:OROWS]
                gdown_ref[d] = jnp.concatenate([kept, hold[own]], axis=0).astype(BF16)
                return 0

            lax.fori_loop(0, BLOCKS, pack, 0)

    @pl.when(step >= CHUNKS * rows)
    def _():
        tokens = pl.ds(pl.multiple_of((step - CHUNKS * rows) * TOKB, TOKB), TOKB)
        middle = mid_ref[...]
        out_ref[...] = (middle + (result[tokens, :] + vec_ref[0, 7:8, :])).astype(BF16)
        grad = back[tokens, :]
        scaled, inverse = normalise(middle)
        gvec_ref[5:6, :] += jnp.sum(grad * scaled, axis=0, keepdims=True)
        gvec_ref[6:7, :] += jnp.sum(grad, axis=0, keepdims=True)
        gmid_ref[...] = live[tokens, :].astype(F32) + norm_back(grad, scaled, inverse, vec_ref[0, 5:6, :])


def feed(second, vec, normed, middle, cotangent, segment):
    n = normed.shape[0]
    rows = n // ROW
    one = pl.Buffered(1)

    def chunk(s):
        return jnp.minimum(s // rows, CHUNKS - 1)

    def late(s):
        return (jnp.maximum(s - CHUNKS * rows, 0), 0)

    leaving = pl.BlockSpec((TOKB, D), late)
    return pl.pallas_call(
        partial(feed_kernel, rows),
        grid=(CHUNKS * rows + n // TOKB,),
        in_specs=[
            pl.BlockSpec((BLOCKS // CHUNKS, UROWS, D), lambda s: (chunk(s), 0, 0)),
            pl.BlockSpec((BLOCKS, 2 * OROWS, D), lambda s: (0, 2 + chunk(s) // 2, 0), pipeline_mode=one),
            pl.BlockSpec((2, 8, D), lambda s: (0, 0, 0)),
            pl.BlockSpec((n, D), lambda s: (0, 0), pipeline_mode=one),
            leaving,
            pl.BlockSpec((ROW, D), lambda s: (jnp.minimum(s, rows - 1), 0), pipeline_mode=one),
            pl.BlockSpec((1, 1, ROW), lambda s: (jnp.minimum(s, rows - 1), 0, 0)),
        ],
        out_specs=[
            leaving,
            leaving,
            pl.BlockSpec((D, D), lambda s: (chunk(s), 0)),
            pl.BlockSpec((BLOCKS, 2 * OROWS, D), lambda s: (0, chunk(s) // 2, 0), pipeline_mode=one),
            pl.BlockSpec((8, D), lambda s: (0, 0)),
        ],
        out_shape=[
            jax.ShapeDtypeStruct((n, D), BF16),
            jax.ShapeDtypeStruct((n, D), F32),
            jax.ShapeDtypeStruct((FF, D), BF16),
            jax.ShapeDtypeStruct((BLOCKS, UROWS, D), BF16),
            jax.ShapeDtypeStruct((8, D), F32),
        ],
        scratch_shapes=[
            pltpu.VMEM((D, D), BF16),
            pltpu.VMEM((n, D), F32),
            pltpu.VMEM((n, D), F32),
            pltpu.VMEM((n, D), BF16),
            pltpu.VMEM((n, D), BF16),
            pltpu.VMEM((n, D), BF16),
            pltpu.VMEM((D, D), F32),
        ],
        compiler_params=pltpu.CompilerParams(vmem_limit_bytes=60 * MIB),
        name="feed_forward",
    )(second, second, vec, normed, middle, cotangent, segment.reshape(rows, 1, ROW))


def three_parts(row):
    r = lax.broadcasted_iota(jnp.int32, (16, row.shape[1]), 0)
    a = row.astype(BF16).astype(F32)
    b = (row - a).astype(BF16).astype(F32)
    c = row - a - b
    return jnp.where(r == 0, -a, jnp.where(r == 1, -b, jnp.where(r == 2, -c, 0.0))).astype(BF16)


def backward_kernel(
    planes, side, rows,
    w_out, seg_ref, packed_q, packed_k, packed_v, mixed_ref, total_ref, gmid_ref, gvec_ref, gup_ref, gdown_ref,
    gpacked_ref, sums_ref, *rest,
):
    if planes:
        up_out, down_out, out_out, vec_out, mask_q, mask_k, grad_mixed, delta, sum_out, sum_bias, tail, mine, *transfer = rest
    else:
        tail, mask_q, mask_k, grad_mixed, delta, sum_out, sum_bias = rest
    step = pl.program_id(0)
    entry = 2 * rows
    heads = step >= entry

    if planes:
        place = Place(planes, side)
        scatter = Scatter(place, (gup_ref, gdown_ref, tail), *transfer[:5], mine, *transfer[5:])

        @pl.when(step == 0)
        def _():
            place.arrive()

        @pl.when(step == 1)
        def _():
            place.meet()
            scatter.start(0)
            scatter.start(1)

        @pl.when(step == entry)
        def _():
            scatter.start(2)
            scatter.load_first()

        for at, t, act in BACK:
            @pl.when(step == entry + at)
            def _(t=t, act=act):
                getattr(scatter, act)(t)

    @pl.when(step == 0)
    def _():
        sum_out[...] = jnp.zeros_like(sum_out)
        sum_bias[...] = jnp.zeros_like(sum_bias)

    @pl.when(step < entry)
    def _():
        at = pl.ds(pl.multiple_of(step * TOKB, TOKB), TOKB)
        mixed = mixed_ref[...]
        branch = gmid_ref[...].astype(BF16)
        sum_bias[0:1, :] += jnp.sum(branch.astype(F32), axis=0, keepdims=True)
        sum_out[...] += mm(branch, mixed.astype(BF16), 0, 0)
        grad = mm(branch, w_out[...], 1, 0).astype(BF16).astype(F32)
        grad_mixed[:, at] = grad.T.astype(BF16)
        inner = (grad * mixed).T
        delta[:, at] = jnp.concatenate(
            [jnp.sum(inner[HEAD * h : HEAD * (h + 1)], axis=0, keepdims=True) for h in range(HEADS)]
            + [jnp.zeros((16 - HEADS, TOKB), F32)],
            axis=0,
        )

    @pl.when(step == entry - 1)
    def _():
        r = lax.broadcasted_iota(jnp.int32, (8, D), 0)
        vectors = jnp.where(r == 7, sum_bias[0:1, :], gvec_ref[...])

        def pack(d, _):
            at = pl.ds(pl.multiple_of(d * OROWS, 8), OROWS)
            tail[d] = jnp.concatenate([sum_out[at, :], vectors], axis=0).astype(BF16)
            return 0

        lax.fori_loop(0, BLOCKS, pack, 0)

    row, pair = (step - entry) // 6, (step - entry) % 6

    @pl.when(heads & (pair == 0))
    def _():
        query_side, key_side = mask_rows(seg_ref[0])
        mask_q[...] = query_side
        mask_k[...] = key_side

    @pl.when(heads)
    def _():
        tokens = pl.ds(pl.multiple_of(row * ROW, ROW), ROW)
        r = lax.broadcasted_iota(jnp.int32, (16, ROW), 0)
        ones_rows = jnp.where(r < 3, 1.0, 0.0).astype(BF16)
        base = pl.multiple_of(pair * 128, 128)
        column_sums = []
        for h in range(2):
            at_rows = slice(HEAD * h, HEAD * (h + 1))
            queries, keys, values = packed_q[at_rows, :], packed_k[at_rows, :], packed_v[at_rows, :]
            grad = grad_mixed[pl.ds(base + HEAD * h, HEAD), tokens]
            wide_q = jnp.concatenate(scaled_query(queries) + [mask_q[...], three_parts(total_ref[0, h : h + 1, :])], axis=0)
            wide_k = jnp.concatenate([keys, keys, keys, mask_k[...], ones_rows], axis=0)
            wide_g = jnp.concatenate([grad, three_parts(delta[pl.ds(2 * pair + h, 1), tokens])], axis=0)
            wide_v = jnp.concatenate([values, ones_rows], axis=0)
            grad_v = jnp.zeros((HEAD, ROW), F32)
            grad_k = jnp.zeros((HEAD, ROW), F32)
            grad_q = []
            for half in range(2):
                at = slice(half * (ROW // 2), (half + 1) * (ROW // 2))
                probs = jnp.exp2(mm(wide_q[:, at], wide_k, 0, 0))
                grad_probs = mm(wide_g[:, at], wide_v, 0, 0)
                grad_scores = (probs * grad_probs).astype(BF16)
                grad_v = grad_v + mm(grad[:, at], probs.astype(BF16), 1, 0)
                grad_k = grad_k + mm(queries[:, at], grad_scores, 1, 0)
                grad_q.append(mm(keys, grad_scores, 1, 1))
            grads = (
                (jnp.concatenate(grad_q, axis=1) * 0.125).astype(BF16),
                (grad_k * 0.125).astype(BF16),
                grad_v.astype(BF16),
            )
            for part in range(3):
                gpacked_ref[pl.ds(part * D + base + HEAD * h, HEAD), :] = grads[part]
            column_sums.append([jnp.sum(g.astype(F32), axis=1, keepdims=True) for g in grads])
        for part in range(3):
            both = jnp.concatenate([column_sums[0][part], column_sums[1][part]], axis=0)
            at = pl.ds(part * D + base, 128)

            @pl.when(row == 0)
            def _():
                sums_ref[at, :] = both

            @pl.when(row > 0)
            def _():
                sums_ref[at, :] += both

    if planes:
        @pl.when(step == entry + 6 * rows - 1)
        def _():
            scatter.finish()
            up_out[...] = mine[0:UROWS, :]
            for c in range(CHUNKS):
                down_out[:, c * D : (c + 1) * D] = mine[UROWS + c * OROWS : UROWS + (c + 1) * OROWS, :]
            out_out[...] = mine[2 * UROWS : 2 * UROWS + OROWS, :]
            vec_out[...] = mine[2 * UROWS + OROWS : 2 * UROWS + 32, :]


def backward(planes, side, w_out, segment, packed, mixed, totals, gmid, gvec, gup, gdown):
    n = mixed.shape[0]
    rows = n // ROW
    entry = 2 * rows
    one = pl.Buffered(1)
    hbm = pl.BlockSpec(memory_space=pl.ANY)

    def early(s):
        return (jnp.minimum(s, entry - 1), 0)

    def row(s):
        return jnp.maximum(s - entry, 0) // 6

    def pair(s):
        return jnp.maximum(s - entry, 0) % 6

    def heads(part):
        return pl.BlockSpec((128, ROW), lambda s: (6 * part + pair(s), row(s)))

    out_specs = [
        pl.BlockSpec((3 * D, ROW), lambda s: (0, row(s))),
        pl.BlockSpec((3 * D, 1), lambda s: (0, 0), pipeline_mode=one),
    ]
    out_shape = [jax.ShapeDtypeStruct((3 * D, n), BF16), jax.ShapeDtypeStruct((3 * D, 1), F32)]
    scratch = [
        pltpu.VMEM((32, ROW), BF16),
        pltpu.VMEM((32, ROW), BF16),
        pltpu.VMEM((D, n), BF16),
        pltpu.VMEM((16, n), F32),
        pltpu.VMEM((D, D), F32),
        pltpu.VMEM((8, D), F32),
    ]
    params = dict(vmem_limit_bytes=56 * MIB)
    if planes:
        rows1 = 2 * UROWS + 32
        for shape in ((UROWS, D), (OROWS, FF), (OROWS, D), (8, D)):
            out_specs.append(pl.BlockSpec(shape, lambda s: (0, 0), pipeline_mode=one))
            out_shape.append(jax.ShapeDtypeStruct(shape, F32))
        scratch += [pltpu.VMEM((BLOCKS, 32, D), BF16), pltpu.VMEM((rows1, D), F32)]
        scratch += Scatter.scratch(planes, side, 3, rows1)
        params.update(collective_id=2, has_side_effects=True)
    else:
        out_specs.append(pl.BlockSpec((BLOCKS, 32, D), lambda s: (0, 0, 0), pipeline_mode=one))
        out_shape.append(jax.ShapeDtypeStruct((BLOCKS, 32, D), BF16))
    return pl.pallas_call(
        partial(backward_kernel, planes, side, rows),
        grid=(entry + 6 * rows,),
        in_specs=[
            pl.BlockSpec((D, D), lambda s: (0, 0), pipeline_mode=one),
            pl.BlockSpec((1, 1, ROW), lambda s: (row(s), 0, 0)),
            heads(0),
            heads(1),
            heads(2),
            pl.BlockSpec((TOKB, D), early),
            pl.BlockSpec((1, 8, ROW), lambda s: (pair(s), 0, row(s))),
            pl.BlockSpec((TOKB, D), early),
            pl.BlockSpec((8, D), lambda s: (0, 0)),
            hbm,
            hbm,
        ],
        out_specs=out_specs,
        out_shape=out_shape,
        scratch_shapes=scratch,
        compiler_params=pltpu.CompilerParams(**params),
        name="attention_backward",
    )(w_out, segment.reshape(rows, 1, ROW), packed, packed, packed, mixed, totals, gmid, gvec, gup, gdown)


def enter_kernel(
    planes, side, blocks,
    w_hbm, vec_ref, hid_ref, emb_ref, gmid_ref, grad_hbm, sums_ref, scaled_hbm,
    ghid_ref, out_ref, *rest,
):
    if planes:
        vec_out, scaled_all, w_qkv, grad_packed, totals, load, packed, mine, *transfer = rest
    else:
        packed, (scaled_all, w_qkv, grad_packed, totals, load) = out_ref, rest
    step = pl.program_id(0)
    chunks = 4
    size = 3 * D // chunks
    begin, late = 0, chunks
    if planes:
        place = Place(planes, side)

    def chunk_of(t):
        return place.plane(t + 1) if planes else t

    def grad_load(t):
        rows = pl.ds(pl.multiple_of(chunk_of(t) * size, size), size)
        return pltpu.make_async_copy(grad_hbm.at[rows], grad_packed.at[rows], load.at[t])

    loads = [
        pltpu.make_async_copy(scaled_hbm, scaled_all, load.at[chunks]),
        pltpu.make_async_copy(w_hbm, w_qkv, load.at[chunks + 1]),
    ]

    if planes:
        rider = Rider(place, *transfer[:4])
        scatter = Scatter(place, (packed,), *transfer[4:9], mine, *transfer[9:])

    @pl.when(step == 0)
    def _():
        loads[0].start()
        grad_load(0).start()
        loads[1].start()
        for t in range(1, chunks):
            grad_load(t).start()
        totals[...] = jnp.zeros_like(totals)
        if planes:
            place.arrive()

    def entering():
        return normalise(hid_ref[...].astype(F32) + emb_ref[...].astype(F32))

    @pl.when(step == begin)
    def _():
        for c in loads:
            c.wait()
        if planes:
            place.meet()

    for t in range(chunks):
        @pl.when(step == t)
        def _(t=t):
            grad_load(t).wait()

    if planes:
        for at, t, act in ENTER:
            @pl.when(step == begin + at)
            def _(t=t, act=act):
                getattr(scatter, act)(t)
                if t == planes - 1:
                    rider.arrive(("arrive_core", "arrive_b", "arrive_a").index(act))

    @pl.when((step >= begin) & (step < late))
    def _():
        t = step - begin
        chunk = chunk_of(t)
        at = pl.ds(pl.multiple_of(chunk * size, size), size)
        product = mm(grad_packed[at, :], scaled_all[...], 1, 0)
        weight = w_qkv[at, :].astype(F32)
        sums = sums_ref[at, :]
        totals[0:1, :] += jnp.sum(weight * product, axis=0, keepdims=True)
        totals[1:2, :] += jnp.sum(weight * sums, axis=0, keepdims=True)
        grad_w = product * vec_ref[0, 0:1, :] + sums * vec_ref[0, 1:2, :]
        count = BLOCKS // chunks
        for i in range(count):
            rows = [grad_w[i * QROWS : (i + 1) * QROWS], jnp.zeros((8, D), F32)]
            packed[chunk * count + i] = jnp.concatenate(rows, axis=0).astype(BF16)

    if planes:
        for t in range(planes):
            @pl.when(step == begin + t)
            def _(t=t):
                if t == 0:
                    scatter.load_first()
                scatter.start_one(t)

    @pl.when(step == late - 1)
    def _():
        ends = [jnp.broadcast_to(sums_ref[at : at + D, :], (D, 128)).T[0:1, :] for at in (0, 2 * D)]
        vectors = jnp.concatenate([totals[0:2, :]] + ends + [jnp.zeros((4, D), F32)], axis=0)
        if planes:
            rider.stages[0] = vectors
            rider.start()
        else:
            kept = packed[0, QROWS - 8 : QROWS + 8, :].astype(F32)[:8]
            packed[0, QROWS - 8 : QROWS + 8, :] = jnp.concatenate([kept, vectors], axis=0).astype(BF16)

    @pl.when(step >= late)
    def _():
        at = pl.ds(pl.multiple_of((step - late) * TOKB, TOKB), TOKB)
        scaled, inverse = entering()
        grad = mm(grad_packed[:, at], w_qkv[...], 0, 0)
        ghid_ref[...] = (gmid_ref[...] + norm_back(grad, scaled, inverse, vec_ref[0, 0:1, :])).astype(BF16)

    if planes:
        @pl.when(step == late + blocks - 1)
        def _():
            for t, act in ENTER_LAST:
                getattr(scatter, act)(t)
                if t == planes - 1:
                    rider.arrive(("arrive_core", "arrive_b", "arrive_a").index(act))
            scatter.finish()
            out_ref[...] = mine[0:QROWS, :]
            vec_out[...] = rider.finish()


def enter(planes, side, w_qkv, vec, hidden, embed, gmid, gpacked, sums, scaled):
    n = hidden.shape[0]
    blocks = n // TOKB
    late_at = 4
    one = pl.Buffered(1)
    hbm = pl.BlockSpec(memory_space=pl.ANY)

    def late(s):
        return (jnp.maximum(s - late_at, 0), 0)

    tokens = pl.BlockSpec((TOKB, D), late)
    out_specs = [pl.BlockSpec((TOKB, D), late)]
    out_shape = [jax.ShapeDtypeStruct((n, D), BF16)]
    scratch = [
        pltpu.VMEM((n, D), BF16),
        pltpu.VMEM((3 * D, D), BF16),
        pltpu.VMEM((3 * D, n), BF16),
        pltpu.VMEM((8, D), F32),
        pltpu.SemaphoreType.DMA((6,)),
    ]
    params = dict(vmem_limit_bytes=56 * MIB)
    if planes:
        for shape in ((QROWS, D), (8, D)):
            out_specs.append(pl.BlockSpec(shape, lambda s: (0, 0), pipeline_mode=one))
            out_shape.append(jax.ShapeDtypeStruct(shape, F32))
        scratch += [pltpu.VMEM((BLOCKS, FIRST, D), BF16), pltpu.VMEM((FIRST, D), F32)]
        scratch += Rider.scratch(planes) + Scatter.scratch(planes, side, 1, FIRST)
        params.update(collective_id=3, has_side_effects=True)
    else:
        out_specs.append(pl.BlockSpec((BLOCKS, FIRST, D), lambda s: (0, 0, 0), pipeline_mode=one))
        out_shape.append(jax.ShapeDtypeStruct((BLOCKS, FIRST, D), BF16))
    return pl.pallas_call(
        partial(enter_kernel, planes, side, blocks),
        grid=(late_at + blocks,),
        in_specs=[
            hbm,
            pl.BlockSpec((2, 8, D), lambda s: (0, 0, 0)),
            tokens,
            tokens,
            pl.BlockSpec((TOKB, D), late),
            hbm,
            pl.BlockSpec((3 * D, 1), lambda s: (0, 0), pipeline_mode=one),
            hbm,
        ],
        out_specs=out_specs,
        out_shape=out_shape,
        scratch_shapes=scratch,
        compiler_params=pltpu.CompilerParams(**params),
        name="projection_backward",
    )(w_qkv, vec, hidden, embed, gmid, gpacked, sums, scaled)


def body(
    planes, side, devices,
    hidden, time_embed, segment_ids,
    ln1_gain, ln1_bias, w_qkv, b_query, b_value, w_out, b_out, ln2_gain, ln2_bias, w_up, b_up, w_down, b_down,
    cotangent,
):
    index = lax.axis_index("dp") * lax.axis_size("fsdp") + lax.axis_index("fsdp")
    axes = ("dp", "fsdp")
    small = (ln1_gain, ln1_bias, b_query, b_value, b_out, ln2_gain, ln2_bias, b_down)
    if planes:
        weights = (w_qkv.T, w_out.T, w_up.T, w_down.T, jnp.stack(small), b_up[None, :])
    else:
        def whole(a, dim):
            return lax.all_gather(a, axes, axis=dim, tiled=True)

        def only_first(rows):
            return jnp.concatenate([rows[None], jnp.zeros((BLOCKS - 1,) + rows.shape, BF16)], axis=0)

        vec1 = jnp.stack([whole(v, 0) for v in small])
        vec2 = jnp.concatenate([whole(b_up, 0).reshape(CHUNKS, D), jnp.zeros((8 - CHUNKS, D), BF16)], axis=0)
        down_rows = whole(w_down, 1).T.reshape(BLOCKS, OROWS, CHUNKS, D).transpose(0, 2, 1, 3)
        first = jnp.concatenate([whole(w_qkv, 1).T.reshape(BLOCKS, QROWS, D), only_first(vec1)], axis=1)
        second = jnp.concatenate(
            [
                whole(w_up, 1).T.reshape(BLOCKS, UROWS, D),
                down_rows.reshape(BLOCKS, UROWS, D),
                whole(w_out, 1).T.reshape(BLOCKS, OROWS, D),
                only_first(vec2),
            ],
            axis=1,
        )
        weights = (first, second)
    packed, mixed, middle, normed, totals, vec, full_qkv, full_out, scaled, second = forward(
        planes, side, weights, hidden, time_embed, segment_ids
    )
    output, gmid, gup, gdown, gvec = feed(second, vec, normed, middle, cotangent, segment_ids)
    gup = gup.reshape(BLOCKS, UROWS, D)
    gpacked, sums, *late = backward(
        planes, side, full_out, segment_ids, packed, mixed, totals, gmid, gvec, gup, gdown
    )
    ghid, *last = enter(planes, side, full_qkv, vec, hidden, time_embed, gmid, gpacked, sums, scaled)
    if planes:
        part_up, part_down, part_out, vectors = late
        part_qkv, vectors_qkv = last
        vectors = jnp.concatenate([vectors, vectors_qkv], axis=0)
        short = lax.dynamic_slice(vectors, (0, index * OROWS), (16, OROWS))
        part_bup = lax.dynamic_slice(vectors[:CHUNKS].reshape(-1), (index * UROWS,), (UROWS,))
    else:
        def shared(a, dim):
            return lax.psum_scatter(a.astype(F32), axes, scatter_dimension=dim, tiled=True)

        (late,), (last,) = late, last
        part_up = shared(gup.reshape(FF, D), 0)
        part_down = shared(gdown.reshape(BLOCKS, CHUNKS, OROWS, D).transpose(0, 2, 1, 3).reshape(D, FF), 0)
        part_out = shared(late[:, :OROWS].reshape(D, D), 0)
        part_qkv = shared(last[:, :QROWS].reshape(3 * D, D), 0)
        vectors = jnp.concatenate([late[0, OROWS:], last[0, QROWS:]], axis=0)
        short = shared(vectors, 1)
        part_bup = shared(vectors[:CHUNKS].reshape(-1), 0)
    return (
        output, ghid,
        short[8], short[9], part_qkv.T, short[10], short[11], part_out.T, short[7],
        short[5], short[6], part_up.T, part_bup, part_down.T, short[4],
    )


def solution(mesh):
    groups, cells = mesh.shape["dp"], mesh.shape["fsdp"]
    side = math.isqrt(cells)
    own_transfers = groups * cells == BLOCKS and side == 2 and cells == 4 and groups % 2 == 0
    split = ("dp", "fsdp")
    rows, flat, cols = P(split, None), P(split), P(None, split)
    return jax.shard_map(
        partial(body, groups // 2 if own_transfers else 0, side, groups * cells),
        mesh=mesh,
        in_specs=(
            rows, rows, flat, flat, flat, cols, flat, flat, cols, flat, flat, flat, cols, flat, cols, flat, rows,
        ),
        out_specs=(
            rows, rows, flat, flat, cols, flat, flat, cols, flat, flat, flat, cols, flat, cols, flat,
        ),
        check_vma=False,
    )
```
